32 devices in a mesh: section: 2 (over x), dp: 16 (over z, y, core).
Axes of the slice: x: 2, y: 2, z: 4, core: 2. Of those that a mesh axis runs over, the one named last changes fastest.
Arguments:
- tokens: bfloat16 [2, 2, 4096, 512], P('section', None, 'dp'), may hold values from -6 to 6
- lengths: int32 [2, 2, 16, 32], P(None, None, 'dp'), may hold values from 1 to 224, 256 in all within a row
- params: float32 [2, 51440, 128], P('section', 'dp'), may hold values from -2 to 2
- cotangent: bfloat16 [2, 4096, 512], P(None, 'dp'), may hold values from -6 to 6
Outputs:
- results: bfloat16 [2, 2, 4096, 512], P('section', None, 'dp')
- token_grads: float32 [2, 2, 4096, 512], P('section', None, 'dp')
- param_grads: float32 [2, 51440, 128], P('section', 'dp')
The draws below stay inside these ranges and needn't reach their ends.
Inputs may be any that keep to these rules, and one draw needn't show every extreme that they name: Each row of 32 numbers holds, in order, the lengths of the sentences packed into one side of one pack; a row sums to 256 and its largest entry is exactly 224. Source sentence k and target sentence k form a pair.
All inputs are finite; a program needn't handle non-finite values.
Results may differ from the reference program's by a relative error of at most 0.025.
Values may be sent and summed in bfloat16 or wider, within the bound.
No kernel may reach another device: no remote copies, remote signals or barrier semaphores. Data moves between devices by JAX's collectives and lax.ppermute only.
A program may use at most 512 MiB of HBM per device.

```python
import math
import jax
import jax.numpy as jnp
import numpy as np
from jax import lax

D = 512
FF = 2048
HEADS = 8
BRANCH_HEADS = 16
TOK = 256
MICRO = 2
SENT_MAX = 224
SENTS = 32
GROUP_TOK = 4096
P_E = 5668864
P_D = 7499008
EROWS = 2768
DROWS = 3662
QROWS = 3215
N_DP = 16


def attention_entries_drawn(prefix):
    return [(prefix + '_query', (D, D), D ** (-0.5), 0.0), (prefix + '_key', (D, D), D ** (-0.5), 0.0), (prefix + '_value', (D, D), D ** (-0.5), 0.0), (prefix + '_output', (D, D), 4.0 / math.sqrt(D), 0.0)]


def norm_entries_drawn(prefix, width_of):
    return [(prefix + '_gain', (width_of,), 0.1, 1.0), (prefix + '_bias', (width_of,), 0.2, 0.0)]


def encoder_layout_drawn():
    half_width = D // 2
    return norm_entries_drawn('norm_glu', D) + [('glu_weight', (D, 2 * D), D ** (-0.5), 0.0), ('glu_bias', (2 * D,), 0.2, 0.0)] + norm_entries_drawn('norm_conv', D) + [('left_weight', (D, FF), D ** (-0.5), 0.0), ('left_bias', (FF,), 0.2, 0.0), ('right_weight', (3 * D, half_width), (3 * D) ** (-0.5), 0.0), ('right_bias', (half_width,), 0.2, 0.0)] + norm_entries_drawn('middle', FF) + [('depth_taps', (9, FF), 1.0 / 3.0, 0.0), ('point_weight', (FF, half_width), FF ** (-0.5), 0.0), ('point_bias', (half_width,), 0.2, 0.0)] + norm_entries_drawn('norm_attn', D) + attention_entries_drawn('attn') + norm_entries_drawn('norm_feed', D) + [('feed_in_weight', (D, FF), D ** (-0.5), 0.0), ('feed_in_bias', (FF,), 0.2, 0.0), ('feed_out_weight', (FF, D), FF ** (-0.5), 0.0), ('feed_out_bias', (D,), 0.2, 0.0)]


def decoder_layout_drawn():
    half_width = D // 2
    return norm_entries_drawn('norm_branch', D) + attention_entries_drawn('wide_self') + attention_entries_drawn('wide_cross') + norm_entries_drawn('norm_conv', D) + [('left_taps', (11, D), 11 ** (-0.5), 0.0), ('left_weight', (D, 2 * D), D ** (-0.5), 0.0), ('left_bias', (2 * D,), 0.2, 0.0), ('right_taps', (7, D), 7 ** (-0.5), 0.0), ('right_weight', (D, half_width), D ** (-0.5), 0.0), ('right_bias', (half_width,), 0.2, 0.0)] + norm_entries_drawn('middle', 2 * D) + [('out_taps', (7, 2 * D), 7 ** (-0.5), 0.0), ('out_weight', (2 * D, D), (2 * D) ** (-0.5), 0.0), ('out_bias', (D,), 0.2, 0.0)] + norm_entries_drawn('norm_self', D) + attention_entries_drawn('self') + norm_entries_drawn('norm_cross', D) + attention_entries_drawn('cross') + norm_entries_drawn('norm_feed', D) + [('feed_in_weight', (D, FF), D ** (-0.5), 0.0), ('feed_in_bias', (FF,), 0.2, 0.0), ('feed_out_weight', (FF, D), FF ** (-0.5), 0.0), ('feed_out_bias', (D,), 0.2, 0.0)]


def scale_tables(layout):
    starts = []
    spreads = []
    centers = []
    offset = 0
    for label, dimensions, spread, center in layout:
        starts.append(offset)
        spreads.append(spread)
        centers.append(center)
        offset = offset + math.prod(dimensions)
    starts.append(offset)
    spreads.append(0.02)
    centers.append(0.0)
    return (np.array(starts, np.int32), np.array(spreads, np.float32), np.array(centers, np.float32))


def look_up(flat_index, tables):
    starts, spreads, centers = tables
    found_at = jnp.searchsorted(jnp.asarray(starts), flat_index, side='right') - 1
    return (jnp.asarray(spreads)[found_at], jnp.asarray(centers)[found_at])


def draw_params(key, part):
    key = jax.random.fold_in(key, 11)
    enc_tables = scale_tables(encoder_layout_drawn())
    dec_tables = scale_tables(decoder_layout_drawn())
    row_index = jnp.arange(N_DP * QROWS, dtype=jnp.int32)
    column = jnp.arange(128, dtype=jnp.int32)
    piece_index = row_index // QROWS
    within = row_index % QROWS
    enc_flat = (piece_index * EROWS + within)[:, None] * 128 + column[None, :]
    tail_flat = (piece_index * DROWS + QROWS + within - EROWS)[:, None] * 128 + column[None, :]
    head_flat = (piece_index * DROWS + within)[:, None] * 128 + column[None, :]
    enc_spread, enc_center = look_up(enc_flat, enc_tables)
    tail_spread, tail_center = look_up(tail_flat, dec_tables)
    head_spread, head_center = look_up(head_flat, dec_tables)
    in_encoder = (within < EROWS)[:, None]
    first_spread = jnp.where(in_encoder, enc_spread, tail_spread)
    first_center = jnp.where(in_encoder, enc_center, tail_center)
    spreads = jnp.stack([first_spread, head_spread])
    centers = jnp.stack([first_center, head_center])
    normal_draw = jax.random.truncated_normal(key, -4.0, 4.0, (2, N_DP * QROWS, 128), jnp.float32)
    return (centers + spreads * normal_draw).astype(jnp.float32)


def steps_of(stream_key, extent, shards, least, largest):
    level = 1.0
    for axis_at, shards_of in shards:
        steps = jax.random.uniform(jax.random.fold_in(jax.random.fold_in(stream_key, 6), axis_at), (shards_of,), jnp.float32, least / len(shards), largest / len(shards))
        level = level * jnp.repeat(jnp.exp(steps), extent[axis_at] // shards_of).reshape((-1,) + (1,) * (len(extent) - 1 - axis_at))
    return level


def profile(number_of, total, most, lean):
    weights = [(1 << 20) // math.isqrt(rank ** lean) + 1 for rank in range(2, number_of + 1)]
    spare, counts = total - most - (number_of - 1), [1] * (number_of - 1)
    while spare > 0:
        movable = [i for i in range(number_of - 1) if counts[i] < most]
        whole, left = sum([weights[i] for i in movable]), spare
        for i in movable:
            more = min(most - counts[i], max(1, left * weights[i] // whole), spare)
            counts[i] = counts[i] + more
            spare = spare - more
    return np.array([most] + counts)


def uneven(stream_key, amount, total, most, slope):
    if amount == 2:
        one = jax.random.randint(stream_key, (), max(1, total - most), min(most, total - 1) + 1)
        return jnp.stack([one, total - one])
    sizes = jnp.asarray(profile(amount, total, most, slope), jnp.int32)
    pairs = (amount - 1) // 2
    source_of, taker = sizes[1:1 + 2 * pairs:2], sizes[2:2 + 2 * pairs:2]
    margin = jnp.minimum(source_of - 1, most - taker)
    moved = jax.random.randint(jax.random.fold_in(stream_key, 1), (pairs,), 0, 1 << 20) % (margin + 1)
    sizes = sizes.at[1:1 + 2 * pairs:2].set(source_of - moved).at[2:2 + 2 * pairs:2].set(taker + moved)
    return sizes[jax.random.permutation(jax.random.fold_in(stream_key, 2), amount)]


def scatter_about(stream_key, dims, deviation, most, shards=(), held_as=jnp.bfloat16):
    factor_of = steps_of(stream_key, dims, shards, -0.22, 0.18) if shards else 1.0
    entries = jax.random.normal(stream_key, dims, jnp.float32) * deviation * factor_of
    return jnp.minimum(jnp.maximum(entries, -most), most).astype(held_as)


def setup_inputs(seed: int = 0) -> dict:
    key_list = jax.random.split(jax.random.key(seed), 5)
    tokens = scatter_about(key_list[0], (2, MICRO, GROUP_TOK, D), 1.0, 6.0, ((0, 2), (2, 16)))
    lengths = jax.vmap(lambda own: uneven(own, SENTS, TOK, SENT_MAX, 2))(jax.random.split(key_list[1], 2 * MICRO * N_DP)).reshape((2, MICRO, N_DP, SENTS)).astype(jnp.int32)
    params = draw_params(jax.random.fold_in(key_list[4], 71), 0)
    cotangent = scatter_about(key_list[3], (MICRO, GROUP_TOK, D), 1.0, 6.0, ((1, 16),))
    return {"tokens": tokens, "lengths": lengths, "params": params, "cotangent": cotangent}


@jax.custom_vjp
def low(v):
    return lax.optimization_barrier(v.astype(jnp.bfloat16)).astype(jnp.float32)

@jax.custom_vjp
def low_back(v):
    return v

def low_keep(v):
    return (low(v), None)

def low_pass(kept, grad):
    return (grad,)

def back_keep(v):
    return (v, None)

def back_low(kept, grad):
    return (low(grad),)
low.defvjp(low_keep, low_pass)
low_back.defvjp(back_keep, back_low)
epsilon = 1e-06
blocked = -1000000000.0

def attention_entries(prefix):
    return [(prefix + '_query', (D, D), D ** (-0.5), 0.0), (prefix + '_key', (D, D), D ** (-0.5), 0.0), (prefix + '_value', (D, D), D ** (-0.5), 0.0), (prefix + '_output', (D, D), 4.0 / math.sqrt(D), 0.0)]

def norm_entries(prefix, width_of):
    return [(prefix + '_gain', (width_of,), 0.1, 1.0), (prefix + '_bias', (width_of,), 0.2, 0.0)]

def encoder_layout():
    half_width = D // 2
    return norm_entries('norm_glu', D) + [('glu_weight', (D, 2 * D), D ** (-0.5), 0.0), ('glu_bias', (2 * D,), 0.2, 0.0)] + norm_entries('norm_conv', D) + [('left_weight', (D, FF), D ** (-0.5), 0.0), ('left_bias', (FF,), 0.2, 0.0), ('right_weight', (3 * D, half_width), (3 * D) ** (-0.5), 0.0), ('right_bias', (half_width,), 0.2, 0.0)] + norm_entries('middle', FF) + [('depth_taps', (9, FF), 1.0 / 3.0, 0.0), ('point_weight', (FF, half_width), FF ** (-0.5), 0.0), ('point_bias', (half_width,), 0.2, 0.0)] + norm_entries('norm_attn', D) + attention_entries('attn') + norm_entries('norm_feed', D) + [('feed_in_weight', (D, FF), D ** (-0.5), 0.0), ('feed_in_bias', (FF,), 0.2, 0.0), ('feed_out_weight', (FF, D), FF ** (-0.5), 0.0), ('feed_out_bias', (D,), 0.2, 0.0)]

def decoder_layout():
    half_width = D // 2
    return norm_entries('norm_branch', D) + attention_entries('wide_self') + attention_entries('wide_cross') + norm_entries('norm_conv', D) + [('left_taps', (11, D), 11 ** (-0.5), 0.0), ('left_weight', (D, 2 * D), D ** (-0.5), 0.0), ('left_bias', (2 * D,), 0.2, 0.0), ('right_taps', (7, D), 7 ** (-0.5), 0.0), ('right_weight', (D, half_width), D ** (-0.5), 0.0), ('right_bias', (half_width,), 0.2, 0.0)] + norm_entries('middle', 2 * D) + [('out_taps', (7, 2 * D), 7 ** (-0.5), 0.0), ('out_weight', (2 * D, D), (2 * D) ** (-0.5), 0.0), ('out_bias', (D,), 0.2, 0.0)] + norm_entries('norm_self', D) + attention_entries('self') + norm_entries('norm_cross', D) + attention_entries('cross') + norm_entries('norm_feed', D) + [('feed_in_weight', (D, FF), D ** (-0.5), 0.0), ('feed_in_bias', (FF,), 0.2, 0.0), ('feed_out_weight', (FF, D), FF ** (-0.5), 0.0), ('feed_out_bias', (D,), 0.2, 0.0)]

def unpack(flat_vec, layout):
    tensors = {}
    offset = 0
    for label, dimensions, spread, center in layout:
        number = math.prod(dimensions)
        tensors[label] = flat_vec[offset:offset + number].reshape(dimensions)
        offset = offset + number
    return tensors

def product(left_op, right_op):
    return jnp.matmul(left_op, right_op, precision=lax.Precision.HIGHEST)

def linear(inputs, weight):
    return low_back(product(inputs, weight))

def rounded(array_in):
    return low(low_back(array_in))

def layer_norm(array_in, gain_vec, bias_vec):
    centered = array_in - lax.optimization_barrier(jnp.mean(array_in, axis=-1, keepdims=True))
    variance = lax.optimization_barrier(jnp.mean(centered * centered, axis=-1, keepdims=True))
    return centered * lax.rsqrt(variance + epsilon) * gain_vec + bias_vec

def segment_ids(lengths_row, token_count):
    ends_at = jnp.cumsum(lengths_row)
    places = jnp.arange(token_count, dtype=jnp.int32)
    return lax.optimization_barrier(jnp.sum((places[:, None] >= ends_at[None, :]).astype(jnp.int32), axis=1)).astype(jnp.int32)

def take_tap(array_in, segments, offset):
    if offset == 0:
        return array_in
    row_count = array_in.shape[0]
    padding = jnp.zeros((abs(offset),) + array_in.shape[1:], array_in.dtype)
    outside = jnp.full((abs(offset),), -1, jnp.int32)
    if offset > 0:
        shifted = jnp.concatenate([array_in[offset:], padding], axis=0)
        shifted_seg = jnp.concatenate([segments[offset:], outside], axis=0)
    else:
        shifted = jnp.concatenate([padding, array_in[:row_count + offset]], axis=0)
        shifted_seg = jnp.concatenate([outside, segments[:row_count + offset]], axis=0)
    inside = (shifted_seg == segments)[:, None]
    return jnp.where(inside, shifted, jnp.zeros_like(shifted))

def depthwise(array_in, segments, taps, first_tap):
    summed = jnp.zeros_like(array_in)
    for tap_index in range(taps.shape[0]):
        summed = summed + taps[tap_index] * take_tap(array_in, segments, first_tap + tap_index)
    return summed

def attention(query_in, source_in, tensors, prefix, head_count, allowed):
    queries = rounded(linear(query_in, tensors[prefix + '_query']))
    key_rows = rounded(linear(source_in, tensors[prefix + '_key']))
    value_rows = rounded(linear(source_in, tensors[prefix + '_value']))
    row_count, model_width = queries.shape
    key_count = key_rows.shape[0]
    head_size = model_width // head_count
    q_heads = queries.reshape(row_count, head_count, head_size).transpose(1, 0, 2)
    k_heads = key_rows.reshape(key_count, head_count, head_size).transpose(1, 2, 0)
    v_heads = value_rows.reshape(key_count, head_count, head_size).transpose(1, 0, 2)
    block_count = max(1, row_count // 512)
    block_rows = row_count // block_count
    scale_factor = head_size ** (-0.5)

    def one_block(pieces):
        q_block, mask_block = pieces
        scores = low_back(product(q_block, k_heads)) * scale_factor
        scores = jnp.where(mask_block[None], scores, blocked)
        top_score = lax.optimization_barrier(jnp.max(scores, axis=-1, keepdims=True))
        raw_weights = jnp.exp(scores - top_score)
        probabilities = raw_weights / lax.optimization_barrier(jnp.sum(raw_weights, axis=-1, keepdims=True))
        return rounded(product(low(probabilities), v_heads))
    q_split = q_heads.reshape(head_count, block_count, block_rows, head_size).transpose(1, 0, 2, 3)
    mask_split = allowed.reshape(block_count, block_rows, key_count)
    outputs = lax.map(jax.checkpoint(one_block), (q_split, mask_split))
    merged = outputs.transpose(0, 2, 1, 3).reshape(row_count, model_width)
    return linear(merged, tensors[prefix + '_output'])

def encoder_cell(source, segments, tensors):
    model_width = source.shape[1]
    half_width = model_width // 2
    feed_width = tensors['left_weight'].shape[1]
    normed = low(layer_norm(source, tensors['norm_glu_gain'], tensors['norm_glu_bias']))
    gated = linear(normed, tensors['glu_weight']) + tensors['glu_bias']
    after_glu = source + gated[:, :model_width] * jax.nn.sigmoid(gated[:, model_width:])
    normed = low(layer_norm(after_glu, tensors['norm_conv_gain'], tensors['norm_conv_bias']))
    left_side = jax.nn.gelu(linear(normed, tensors['left_weight']) + tensors['left_bias'])
    stacked = jnp.concatenate([take_tap(normed, segments, -1), normed, take_tap(normed, segments, 1)], axis=1)
    right_side = jax.nn.gelu(linear(stacked, tensors['right_weight']) + tensors['right_bias'])
    mixed = left_side + jnp.pad(right_side, ((0, 0), (0, feed_width - half_width)))
    middle = layer_norm(mixed, tensors['middle_gain'], tensors['middle_bias'])
    spread_out = depthwise(middle, segments, tensors['depth_taps'], -4)
    narrow = linear(low(spread_out), tensors['point_weight']) + tensors['point_bias']
    after_conv = after_glu + jnp.pad(narrow, ((0, 0), (0, model_width - half_width)))
    normed = low(layer_norm(after_conv, tensors['norm_attn_gain'], tensors['norm_attn_bias']))
    allowed = segments[:, None] == segments[None, :]
    after_attn = after_conv + attention(normed, normed, tensors, 'attn', HEADS, allowed)
    normed = low(layer_norm(after_attn, tensors['norm_feed_gain'], tensors['norm_feed_bias']))
    inner = jax.nn.gelu(linear(normed, tensors['feed_in_weight']) + tensors['feed_in_bias'])
    return after_attn + linear(low(inner), tensors['feed_out_weight']) + tensors['feed_out_bias']

def decoder_cell(target, memory, tgt_seg, src_seg, tensors):
    row_count, model_width = target.shape
    half_width = model_width // 2
    places = jnp.arange(row_count, dtype=jnp.int32)
    self_mask = (tgt_seg[:, None] == tgt_seg[None, :]) & (places[None, :] <= places[:, None])
    cross_mask = tgt_seg[:, None] == src_seg[None, :]
    normed = low(layer_norm(target, tensors['norm_branch_gain'], tensors['norm_branch_bias']))
    first_sum = target + attention(normed, normed, tensors, 'wide_self', BRANCH_HEADS, self_mask) + attention(normed, memory, tensors, 'wide_cross', BRANCH_HEADS, cross_mask)
    normed_conv = layer_norm(first_sum, tensors['norm_conv_gain'], tensors['norm_conv_bias'])
    left_in = low(depthwise(normed_conv, tgt_seg, tensors['left_taps'], -10))
    left_side = jax.nn.gelu(linear(left_in, tensors['left_weight']) + tensors['left_bias'])
    right_in = low(depthwise(normed_conv, tgt_seg, tensors['right_taps'], -6))
    right_side = linear(right_in, tensors['right_weight']) + tensors['right_bias']
    mixed = left_side + jnp.pad(right_side, ((0, 0), (0, 2 * model_width - half_width)))
    middle = layer_norm(mixed, tensors['middle_gain'], tensors['middle_bias'])
    out_in = low(depthwise(middle, tgt_seg, tensors['out_taps'], -6))
    second_sum = first_sum + linear(out_in, tensors['out_weight']) + tensors['out_bias']
    normed = low(layer_norm(second_sum, tensors['norm_self_gain'], tensors['norm_self_bias']))
    third_sum = second_sum + attention(normed, normed, tensors, 'self', HEADS, self_mask)
    normed = low(layer_norm(third_sum, tensors['norm_cross_gain'], tensors['norm_cross_bias']))
    fourth_sum = third_sum + attention(normed, memory, tensors, 'cross', HEADS, cross_mask)
    normed = low(layer_norm(fourth_sum, tensors['norm_feed_gain'], tensors['norm_feed_bias']))
    inner = jax.nn.silu(linear(normed, tensors['feed_in_weight']) + tensors['feed_in_bias'])
    return fourth_sum + linear(low(inner), tensors['feed_out_weight']) + tensors['feed_out_bias']

def unpack_cells(params_f):
    stacked = params_f.reshape(2, N_DP, QROWS, 128)
    enc_flat = stacked[0, :, :EROWS].reshape(-1)[:P_E]
    dec_flat = jnp.concatenate([stacked[1], stacked[0, :, EROWS:]], axis=1).reshape(-1)[:P_D]
    return (unpack(low(enc_flat), encoder_layout()), unpack(low(dec_flat), decoder_layout()))

def reference(tokens, lengths, params, cotangent):
    micro_count = tokens.shape[1]
    group_tokens = tokens.shape[2]
    pack_count = group_tokens // TOK
    pack_lengths = jnp.transpose(lengths, (1, 2, 0, 3)).reshape(micro_count * pack_count, 2, SENTS)

    def forward(tokens_f, params_f, probe):
        enc_tensors, dec_tensors = unpack_cells(params_f)
        sources = tokens_f[0].reshape(micro_count * pack_count, TOK, D)
        targets = tokens_f[1].reshape(micro_count * pack_count, TOK, D)
        probes = probe.reshape(micro_count * pack_count, TOK, D)

        def one_pack(pieces):
            source, target, probe_piece, lengths_pair = pieces
            src_seg = segment_ids(lengths_pair[0], TOK)
            tgt_seg = segment_ids(lengths_pair[1], TOK)
            memory = low_back(low(encoder_cell(source, src_seg, enc_tensors))) + probe_piece
            return decoder_cell(target, memory, tgt_seg, src_seg, dec_tensors)
        outputs = lax.map(jax.checkpoint(one_pack), (sources, targets, probes, pack_lengths))
        return outputs.reshape(micro_count, group_tokens, D)
    tokens_f = tokens.astype(jnp.float32)
    probe = jnp.zeros((micro_count, group_tokens, D), jnp.float32)
    outputs, pullback = jax.vjp(forward, tokens_f, params, probe)
    token_grads, param_grads, memory_grads = pullback(cotangent.astype(jnp.float32))
    results = jnp.stack([memory_grads.astype(jnp.bfloat16), outputs.astype(jnp.bfloat16)])
    return (results, token_grads, param_grads)
```

```python
import math

import jax
import jax.numpy as jnp
from jax import lax
from jax.experimental import pallas as pl
from jax.experimental.pallas import tpu as pltpu
from jax.sharding import PartitionSpec as P


class Names:
    def __getattr__(self, name):
        return name


N = Names()
D = 512
FF = 2048
HEADS = 8
BRANCH_HEADS = 16
LANES = 128
PACK = 256
EDGE = 16

epsilon = 1e-06
blocked = -1000000000.0
BF = jnp.bfloat16
F32 = jnp.float32


def attention_entries(prefix):
    return [(prefix + part, (D, D)) for part in (N._query, N._key, N._value, N._output)]


def norm_entries(prefix, width_of):
    return [(prefix + N._gain, (width_of,)), (prefix + N._bias, (width_of,))]


def encoder_layout():
    half_width = D // 2
    return (
        norm_entries(N.norm_glu, D)
        + [(N.glu_weight, (D, 2 * D)), (N.glu_bias, (2 * D,))]
        + norm_entries(N.norm_conv, D)
        + [
            (N.left_weight, (D, FF)),
            (N.left_bias, (FF,)),
            (N.right_weight, (3 * D, half_width)),
            (N.right_bias, (half_width,)),
        ]
        + norm_entries(N.middle, FF)
        + [
            (N.depth_taps, (9, FF)),
            (N.point_weight, (FF, half_width)),
            (N.point_bias, (half_width,)),
        ]
        + norm_entries(N.norm_attn, D)
        + attention_entries(N.attn)
        + norm_entries(N.norm_feed, D)
        + [
            (N.feed_in_weight, (D, FF)),
            (N.feed_in_bias, (FF,)),
            (N.feed_out_weight, (FF, D)),
            (N.feed_out_bias, (D,)),
        ]
    )


def decoder_layout():
    half_width = D // 2
    return (
        norm_entries(N.norm_branch, D)
        + attention_entries(N.wide_self)
        + attention_entries(N.wide_cross)
        + norm_entries(N.norm_conv, D)
        + [
            (N.left_taps, (11, D)),
            (N.left_weight, (D, 2 * D)),
            (N.left_bias, (2 * D,)),
            (N.right_taps, (7, D)),
            (N.right_weight, (D, half_width)),
            (N.right_bias, (half_width,)),
        ]
        + norm_entries(N.middle, 2 * D)
        + [
            (N.out_taps, (7, 2 * D)),
            (N.out_weight, (2 * D, D)),
            (N.out_bias, (D,)),
        ]
        + norm_entries(N.norm_self, D)
        + attention_entries(N.self)
        + norm_entries(N.norm_cross, D)
        + attention_entries(N.cross)
        + norm_entries(N.norm_feed, D)
        + [
            (N.feed_in_weight, (D, FF)),
            (N.feed_in_bias, (FF,)),
            (N.feed_out_weight, (FF, D)),
            (N.feed_out_bias, (D,)),
        ]
    )


class Table:
    def __init__(self, entries):
        self.at, self.weights, self.vectors, self.heights = {}, {}, {}, {}
        offset = weight_rows = vector_rows = 0
        for name, shape in entries:
            rows = math.prod(shape) // LANES
            self.at[name] = offset
            self.heights[name] = rows
            if len(shape) == 2 and shape[0] >= D:
                self.weights[name] = (weight_rows, shape[0], shape[1] // LANES)
                weight_rows += rows
            else:
                self.vectors[name] = (vector_rows, rows)
                vector_rows += rows
            offset += rows
        self.rows, self.weight_rows, self.vector_rows = offset, weight_rows, vector_rows


ENC = Table(encoder_layout())
DEC = Table(decoder_layout())
WEIGHT_ROWS = max(ENC.weight_rows, DEC.weight_rows)
VECTOR_ROWS = -(-max(ENC.vector_rows, DEC.vector_rows) // 16) * 16


def up_to(value, step):
    return -(-value // step) * step


AXES = ("section", "dp")


def pairs(count, move, sections):
    return [
        (s * count + i, s * count + j)
        for s in sections
        for i in range(count)
        for j in [move(i)]
        if j is not None
    ]


def swap(value, bit, count, sections):
    return lax.ppermute(value, AXES, pairs(count, lambda i: i ^ bit, sections))


def shift(value, step, count, sections, senders):
    def move(i):
        return i + 4 * step if i // 4 in senders and 0 <= i + 4 * step < count else None

    return lax.ppermute(value, AXES, pairs(count, move, sections))


def pick(z, options):
    out = options[0]
    for k in range(1, len(options)):
        if options[k] is not options[k - 1]:
            out = jnp.where(z >= k, options[k], out)
    return out


def by_neighbours(count):
    return count == 16


REDUCE_ORDER = [[3, 2, 1, 0], [3, 2, 0, 1], [0, 1, 3, 2], [0, 1, 2, 3]]
GATHER_ORDER = [[0, 1, 2, 3], [1, 0, 2, 3], [2, 1, 3, 0], [3, 2, 1, 0]]


def slot_devices(order, count):
    if not by_neighbours(count):
        return jnp.arange(count, dtype=jnp.int32)
    me = lax.axis_index("dp")
    z, y, c = me // 4, (me // 2) % 2, me % 2
    return jnp.stack(
        [
            pick(z, [own[k] for own in order]) * 4 + yy * 2 + cc
            for k in range(4)
            for yy in (y, 1 - y)
            for cc in (c, 1 - c)
        ]
    ).astype(jnp.int32)


def gather_slots(own, start, count):
    if not by_neighbours(count):
        held = lax.all_gather(own, "dp", axis=0)
        tails = lax.ppermute(held[:, start:], "section", [(0, 1)])
        tails = jnp.pad(tails, ((0, 0), (0, -tails.shape[1] % 16), (0, 0)))
        return [(held, j) for j in range(count)], [tails]
    z = lax.axis_index("dp") // 4
    both = (0, 1)
    near, far, near_other, far_other = [own], [], [], []
    up = down = own
    held = []
    ends = []

    def cross(steps):
        tails = jnp.stack([slot[start:] for k in steps for slot in (near[k], far[k])])
        ends.append(lax.ppermute(tails, "section", [(0, 1)]))

    for step in range(4):
        swapped = swap(near[step], 2, count, both)
        ups, downs = up, down
        if step == 3:
            cross((0, 1, 2))
        if step < 3:
            up = shift(ups, 1, count, both, [(0, 1, 2), (1, 2), (2,)][step])
            down = shift(downs, -1, count, both, [(3, 2, 1), (1, 2), (1,)][step])
        near_other.append(swap(near[step], 1, count, both))
        if step:
            far_other.append(swap(far[step - 1], 1, count, both))
        swapped, up, down, near_other, far_other = lax.optimization_barrier(
            (swapped, up, down, near_other, far_other)
        )
        far.append(swapped)
        held.append((up, down))
        if step == 0:
            near.append(pick(z, [down, up, up, up]))
        if step == 1:
            first_down = held[0][1]
            near.append(pick(z, [down, first_down, first_down, up]))
        if step == 2:
            near.append(pick(z, [down, held[1][1], held[1][0], up]))
    far_other.append(swap(far[3], 1, count, both))
    cross((3,))
    whole = [
        (slot, None) for k in range(4) for slot in (near[k], near_other[k], far[k], far_other[k])
    ]
    return whole, ends


def share_tails(tails, count):
    if not by_neighbours(count):
        return [(tails[0], j) for j in range(count)]
    others = [swap(part, 1, count, (1,)) for part in tails]
    return [
        (held[part], n) for part in range(2) for n in range((6, 2)[part]) for held in (tails, others)
    ]


def hand_over_tails(tails, count):
    if not by_neighbours(count):
        tail = lax.psum_scatter(tails[0], "dp", scatter_dimension=0, tiled=False)
        return lax.ppermute(tail, "section", [(1, 0)])
    same, other = tails
    mine = same.astype(F32) + swap(other, 1, count, (1,)).astype(F32)
    return lax.ppermute(mine.astype(BF), "section", [(1, 0)])


def reduce_slots(slots, tails, start, count):
    if not by_neighbours(count):
        return [lax.psum_scatter(slots[0], "dp", scatter_dimension=0, tiled=False)], tails
    z = lax.axis_index("dp") // 4
    both = (0, 1)
    low = BF

    def add(*terms):
        return sum([term.astype(F32) for term in terms])

    def with_tail(total, n):
        return total + jnp.pad(tails[n].astype(F32), ((start, 0), (0, 0)))

    def crossed(k):
        return [swap(slots[4 * k + 2 * f + 1], 1, count, both) for f in (1, 0)]

    def leaving(k):
        return with_tail(add(slots[4 * k + 2], others[k][0]), 2 * k + 1).astype(low)

    def arrived(k):
        return with_tail(add(*joined[k]), 2 * k)

    others = [crossed(0), crossed(1)]
    out = leaving(0)
    joined = []
    up = down = None
    for k in range(4):
        got = swap(out, 2, count, both)
        sent_up = sent_down = None
        if k:
            sent_up = shift(up, 1, count, both, range(k))
            sent_down = shift(down, -1, count, both, range(4 - k, 4))
        if k < 3:
            out = leaving(k + 1)
        if k < 2:
            others.append(crossed(k + 2))
        got, sent_up, sent_down, out, others = lax.optimization_barrier(
            (got, sent_up, sent_down, out, others)
        )
        joined.append([slots[4 * k], others[k][1], got])
        if k == 0:
            up = down = arrived(0).astype(low)
        if k in (1, 2):
            up_from = [[k, k - 1, k - 1, k - 1], [2, 1, 2, 2]][k - 1]
            down_from = [[k - 1, k - 1, k - 1, k], [2, 2, 1, 2]][k - 1]
            totals = [arrived(n) for n in range(k + 1)]
            up = (pick(z, [totals[n] for n in up_from]) + sent_up.astype(F32)).astype(low)
            down = (pick(z, [totals[n] for n in down_from]) + sent_down.astype(F32)).astype(low)
    return joined[3] + [sent_up, sent_down], tails[6]


def loop(count, body, together=1):
    together = math.gcd(count, together)

    def step(i, carry):
        for part in range(together):
            body(i * together + part)
        return carry

    lax.fori_loop(0, count // together, step, 0)


def at(i, size):
    if isinstance(i, int):
        return pl.ds(i * size, size)
    return pl.ds(pl.multiple_of(i * size, size), size)


def block_at(start, size):
    if isinstance(start, int):
        return pl.ds(start, size)
    return pl.ds(pl.multiple_of(start, 256), size)


class Kernel:
    def __init__(self, table, weight_ref, copies, refs, outgoing):
        self.table, self.w, self.copies, self.refs = table, weight_ref, copies, refs
        self.outgoing, self.sent = outgoing, []

    def __getitem__(self, name):
        copy = self.copies.pop(name, None)
        if copy is not None:
            copy.wait()
        return self.refs[name]

    def put(self, *names):
        for name in names:
            copy = self.outgoing.pop(name)
            copy.start()
            self.sent.append(copy)

    def columns(self, name, first, blocks):
        self.need(name)
        offset, height, unused = self.table.weights[name]
        parts = [
            self.w[block_at(offset + (first + i) * height, height), :]
            for i in range(blocks)
        ]
        return jnp.concatenate(parts, axis=1)

    def strip(self, name, first, rows, low=0):
        self.need(name)
        offset, height, blocks = self.table.weights[name]
        parts = [
            self.w[block_at(offset + j * height + low + first * rows, rows), :]
            for j in range(blocks)
        ]
        return jnp.concatenate(parts, axis=1)

    def need(self, name):
        copy = self.copies.pop(name, None)
        if copy is not None:
            copy.wait()

    def row(self, name, j, blocks=1):
        offset, unused = self.table.vectors[name]
        parts = [self.refs[N.vectors][pl.ds(offset + j + i, 1), :] for i in range(blocks)]
        return parts[0] if blocks == 1 else jnp.concatenate(parts, axis=1)

    def add_rows(self, name, j, value):
        offset, unused = self.table.vectors[name]
        blocks = value.shape[1] // LANES
        for i in range(blocks):
            part = value[:, i * LANES : (i + 1) * LANES]
            part = part.reshape(part.shape[0] // 8, 8, LANES).sum(axis=0)
            place = at(offset + j + i, 8)
            self.refs[N.vector_sums][place, :] += part


def fused(body, table, weight_array, weight_names, ins, outs, blanks, temps):
    in_names, out_names, blank_names = list(ins), list(outs), list(blanks)
    temp_names = list(temps)
    copies_in = list(weight_names) + in_names
    total = len(copies_in) + len(out_names)

    def kernel(*refs):
        refs = list(refs)
        weight_hbm = refs.pop(0)
        in_hbm = {n: refs.pop(0) for n in in_names}
        out_hbm = {n: refs.pop(0) for n in out_names}
        for unused in blank_names:
            refs.pop(0)
        weight_vmem = refs.pop(0)
        vmem = {n: refs.pop(0) for n in in_names + out_names + temp_names}
        sems = refs.pop(0)
        copies = {}
        for at_sem, name in enumerate(copies_in):
            if name in table.weights:
                offset, height, blocks = table.weights[name]
                place = pl.ds(offset, height * blocks)
                pair = (weight_hbm.at[place], weight_vmem.at[place])
            else:
                pair = (in_hbm[name], vmem[name])
            copies[name] = pltpu.make_async_copy(pair[0], pair[1], sems.at[at_sem])
        outgoing = {
            name: pltpu.make_async_copy(vmem[name], out_hbm[name], sems.at[len(copies_in) + i])
            for i, name in enumerate(out_names)
        }
        order = in_names + list(weight_names)
        for name in order:
            copies[name].start()
        k = Kernel(table, weight_vmem, copies, vmem, outgoing)
        body(k)
        for name in list(copies):
            copies.pop(name).wait()
        for name in list(outgoing):
            k.put(name)
        for copy in k.sent:
            copy.wait()

    any_spec = pl.BlockSpec(memory_space=pl.ANY)
    result = pl.pallas_call(
        kernel,
        out_shape=[outs[n] for n in out_names] + [blanks[n] for n in blank_names],
        in_specs=[any_spec] * (1 + len(in_names)),
        out_specs=[any_spec] * (len(out_names) + len(blank_names)),
        scratch_shapes=[pltpu.VMEM((weight_rows_used(table, weight_names), LANES), BF)]
        + [pltpu.VMEM(ins[n].shape, ins[n].dtype) for n in in_names]
        + [pltpu.VMEM(outs[n].shape, outs[n].dtype) for n in out_names]
        + [pltpu.VMEM(*temps[n]) for n in temp_names]
        + [pltpu.SemaphoreType.DMA((total,))],
        compiler_params=pltpu.CompilerParams(vmem_limit_bytes=62 * 2**20),
    )(weight_array, *[ins[n] for n in in_names])
    return dict(zip(out_names + blank_names, result))


def weight_rows_used(table, names):
    return max(table.weights[n][0] + table.heights[n] for n in names)


def dot(left, right):
    return jnp.dot(left, right, preferred_element_type=F32)


def dot_t(left, right):
    return lax.dot_general(left, right, (((1,), (1,)), ((), ())), preferred_element_type=F32)


def blocks_of(width):
    return range(width // LANES)


def lanes(j):
    return slice(j * LANES, (j + 1) * LANES)


def normalize(k, read, norm, width, size, block, write):
    def body(i):
        rows = at(i, block)
        values = [read(rows, j) for j in blocks_of(width)]
        mean = jnp.sum(sum(values), axis=1, keepdims=True) * (1.0 / width)
        values = [v - mean for v in values]
        var = jnp.sum(sum([v * v for v in values]), axis=1, keepdims=True) * (1.0 / width)
        r = lax.rsqrt(var + epsilon)
        for j in blocks_of(width):
            z = values[j] * r
            write(rows, j, z, z * k.row(norm + N._gain, j) + k.row(norm + N._bias, j), r)

    loop(size // block, body, 4)


def norm_gradient(k, norm, width, zs, douts, r):
    dzs = []
    for j in blocks_of(width):
        k.add_rows(norm + N._gain, j, douts[j] * zs[j])
        k.add_rows(norm + N._bias, j, douts[j])
        dzs.append(douts[j] * k.row(norm + N._gain, j))
    first = jnp.sum(sum(dzs), axis=1, keepdims=True) * (1.0 / width)
    second = jnp.sum(sum([a * b for a, b in zip(dzs, zs)]), axis=1, keepdims=True) * (1.0 / width)
    return [(dz - first - z * second) * r for dz, z in zip(dzs, zs)]


GELU_A = math.sqrt(2.0 / math.pi)
GELU_B = GELU_A * 0.044715


def gelu_both(x):
    square = x * x
    half = 0.5 + 0.5 * jnp.tanh(x * (GELU_A + GELU_B * square))
    value = x * half
    slope = half + 2.0 * value * (1.0 - half) * (GELU_A + 3.0 * GELU_B * square)
    return value, slope


def sigmoid(x):
    return 0.5 + 0.5 * jnp.tanh(0.5 * x)


def silu_both(x):
    s = sigmoid(x)
    value = x * s
    return value, s + value * (1.0 - s)


def head_mask(h, size):
    lane = lax.broadcasted_iota(jnp.int32, (1, LANES), 1)
    return ((lane >= h * size) & (lane < (h + 1) * size)).astype(BF)


class Group:
    def __init__(self, index, **refs):
        groups = D // LANES
        pack, column = index // groups, lax.rem(index, groups)
        self.index, self.pack = index, pack
        self.rows, self.cols = at(pack, PACK), at(column, LANES)
        for name, ref in refs.items():
            setattr(self, name, ref[self.rows, self.cols])


def in_turn(count, stages):
    for k in range(count + max(delay for unused, delay in stages)):
        for stage, delay in stages:
            if 0 <= k - delay < count:
                stage(k - delay)


def attend(q, key, value, caps, probs, out, heads, tokens):
    size = D // heads
    per = LANES // size
    scale = size ** (-0.5) * math.log2(math.e)
    together = 4
    halves = [slice(0, LANES), slice(LANES, PACK)]

    def body(step):
        groups, scores, weights, parts = {}, {}, {}, {}

        def score(i):
            g, h = divmod(i, per)
            if h == 0:
                groups[g] = Group(step * together + g, q=q, key=key, value=value)
                groups[g].value = groups[g].value.T
                parts[g] = []
            masked = groups[g].key * head_mask(h, size)
            scores[i] = [dot_t(masked, groups[g].q[half]) for half in halves]

        def soften(i):
            g, h = divmod(i, per)
            done = []
            for half, s in zip(halves, scores.pop(i)):
                s = jnp.minimum(s * scale, caps[groups[g].pack, :, half])
                e = jnp.exp2(s - jnp.max(s, axis=0, keepdims=True))
                done.append((e * (1.0 / jnp.sum(e, axis=0, keepdims=True))).astype(BF))
            weights[i] = jnp.concatenate(done, axis=1)
            probs[at(groups[g].index * per + h, PACK), :] = weights[i]

        def collect(i):
            g, h = divmod(i, per)
            group = groups[g]
            parts[g].append(dot(group.value[h * size : (h + 1) * size], weights.pop(i)))
            if h == per - 1:
                out[group.rows, group.cols] = jnp.concatenate(parts[g], axis=0).T.astype(BF)

        in_turn(together * per, [(score, 0), (soften, 2), (collect, 3)])

    loop((tokens // PACK) * (D // LANES) // together, body)


def attend_back(q, key, value, probs, dout, dq, dkey, dvalue, heads, tokens):
    size = D // heads
    per = LANES // size
    scale = size ** (-0.5)
    together = 4
    masks = [head_mask(h, size) for h in range(per)]

    def body(step):
        groups, grads, weights, moved, parts = {}, {}, {}, {}, {}

        def first(i):
            g, h = divmod(i, per)
            if h == 0:
                groups[g] = Group(
                    step * together + g, q=q, key=key, value=value, dout=dout
                )
                groups[g].key = groups[g].key.T
                weights[g], moved[g], parts[g] = [], [], []
            grads[i] = dot_t(groups[g].value * masks[h], groups[g].dout)

        def soften(i):
            g, h = divmod(i, per)
            dp = grads.pop(i)
            low = probs[at(groups[g].index * per + h, PACK), :]
            wide = low.astype(F32)
            mean = jnp.sum(wide * dp, axis=0, keepdims=True)
            mean = mean / jnp.sum(wide, axis=0, keepdims=True)
            weights[g].append(low)
            moved[g].append((wide * (dp - mean)).astype(BF))

        def collect(i):
            g, h = divmod(i, per)
            group = groups[g]
            parts[g].append(dot(group.key[h * size : (h + 1) * size], moved[g][h]))
            if h == per - 1:
                douts = jnp.concatenate([group.dout * mask for mask in masks], axis=0)
                queries = jnp.concatenate([group.q * mask for mask in masks], axis=0)
                place = (group.rows, group.cols)
                dvalue[place] = dot(jnp.concatenate(weights[g], axis=1), douts).astype(BF)
                dkey[place] = (dot(jnp.concatenate(moved[g], axis=1), queries) * scale).astype(BF)
                dq[place] = (jnp.concatenate(parts[g], axis=0).T * scale).astype(BF)

        in_turn(together * per, [(first, 0), (soften, 2), (collect, 3)])

    loop((tokens // PACK) * (D // LANES) // together, body)


def chunks(count, product, finish):
    held = {}

    def ask(j):
        held[j] = product(j)

    in_turn(count, [(ask, 0), (lambda j: finish(j, held.pop(j)), 1)])


def project(k, name, x, out):
    def finish(j, total):
        out[:, at(j, 256)] = total.astype(BF)

    chunks(out.shape[1] // 256, lambda j: dot(x[...], k.columns(name, 2 * j, 2)), finish)


def project_back(k, terms, write, height, low=0):
    def product(j):
        return sum([dot_t(dout[...], k.strip(name, j, 256, low)) for name, dout in terms])

    chunks(height // 256, product, write)


def same_segment(segments, base, block, moves):
    here = segments[pl.ds(base + EDGE, block), :]
    return {
        move: jnp.where(segments[pl.ds(base + (EDGE + move), block), :] == here, 1.0, 0.0)
        for move in moves
        if move
    }


def masked(ref, base, block, j, move, held):
    value = ref.load(base + move, block, j)
    return value * held[move] if move else value


def taps_forward(k, name, moves, source, segments, out, width, size):
    block = 16

    def body(i):
        base = pl.multiple_of(i * block, block)
        held = same_segment(segments, base, block, moves)
        for j in blocks_of(width):
            total = jnp.zeros((block, LANES), F32)
            for tap, move in enumerate(moves):
                value = masked(source, base, block, j, move, held)
                total = total + value * k.row(name, tap * (width // LANES) + j)
            out[pl.ds(base, block), lanes(j)] = total.astype(out.dtype)

    loop(size // block, body, 2)


def taps_back(k, terms, center, segments, width, size, write):
    block = 32

    def body(i):
        base = pl.multiple_of(i * block, block)
        rows = pl.ds(base, block)
        held = same_segment(
            segments, base, block, sorted({-move for term in terms for move in term[1]})
        )
        for j in blocks_of(width):
            total = jnp.zeros((block, LANES), F32)
            here = center(rows, j)
            for name, moves, dout in terms:
                for tap, move in enumerate(moves):
                    entry = tap * (width // LANES) + j
                    value = masked(dout, base, block, j, -move, held)
                    total = total + value * k.row(name, entry)
                    k.add_rows(name, entry, value * here)
            write(rows, j, total)

    loop(size // block, body)


class Edged:
    def __init__(self, ref, size):
        self.ref, self.size, self.height = ref, size, size + 2 * EDGE
        for j in range(ref.shape[0] // self.height):
            for start in (0, size + EDGE):
                ref[pl.ds(j * self.height + start, EDGE), :] = jnp.zeros((EDGE, LANES), F32)

    def part(self, first, blocks):
        place = pl.ds(first * self.height, blocks * self.height)
        return Edged(self.ref.at[place], self.size)

    def place(self, start, rows, j):
        return pl.ds(start + (j * self.height + EDGE), rows)

    def load(self, start, rows, j):
        return self.ref[self.place(start, rows, j), :]

    def store(self, start, rows, j, value):
        self.ref[self.place(start, rows, j), :] = value

    def store_wide(self, j, value, add=False):
        for half in range(2):
            place = pl.ds((2 * j + half) * self.height + EDGE, self.size)
            if add:
                self.ref[place, :] += value[:, lanes(half)]
            else:
                self.ref[place, :] = value[:, lanes(half)]


def moves_of(count, first):
    return [first + i for i in range(count)]


def lay_out(table, sources, starts, piece_rows, devices):
    slots = 8
    count = devices.shape[0]
    heights = [end - start for start, end in zip(starts, starts[1:] + [piece_rows])]
    arrays = []
    for items in sources:
        for array, unused in items:
            if not any(array is other for other in arrays):
                arrays.append(array)

    def spot(array):
        return [array is other for other in arrays].index(True)

    pieces = [
        (a, j, spot(items[j][0]), items[j][1])
        for j in range(count)
        for a, items in enumerate(sources)
    ]

    def kernel(*refs):
        refs = list(refs)
        device = refs.pop(0)
        held = [refs.pop(0) for unused in arrays]
        weight_hbm, vector_hbm, ring, stream, stage, vector_stage, in_sems, out_sems = refs

        def fetch(step):
            a, unused, which, lead = pieces[step]
            rows = pl.ds(0, up_to(heights[a], 16))
            source = held[which] if lead is None else held[which].at[lead]
            place = ring.at[step % slots, rows]
            return pltpu.make_async_copy(source.at[rows], place, in_sems.at[step % slots])

        for step in range(min(slots, len(pieces))):
            fetch(step).start()
        for step, (a, j, unused, unused_too) in enumerate(pieces):
            fetch(step).wait()
            base = device[j] * piece_rows + starts[a]
            whole, rest = heights[a] // 256, heights[a] % 256

            def body(i, base=base, step=step):
                stream[pl.ds(base + i * 256, 256), :] = ring[step % slots, at(i, 256), :].astype(F32)

            if whole:
                loop(whole, body)
            if rest:
                padded = up_to(rest, 16)
                value = ring[step % slots, whole * 256 : whole * 256 + padded, :].astype(F32)
                stream[pl.ds(base + whole * 256, rest), :] = value[:rest]
            if step + slots < len(pieces):
                fetch(step + slots).start()
        copies = []
        for at_sem, (name, (offset, height, blocks)) in enumerate(table.weights.items()):
            start = table.at[name]
            per = height // 512

            def body(i, offset=offset, height=height, blocks=blocks, start=start, per=per):
                j, part = i // per, lax.rem(i, per)
                taken = stream[pl.ds(start + part * (512 * blocks) + j, 512, stride=blocks), :]
                stage[block_at(offset + j * height + part * 512, 512), :] = taken.astype(BF)

            loop(blocks * per, body, 4)
            place = pl.ds(offset, height * blocks)
            copies.append(
                pltpu.make_async_copy(stage.at[place], weight_hbm.at[place], out_sems.at[at_sem])
            )
            copies[-1].start()
        for name, (offset, rows) in table.vectors.items():
            vector_stage[offset : offset + rows, :] = stream[pl.ds(table.at[name], rows), :]
        copies.append(
            pltpu.make_async_copy(vector_stage, vector_hbm, out_sems.at[len(table.weights)])
        )
        copies[-1].start()
        for copy in copies:
            copy.wait()

    any_spec = pl.BlockSpec(memory_space=pl.ANY)
    return tuple(
        pl.pallas_call(
            kernel,
            out_shape=[
                jax.ShapeDtypeStruct((WEIGHT_ROWS, LANES), BF),
                jax.ShapeDtypeStruct((VECTOR_ROWS, LANES), F32),
            ],
            in_specs=[pl.BlockSpec(memory_space=pltpu.SMEM)] + [any_spec] * len(arrays),
            out_specs=[any_spec] * 2,
            scratch_shapes=[
                pltpu.VMEM((slots, up_to(max(heights), 16), LANES), BF),
                pltpu.VMEM((up_to(count * piece_rows, 8) + 64, LANES), F32),
                pltpu.VMEM((WEIGHT_ROWS, LANES), BF),
                pltpu.VMEM((VECTOR_ROWS, LANES), F32),
                pltpu.SemaphoreType.DMA((slots,)),
                pltpu.SemaphoreType.DMA((len(table.weights) + 1,)),
            ],
            compiler_params=pltpu.CompilerParams(vmem_limit_bytes=62 * 2**20),
        )(devices, *arrays)
    )


def weight_gradients(table, products, arrays, sums, shapes, targets, starts, piece_rows, devices):
    count = devices.shape[0]
    heights = [end - start for start, end in zip(starts, starts[1:] + [piece_rows])]
    widths = [shapes[items[0][0]].shape[-2] for items in targets]
    names = list(arrays)
    slots = 4
    size = next(iter(arrays.values())).shape[0]
    widest = max(arrays[x].shape[1] for unused, x, unused_too in products)

    def kernel(*refs):
        refs = list(refs)
        device = refs.pop(0)
        hbm = [refs.pop(0) for unused in names + sums]
        out_hbm = [refs.pop(0) for unused in shapes]
        vmem = [refs.pop(0) for unused in names + sums]
        turned, stream, ring, in_sems, out_sems = refs
        copies = {}
        wanted = []
        for unused, x, dout in products:
            wanted += [x, dout]
        wanted = list(dict.fromkeys(wanted)) + list(range(len(sums)))
        spot = {n: i for i, n in enumerate(names)} | {i: len(names) + i for i in range(len(sums))}
        for name in wanted:
            i = spot[name]
            copies[name] = pltpu.make_async_copy(hbm[i], vmem[i], in_sems.at[i])
            copies[name].start()

        def get(name):
            copy = copies.pop(name, None)
            if copy is not None:
                copy.wait()
            return vmem[spot[name]]

        last = None
        for name, x_name, dout_name in products:
            unused, height, blocks = table.weights[name]
            start = table.at[name]
            x, dout = get(x_name), get(dout_name)
            if x_name != last:
                last = x_name

                def turn(j, x=x):
                    turned[at(j, 256), :] = x[:, at(j, 256)].T

                loop(height // 256, turn, 2)
            per = height // 512

            def product(i):
                j, part = divmod(i, per)
                return dot(turned[at(part, 512), :], dout[:, at(j, 256)])

            def finish(i, total):
                j, part = divmod(i, per)
                base = start + part * (512 * blocks) + 2 * j
                for half in range(2):
                    stream[pl.ds(base + half, 512, stride=blocks), :] = total[:, lanes(half)]

            chunks((blocks // 2) * per, product, finish)
        parts = [get(i) for i in range(len(sums))]
        for name, (offset, rows) in table.vectors.items():
            total = None
            for part in parts:
                for s in range(8):
                    value = part[pl.ds(offset * 8 + s, rows, stride=8), :]
                    total = value if total is None else total + value
            stream[pl.ds(table.at[name], rows), :] = total
        if table.rows < count * piece_rows:
            stream[pl.ds(table.rows, count * piece_rows - table.rows), :] = jnp.zeros(
                (count * piece_rows - table.rows, LANES), F32
            )
        sent = []
        if len(starts) == 1:
            gap = up_to(heights[0], 16)
            for slot in range(slots):
                ring[slot, gap : widths[0], :] = jnp.zeros((widths[0] - gap, LANES), BF)
        pieces = [(a, j) for j in range(count) for a in range(len(starts))]
        for step, (a, j) in enumerate(pieces):
            slot = step % slots
            base = device[j] * piece_rows + starts[a]
            if step >= slots:
                sent[step - slots].wait()
            height = up_to(heights[a], 16)
            whole, rest = height // 256, height % 256

            def body(i, base=base, slot=slot):
                ring[slot, at(i, 256), :] = stream[pl.ds(base + i * 256, 256), :].astype(BF)

            if whole:
                loop(whole, body)
            if rest:
                ring[slot, whole * 256 : whole * 256 + rest, :] = stream[
                    pl.ds(base + whole * 256, rest), :
                ].astype(BF)
            which, lead = targets[a][j]
            target = out_hbm[which] if lead is None else out_hbm[which].at[lead]
            sent.append(
                pltpu.make_async_copy(
                    ring.at[slot, pl.ds(0, widths[a])], target, out_sems.at[slot]
                )
            )
            sent[-1].start()
        for copy in sent[-slots:]:
            copy.wait()

    any_spec = pl.BlockSpec(memory_space=pl.ANY)
    given = [arrays[n] for n in names] + sums
    return tuple(
        pl.pallas_call(
            kernel,
            out_shape=list(shapes),
            in_specs=[pl.BlockSpec(memory_space=pltpu.SMEM)] + [any_spec] * len(given),
            out_specs=[any_spec] * len(shapes),
            scratch_shapes=[pltpu.VMEM(a.shape, a.dtype) for a in given]
            + [
                pltpu.VMEM((widest, size), BF),
                pltpu.VMEM((up_to(count * piece_rows, 8) + 64, LANES), F32),
                pltpu.VMEM((slots, max(widths), LANES), BF),
                pltpu.SemaphoreType.DMA((len(given),)),
                pltpu.SemaphoreType.DMA((slots,)),
            ],
            compiler_params=pltpu.CompilerParams(vmem_limit_bytes=63 * 2**20),
        )(devices, *given)
    )


def add_up(parts, tail, start, size):
    block = 512
    height = parts[0].shape[0]

    def kernel(*refs):
        refs = list(refs)
        held = [refs.pop(0) for unused in parts]
        tail_ref, out_hbm, stage, sem = refs
        for first in range(0, height, block):
            rows = slice(first, min(first + block, height))
            stage[rows, :] = sum([p[rows, :].astype(F32) for p in held])
        stage[start:size, :] += tail_ref[...].astype(F32)[: size - start]
        copy = pltpu.make_async_copy(stage.at[pl.ds(0, size)], out_hbm.at[:, 0, :], sem)
        copy.start()
        copy.wait()

    return pl.pallas_call(
        kernel,
        out_shape=jax.ShapeDtypeStruct((size, 1, LANES), F32),
        in_specs=[pl.BlockSpec(memory_space=pltpu.VMEM)] * (len(parts) + 1),
        out_specs=pl.BlockSpec(memory_space=pl.ANY),
        scratch_shapes=[pltpu.VMEM((height, LANES), F32), pltpu.SemaphoreType.DMA],
        compiler_params=pltpu.CompilerParams(vmem_limit_bytes=32 * 2**20),
    )(*parts, tail)


def keeping(k, norm, write_out):
    z_ref, r_ref = k[N.z_ + norm], k[N.r_ + norm]

    def write(rows, j, z, out, r):
        z_ref[rows, lanes(j)] = z.astype(BF)
        if j == 0:
            r_ref[rows, :] = jnp.broadcast_to(r, (rows.size, LANES))
        write_out(rows, j, out)

    return write


def to_low(ref):
    def write(rows, j, out):
        ref[rows, lanes(j)] = out.astype(BF)

    return write


def rows_of(ref):
    return lambda rows, j: ref[rows, lanes(j)].astype(F32)


def encoder_forward(k):
    vectors, x0 = k[N.vectors], k[N.tokens]
    size = x0.shape[0]
    h1, x1, glu_a, glu_s = k[N.h1], k[N.x1], k[N.glu_a], k[N.glu_s]
    normalize(k, rows_of(x0), N.norm_glu, D, size, 64, keeping(k, N.norm_glu, to_low(h1)))
    k.put(N.h1)
    def both(j):
        return [dot(h1[...], k.columns(N.glu_weight, c, 2)) for c in (2 * j, 4 + 2 * j)]

    def gate(j, totals):
        a = totals[0] + k.row(N.glu_bias, 2 * j, 2)
        s = sigmoid(totals[1] + k.row(N.glu_bias, 4 + 2 * j, 2))
        cols = at(j, 256)
        glu_a[:, cols] = a.astype(BF)
        glu_s[:, cols] = s.astype(BF)
        x1[:, cols] = x0[:, cols].astype(F32) + a * s

    chunks(2, both, gate)
    k.put(N.glu_a, N.glu_s)
    h2, stacked, mask = k[N.h2], k[N.stacked], k[N.mask]
    edged = Edged(k[N.edged], size)

    def keep_h2(rows, j, out):
        low = out.astype(BF)
        h2[rows, lanes(j)] = low
        stacked[rows, lanes(j + 4)] = low
        edged.store(rows.start, rows.size, j, low.astype(F32))

    normalize(k, rows_of(x1), N.norm_conv, D, size, 64, keeping(k, N.norm_conv, keep_h2))

    def stack(i):
        base = pl.multiple_of(i * 32, 32)
        held = same_segment(mask, base, 32, (-1, 1))
        for first, move in ((0, -1), (8, 1)):
            for j in blocks_of(D):
                value = masked(edged, base, 32, j, move, held)
                stacked[pl.ds(base, 32), lanes(first + j)] = value.astype(BF)

    loop(size // 32, stack, 4)
    k.put(N.h2, N.stacked)
    mixed = Edged(k[N.mixed], size)
    slope_left, slope_right = k[N.slope_left], k[N.slope_right]
    def left(j):
        if j == FF // 256:
            return dot(stacked[...], k.columns(N.right_weight, 0, 2))
        return dot(h2[...], k.columns(N.left_weight, 2 * j, 2))

    def keep_left(j, total):
        if j == FF // 256:
            value, slope = gelu_both(total + k.row(N.right_bias, 0, 2))
            mixed.store_wide(0, value, True)
            slope_right[...] = slope.astype(BF)
            return
        value, slope = gelu_both(total + k.row(N.left_bias, 2 * j, 2))
        mixed.store_wide(j, value)
        slope_left[:, at(j, 256)] = slope.astype(BF)

    chunks(FF // 256 + 1, left, keep_left)
    k.put(N.slope_left, N.slope_right)
    z_middle, r_middle, spread = k[N.z_middle], k[N.r_middle], k[N.spread]

    def keep_middle(rows, j, z, out, r):
        z_middle[rows, lanes(j)] = z.astype(BF)
        mixed.store(rows.start, rows.size, j, out)
        if j == 0:
            r_middle[rows, :] = jnp.broadcast_to(r, (rows.size, LANES))

    normalize(
        k, lambda rows, j: mixed.load(rows.start, rows.size, j), N.middle, FF, size, 16, keep_middle
    )
    k.put(N.z_middle, N.r_middle)
    taps_forward(k, N.depth_taps, moves_of(9, -4), mixed, mask, spread, FF, size)
    k.put(N.spread)
    x2 = k[N.x2]
    x2[:, 0:256] = (
        x1[:, 0:256]
        + dot(spread[...], k.columns(N.point_weight, 0, 2))
        + k.row(N.point_bias, 0, 2)
    )
    x2[:, 256:512] = x1[:, 256:512]
    h3, q, key, value = k[N.h3], k[N.q], k[N.key], k[N.value]
    normalize(k, rows_of(x2), N.norm_attn, D, size, 64, keeping(k, N.norm_attn, to_low(h3)))
    project(k, N.attn_query, h3, q)
    project(k, N.attn_key, h3, key)
    project(k, N.attn_value, h3, value)
    k.put(N.h3, N.q, N.key, N.value)
    attend(q, key, value, k[N.caps], k[N.probs], k[N.heads], HEADS, size)
    heads, x3, h4, inner, slope_feed = k[N.heads], k[N.x3], k[N.h4], k[N.inner], k[N.slope_feed]
    k.put(N.probs, N.heads)
    add_product(k, N.attn_output, heads, x2, x3)
    normalize(k, rows_of(x3), N.norm_feed, D, size, 64, keeping(k, N.norm_feed, to_low(h4)))
    feed_in(k, h4, inner, slope_feed, gelu_both)
    k.put(N.h4, N.inner, N.slope_feed)
    feed_out(k, inner, x3, k[N.memory])


def add_product(k, name, x, base, out):
    def finish(j, total):
        cols = at(j, 256)
        out[:, cols] = base[:, cols] + total

    chunks(D // 256, lambda j: dot(x[...], k.columns(name, 2 * j, 2)), finish)


def feed_in(k, h, inner, slopes, both):
    def finish(j, total):
        value, slope = both(total + k.row(N.feed_in_bias, 2 * j, 2))
        inner[:, at(j, 256)] = value.astype(BF)
        slopes[:, at(j, 256)] = slope.astype(BF)

    chunks(FF // 256, lambda j: dot(h[...], k.columns(N.feed_in_weight, 2 * j, 2)), finish)


def feed_out(k, inner, base, out):
    def finish(j, total):
        cols = at(j, 256)
        out[:, cols] = (base[:, cols] + total + k.row(N.feed_out_bias, 2 * j, 2)).astype(BF)

    chunks(D // 256, lambda j: dot(inner[...], k.columns(N.feed_out_weight, 2 * j, 2)), finish)


def add_all_rows(k, name, ref, width):
    def body(i):
        for j in blocks_of(width):
            k.add_rows(name, j, ref[at(i, 64), lanes(j)].astype(F32))

    loop(ref.shape[0] // 64, body, 4)


def feed_back(k, dout_low, slopes, dpre, dh):
    def finish(j, total):
        grad = total * slopes[:, at(j, 256)].astype(F32)
        k.add_rows(N.feed_in_bias, 2 * j, grad)
        dpre[:, at(j, 256)] = grad.astype(BF)

    chunks(FF // 256, lambda j: dot_t(dout_low[...], k.strip(N.feed_out_weight, j, 256)), finish)

    def write(j, total):
        dh[:, at(j, 256)] = total

    project_back(k, [(N.feed_in_weight, dpre)], write, D)


def add_norm_back(k, norm, size, dh, base, out, low=None):
    z, r = k[N.z_ + norm], k[N.r_ + norm]

    def body(i):
        rows = at(i, 32)
        zs = [z[rows, lanes(j)].astype(F32) for j in blocks_of(D)]
        douts = [dh[rows, lanes(j)] for j in blocks_of(D)]
        grads = norm_gradient(k, norm, D, zs, douts, r[rows, :])
        for j in blocks_of(D):
            total = base(rows, j) + grads[j]
            out[rows, lanes(j)] = total
            if low is not None:
                low[rows, lanes(j)] = total.astype(BF)

    loop(size // 32, body, 4)


def output_of(k, norm):
    z = k[N.z_ + norm]

    def read(rows, j):
        value = z[rows, lanes(j)].astype(F32) * k.row(norm + N._gain, j)
        return value + k.row(norm + N._bias, j)

    return read


def encoder_back(k):
    k[N.vectors]
    dmem = k[N.returned]
    size = dmem.shape[0]
    sums = k[N.vector_sums]
    sums[...] = jnp.zeros(sums.shape, F32)
    dpre, dh, dx = k[N.dpre_feed], k[N.dh], k[N.dx]
    add_all_rows(k, N.feed_out_bias, dmem, D)
    feed_back(k, dmem, k[N.slope_feed], dpre, dh)
    k.put(N.dpre_feed)
    d3 = k[N.d3]
    add_norm_back(k, N.norm_feed, size, dh, rows_of(dmem), dx, d3)
    k.put(N.d3)

    dheads = k[N.dheads]

    def write_heads(j, total):
        dheads[:, at(j, 256)] = total.astype(BF)

    project_back(k, [(N.attn_output, d3)], write_heads, D)
    dq, dkey, dvalue = k[N.dq], k[N.dkey], k[N.dvalue]
    attend_back(
        k[N.q], k[N.key], k[N.value], k[N.probs], dheads, dq, dkey, dvalue, HEADS, size
    )
    k.put(N.dq, N.dkey, N.dvalue)
    def write_dh(j, total):
        dh[:, at(j, 256)] = total

    project_back(
        k, [(N.attn_query, dq), (N.attn_key, dkey), (N.attn_value, dvalue)], write_dh, D
    )
    add_norm_back(k, N.norm_attn, size, dh, rows_of(dx), dx)
    d2, mask = k[N.d2], k[N.mask]
    dspread = Edged(k[N.dspread], size)
    d2[...] = dx[:, 0:256].astype(BF)
    k.put(N.d2)
    add_all_rows(k, N.point_bias, dx.at[:, 0:256], 256)

    def write_spread(j, total):
        dspread.store_wide(j, total)

    project_back(k, [(N.point_weight, d2)], write_spread, FF)
    z_middle, r_middle = k[N.z_middle], k[N.r_middle]

    dmiddle = k[N.dmiddle]

    def write_middle(rows, j, total):
        dmiddle[rows, lanes(j)] = total
    taps_back(
        k, [(N.depth_taps, moves_of(9, -4), dspread)], output_of(k, N.middle), mask, FF, size, write_middle
    )
    slope_left, slope_right = k[N.slope_left], k[N.slope_right]
    dleft, dright = k[N.dleft], k[N.dright]

    def middle(i):
        rows = at(i, 16)
        zs = [z_middle[rows, lanes(j)].astype(F32) for j in blocks_of(FF)]
        douts = [dmiddle[rows, lanes(j)] for j in blocks_of(FF)]
        grads = norm_gradient(k, N.middle, FF, zs, douts, r_middle[rows, :])
        for j in blocks_of(FF):
            grad = grads[j] * slope_left[rows, lanes(j)].astype(F32)
            k.add_rows(N.left_bias, j, grad)
            dleft[rows, lanes(j)] = grad.astype(BF)
        for j in range(2):
            grad = grads[j] * slope_right[rows, lanes(j)].astype(F32)
            k.add_rows(N.right_bias, j, grad)
            dright[rows, lanes(j)] = grad.astype(BF)

    loop(size // 16, middle, 4)
    k.put(N.dleft, N.dright)
    edged, edged_too = dspread.part(0, 4), dspread.part(4, 4)

    def write_before(j, total):
        edged.store_wide(j, total)

    def write_after(j, total):
        edged_too.store_wide(j, total)

    project_back(k, [(N.right_weight, dright)], write_before, D, 0)
    project_back(k, [(N.right_weight, dright)], write_after, D, 2 * D)
    def conv(j):
        total = dot_t(dleft[...], k.strip(N.left_weight, j, 256))
        return total + dot_t(dright[...], k.strip(N.right_weight, j, 256, D))

    chunks(D // 256, conv, write_dh)

    def untap(i):
        base = pl.multiple_of(i * 32, 32)
        held = same_segment(mask, base, 32, (-1, 1))
        for j in blocks_of(D):
            dh[pl.ds(base, 32), lanes(j)] += masked(edged, base, 32, j, 1, held) + masked(
                edged_too, base, 32, j, -1, held
            )

    loop(size // 32, untap, 4)
    add_norm_back(k, N.norm_conv, size, dh, rows_of(dx), dx)
    glu_a, glu_s, dglu = k[N.glu_a], k[N.glu_s], k[N.dglu]

    def gate(i):
        rows = at(i, 32)
        for j in blocks_of(D):
            a, s = glu_a[rows, lanes(j)].astype(F32), glu_s[rows, lanes(j)].astype(F32)
            d = dx[rows, lanes(j)]
            da = d * s
            dg = da * a * (1.0 - s)
            k.add_rows(N.glu_bias, j, da)
            k.add_rows(N.glu_bias, 4 + j, dg)
            dglu[rows, lanes(j)] = da.astype(BF)
            dglu[rows, lanes(4 + j)] = dg.astype(BF)

    loop(size // 32, gate, 4)
    k.put(N.dglu)
    project_back(k, [(N.glu_weight, dglu)], write_dh, D)
    add_norm_back(k, N.norm_glu, size, dh, rows_of(dx), k[N.token_grad])


def decoder_start(k):
    k[N.vectors]
    y0, h = k[N.tokens], k[N.h]
    size = y0.shape[0]
    normalize(k, rows_of(y0), N.norm_branch, D, size, 64, keeping(k, N.norm_branch, to_low(h)))
    k.put(N.h)
    q, key, value = k[N.q_ws], k[N.k_ws], k[N.v_ws]
    project(k, N.wide_self_query, h, q)
    project(k, N.wide_self_key, h, key)
    project(k, N.wide_self_value, h, value)
    k.put(N.q_ws, N.k_ws, N.v_ws)
    project(k, N.wide_cross_query, h, k[N.q_wc])
    k.put(N.q_wc)
    attend(q, key, value, k[N.caps], k[N.p_ws], k[N.o_ws], BRANCH_HEADS, size)
    k.put(N.p_ws, N.o_ws)
    o, base = k[N.o_ws], k[N.base]
    def finish(j, total):
        cols = at(j, 256)
        base[:, cols] = y0[:, cols].astype(F32) + total

    chunks(D // 256, lambda j: dot(o[...], k.columns(N.wide_self_output, 2 * j, 2)), finish)


def decoder_forward(k):
    k[N.vectors]
    memory = k[N.memory]
    size = memory.shape[0]
    project(k, N.wide_cross_key, memory, k[N.k_wc])
    project(k, N.wide_cross_value, memory, k[N.v_wc])
    k.put(N.k_wc, N.v_wc)
    attend(
        k[N.q_wc], k[N.k_wc], k[N.v_wc], k[N.caps_cross], k[N.p_wc], k[N.o_wc], BRANCH_HEADS, size
    )
    k.put(N.p_wc, N.o_wc)
    y1, edged = k[N.y1], Edged(k[N.edged], size)
    add_product(k, N.wide_cross_output, k[N.o_wc], k[N.base], y1)

    def keep_conv(rows, j, out):
        edged.store(rows.start, rows.size, j, out)

    normalize(k, rows_of(y1), N.norm_conv, D, size, 64, keeping(k, N.norm_conv, keep_conv))
    mask, left_in, right_in = k[N.mask], k[N.left_in], k[N.right_in]
    taps_forward(k, N.left_taps, moves_of(11, -10), edged, mask, left_in, D, size)
    taps_forward(k, N.right_taps, moves_of(7, -6), edged, mask, right_in, D, size)
    k.put(N.left_in, N.right_in)
    mixed, slope_left = Edged(k[N.mixed], size), k[N.slope_left]
    def left(j):
        if j == 2 * D // 256:
            return dot(right_in[...], k.columns(N.right_weight, 0, 2))
        return dot(left_in[...], k.columns(N.left_weight, 2 * j, 2))

    def keep_left(j, total):
        if j == 2 * D // 256:
            mixed.store_wide(0, total + k.row(N.right_bias, 0, 2), True)
            return
        value, slope = gelu_both(total + k.row(N.left_bias, 2 * j, 2))
        mixed.store_wide(j, value)
        slope_left[:, at(j, 256)] = slope.astype(BF)

    chunks(2 * D // 256 + 1, left, keep_left)
    k.put(N.slope_left)
    z_middle, r_middle = k[N.z_middle], k[N.r_middle]

    def keep_middle(rows, j, z, out, r):
        z_middle[rows, lanes(j)] = z.astype(BF)
        mixed.store(rows.start, rows.size, j, out)
        if j == 0:
            r_middle[rows, :] = jnp.broadcast_to(r, (rows.size, LANES))

    normalize(
        k, lambda rows, j: mixed.load(rows.start, rows.size, j), N.middle, 2 * D, size, 32, keep_middle
    )
    k.put(N.z_middle, N.r_middle)
    out_in, y2 = k[N.out_in], k[N.y2]
    taps_forward(k, N.out_taps, moves_of(7, -6), mixed, mask, out_in, 2 * D, size)
    k.put(N.out_in)
    def conv_out(j, total):
        cols = at(j, 256)
        y2[:, cols] = y1[:, cols] + total + k.row(N.out_bias, 2 * j, 2)

    chunks(D // 256, lambda j: dot(out_in[...], k.columns(N.out_weight, 2 * j, 2)), conv_out)
    h_s, y3 = k[N.h_s], k[N.y3]
    normalize(k, rows_of(y2), N.norm_self, D, size, 64, keeping(k, N.norm_self, to_low(h_s)))
    project(k, N.self_query, h_s, k[N.q_s])
    project(k, N.self_key, h_s, k[N.k_s])
    project(k, N.self_value, h_s, k[N.v_s])
    k.put(N.h_s, N.q_s, N.k_s, N.v_s)
    attend(k[N.q_s], k[N.k_s], k[N.v_s], k[N.caps], k[N.p_s], k[N.o_s], HEADS, size)
    k.put(N.p_s, N.o_s)
    add_product(k, N.self_output, k[N.o_s], y2, y3)
    h_c, y4 = k[N.h_c], k[N.y4]
    normalize(k, rows_of(y3), N.norm_cross, D, size, 64, keeping(k, N.norm_cross, to_low(h_c)))
    project(k, N.cross_query, h_c, k[N.q_c])
    project(k, N.cross_key, memory, k[N.k_c])
    project(k, N.cross_value, memory, k[N.v_c])
    k.put(N.h_c, N.q_c, N.k_c, N.v_c)
    attend(k[N.q_c], k[N.k_c], k[N.v_c], k[N.caps_cross], k[N.p_c], k[N.o_c], HEADS, size)
    k.put(N.p_c, N.o_c)
    add_product(k, N.cross_output, k[N.o_c], y3, y4)
    h_f, inner, slope_feed = k[N.h_f], k[N.inner], k[N.slope_feed]
    normalize(k, rows_of(y4), N.norm_feed, D, size, 64, keeping(k, N.norm_feed, to_low(h_f)))
    feed_in(k, h_f, inner, slope_feed, silu_both)
    k.put(N.h_f, N.inner, N.slope_feed)
    feed_out(k, inner, y4, k[N.output])


def decoder_back(k):
    k[N.vectors]
    dout = k[N.cotangent]
    size = dout.shape[0]
    sums = k[N.vector_sums]
    sums[...] = jnp.zeros(sums.shape, F32)
    dpre, dh, dx, dmem = k[N.dpre_feed], k[N.dh], k[N.dx], k[N.dmem]
    add_all_rows(k, N.feed_out_bias, dout, D)
    feed_back(k, dout, k[N.slope_feed], dpre, dh)
    k.put(N.dpre_feed)
    d4 = k[N.d4]
    add_norm_back(k, N.norm_feed, size, dh, rows_of(dout), dx, d4)
    k.put(N.d4)
    dheads = k[N.dheads]

    def write_heads(j, total):
        dheads[:, at(j, 256)] = total.astype(BF)

    def write_dh(j, total):
        dh[:, at(j, 256)] = total

    def write_dmem(j, total):
        dmem[:, at(j, 256)] = total

    project_back(k, [(N.cross_output, d4)], write_heads, D)
    dq, dkey, dvalue = k[N.dq_c], k[N.dk_c], k[N.dv_c]
    attend_back(k[N.q_c], k[N.k_c], k[N.v_c], k[N.p_c], dheads, dq, dkey, dvalue, HEADS, size)
    k.put(N.dq_c, N.dk_c, N.dv_c)
    project_back(k, [(N.cross_query, dq)], write_dh, D)
    project_back(k, [(N.cross_key, dkey), (N.cross_value, dvalue)], write_dmem, D)
    d3 = k[N.d3]
    add_norm_back(k, N.norm_cross, size, dh, rows_of(dx), dx, d3)
    k.put(N.d3)
    project_back(k, [(N.self_output, d3)], write_heads, D)
    dq, dkey, dvalue = k[N.dq_s], k[N.dk_s], k[N.dv_s]
    attend_back(k[N.q_s], k[N.k_s], k[N.v_s], k[N.p_s], dheads, dq, dkey, dvalue, HEADS, size)
    k.put(N.dq_s, N.dk_s, N.dv_s)
    project_back(
        k, [(N.self_query, dq), (N.self_key, dkey), (N.self_value, dvalue)], write_dh, D
    )
    d2 = k[N.d2]
    add_norm_back(k, N.norm_self, size, dh, rows_of(dx), dx, d2)
    k.put(N.d2)
    add_all_rows(k, N.out_bias, dx, D)
    dspread, mask = Edged(k[N.dspread], size), k[N.mask]

    def write_spread(j, total):
        dspread.store_wide(j, total)

    project_back(k, [(N.out_weight, d2)], write_spread, 2 * D)
    z_middle, r_middle = k[N.z_middle], k[N.r_middle]

    dmiddle = k[N.dmiddle]

    def write_middle(rows, j, total):
        dmiddle[rows, lanes(j)] = total
    taps_back(
        k, [(N.out_taps, moves_of(7, -6), dspread)], output_of(k, N.middle), mask, 2 * D, size, write_middle
    )
    slope_left, dleft, dright = k[N.slope_left], k[N.dleft], k[N.dright]

    def middle(i):
        rows = at(i, 16)
        zs = [z_middle[rows, lanes(j)].astype(F32) for j in blocks_of(2 * D)]
        douts = [dmiddle[rows, lanes(j)] for j in blocks_of(2 * D)]
        grads = norm_gradient(k, N.middle, 2 * D, zs, douts, r_middle[rows, :])
        for j in blocks_of(2 * D):
            grad = grads[j] * slope_left[rows, lanes(j)].astype(F32)
            k.add_rows(N.left_bias, j, grad)
            dleft[rows, lanes(j)] = grad.astype(BF)
        for j in range(2):
            k.add_rows(N.right_bias, j, grads[j])
            dright[rows, lanes(j)] = grads[j].astype(BF)

    loop(size // 16, middle, 4)
    k.put(N.dleft, N.dright)
    dleft_in, dright_in = dspread.part(0, 4), dspread.part(4, 4)

    def write_left(j, total):
        dleft_in.store_wide(j, total)

    def write_right(j, total):
        dright_in.store_wide(j, total)

    project_back(k, [(N.left_weight, dleft)], write_left, D)
    project_back(k, [(N.right_weight, dright)], write_right, D)
    def write_conv(rows, j, total):
        dh[rows, lanes(j)] = total

    taps_back(
        k,
        [(N.left_taps, moves_of(11, -10), dleft_in), (N.right_taps, moves_of(7, -6), dright_in)],
        output_of(k, N.norm_conv),
        mask,
        D,
        size,
        write_conv,
    )
    d1 = k[N.d1]
    add_norm_back(k, N.norm_conv, size, dh, rows_of(dx), dx, d1)
    k.put(N.d1, N.dx)
    project_back(k, [(N.wide_cross_output, d1)], write_heads, D)
    dq, dkey, dvalue = k[N.dq_wc], k[N.dk_wc], k[N.dv_wc]
    attend_back(
        k[N.q_wc], k[N.k_wc], k[N.v_wc], k[N.p_wc], dheads, dq, dkey, dvalue, BRANCH_HEADS, size
    )
    k.put(N.dq_wc, N.dk_wc, N.dv_wc)
    sent = k[N.sent]

    def write_sent(j, total):
        sent[:, at(j, 256)] = (dmem[:, at(j, 256)] + total).astype(BF)

    project_back(k, [(N.wide_cross_key, dkey), (N.wide_cross_value, dvalue)], write_sent, D)


def branch_back(k):
    k[N.vectors]
    d1 = k[N.d1]
    size = d1.shape[0]
    sums = k[N.vector_sums]
    sums[...] = jnp.zeros(sums.shape, F32)
    dheads, dh = k[N.dheads], k[N.dh]

    def write_heads(j, total):
        dheads[:, at(j, 256)] = total.astype(BF)

    project_back(k, [(N.wide_self_output, d1)], write_heads, D)
    dq, dkey, dvalue = k[N.dq_ws], k[N.dk_ws], k[N.dv_ws]
    attend_back(
        k[N.q_ws], k[N.k_ws], k[N.v_ws], k[N.p_ws], dheads, dq, dkey, dvalue, BRANCH_HEADS, size
    )
    k.put(N.dq_ws, N.dk_ws, N.dv_ws)

    def write_dh(j, total):
        dh[:, at(j, 256)] = total

    project_back(
        k,
        [
            (N.wide_self_query, dq),
            (N.wide_self_key, dkey),
            (N.wide_self_value, dvalue),
            (N.wide_cross_query, k[N.dq_wc]),
        ],
        write_dh,
        D,
    )
    add_norm_back(k, N.norm_branch, size, dh, rows_of(k[N.dx]), k[N.token_grad])


def segment_ids(lengths_rows, token_count):
    ends_at = jnp.cumsum(lengths_rows, axis=-1)
    places = jnp.arange(token_count, dtype=jnp.int32)
    return jnp.sum((places[None, :, None] >= ends_at[:, None, :]).astype(jnp.int32), axis=2)


def spread_segments(segments):
    micro, tokens = segments.shape
    own = segments + tokens * jnp.arange(micro, dtype=jnp.int32)[:, None]
    own = jnp.pad(own.reshape(micro * tokens), (EDGE, EDGE), constant_values=-1)
    return jnp.broadcast_to(own.astype(F32)[:, None], (own.shape[0], LANES))


def caps_of(allowed):
    return jnp.where(allowed, jnp.float32(3e38), jnp.float32(-1e30))


def low_like(size, width, kind=BF):
    return jax.ShapeDtypeStruct((size, width), kind)


def tail_pad(value, rows):
    return jnp.pad(value, ((0, rows - value.shape[0]), (0, 0)))


def local(tokens, lengths, params, cotangent):
    count = lax.axis_size("dp")
    is_first = lax.axis_index("section") == 0
    enc_rows = 2 * -(-ENC.rows // (2 * count))
    dec_rows = 2 * -(-DEC.rows // (2 * count))
    own_rows = params.shape[1]
    own = params[0]
    micro, pack_tokens = tokens.shape[1], tokens.shape[2]
    size = micro * pack_tokens

    holders = slot_devices(GATHER_ORDER, count)
    takers = slot_devices(REDUCE_ORDER, count)
    main_height, tail_height = up_to(own_rows, 16), up_to(own_rows - enc_rows, 16)
    whole, tails = gather_slots(tail_pad(own.astype(BF), main_height), enc_rows, count)

    source_ids = segment_ids(lengths[0, :, 0], pack_tokens)
    target_ids = segment_ids(lengths[1, :, 0], pack_tokens)
    places = jnp.arange(pack_tokens, dtype=jnp.int32)
    early = places[:, None] <= places[None, :]
    mask = spread_segments(jnp.where(is_first, source_ids, target_ids))
    same_source = source_ids[:, :, None] == source_ids[:, None, :]
    same_target = (target_ids[:, :, None] == target_ids[:, None, :]) & early[None]
    caps = caps_of(jnp.where(is_first, same_source, same_target))
    caps_cross = caps_of(source_ids[:, :, None] == target_ids[:, None, :])
    own_tokens = tokens[0].reshape(size, D)
    given = cotangent.reshape(size, D)

    low = low_like(size, D)
    full = low_like(size, D, F32)
    wide = low_like(size, FF)
    rows = low_like(size, LANES, F32)
    edged = ((4 * (size + 2 * EDGE), LANES), F32)
    edged_wide = ((16 * (size + 2 * EDGE), LANES), F32)
    edged_two = ((8 * (size + 2 * EDGE), LANES), F32)
    packs = size // PACK
    probs_16 = low_like(packs * BRANCH_HEADS * PACK, PACK)
    probs_8 = low_like(packs * HEADS * PACK, PACK)
    sums = low_like(VECTOR_ROWS * 8, LANES, F32)

    norm_out = lambda *names: {N.z_ + n: low for n in names} | {N.r_ + n: rows for n in names}
    enc_out = norm_out(N.norm_glu, N.norm_conv, N.norm_attn, N.norm_feed) | dict(
        h1=low, glu_a=low, glu_s=low, h2=low, stacked=low_like(size, 3 * D),
        slope_left=wide, slope_right=low_like(size, 256), z_middle=wide, r_middle=rows,
        spread=wide, h3=low, q=low, key=low, value=low, probs=probs_8, heads=low,
        h4=low, inner=wide, slope_feed=wide, memory=low,
    )
    start_out = norm_out(N.norm_branch) | dict(
        h=low, q_ws=low, k_ws=low, v_ws=low, q_wc=low, p_ws=probs_16, o_ws=low, base=full
    )
    made = dict(
        weights=low_like(WEIGHT_ROWS, LANES), vectors=low_like(VECTOR_ROWS, LANES, F32)
    )

    def encoder_start():
        weights, vectors = lay_out(ENC, [whole], [0], enc_rows, holders)
        result = fused(
            encoder_forward,
            ENC,
            weights,
            list(ENC.weights),
            dict(vectors=vectors, tokens=own_tokens, mask=mask, caps=caps),
            enc_out,
            {},
            dict(
                edged=edged, mixed=edged_wide, x1=((size, D), F32), x2=((size, D), F32),
                x3=((size, D), F32),
            ),
        )
        return result | dict(weights=weights, vectors=vectors)

    enc = lax.cond(is_first, encoder_start, lambda: idle(enc_out | made))
    tails[-1], enc[N.memory] = lax.optimization_barrier((tails[-1], enc[N.memory]))
    ends = share_tails(tails, count)

    def decoder_begin():
        weights, vectors = lay_out(DEC, [whole, ends], [0, own_rows], dec_rows, holders)
        result = fused(
            decoder_start,
            DEC,
            weights,
            [N.wide_self_query, N.wide_self_key, N.wide_self_value, N.wide_cross_query, N.wide_self_output],
            dict(vectors=vectors, tokens=own_tokens, caps=caps),
            start_out,
            {},
            {},
        )
        return result | dict(weights=weights, vectors=vectors)

    dec = lax.cond(~is_first, decoder_begin, lambda: idle(start_out | made))
    memory = lax.ppermute(enc[N.memory], "section", [(0, 1)])

    forward_out = norm_out(N.norm_conv, N.norm_self, N.norm_cross, N.norm_feed) | dict(
        k_wc=low, v_wc=low, p_wc=probs_16, o_wc=low, left_in=low, right_in=low,
        slope_left_d=low_like(size, 2 * D), z_middle_d=low_like(size, 2 * D), r_middle_d=rows,
        out_in=low_like(size, 2 * D), h_s=low, q_s=low, k_s=low, v_s=low, p_s=probs_8, o_s=low,
        h_c=low, q_c=low, k_c=low, v_c=low, p_c=probs_8, o_c=low, h_f=low,
        inner_d=wide, slope_feed_d=wide, output=low,
    )
    early_names = (N.wide_self, N.wide_cross_query)
    later = [n for n in DEC.weights if not n.startswith(early_names)]
    back_out = dict(
        dpre_feed=wide, d4=low, dq_c=low, dk_c=low, dv_c=low, d3=low, dq_s=low, dk_s=low, dv_s=low,
        d2=low, dleft=low_like(size, 2 * D), dright=low_like(size, 256), d1=low, dx=full,
        dq_wc=low, dk_wc=low, dv_wc=low, vector_sums=sums, sent=low,
    )
    back_names = [
        N.feed_out_weight, N.feed_in_weight, N.cross_output, N.cross_query, N.cross_key, N.cross_value,
        N.self_output, N.self_query, N.self_key, N.self_value, N.out_weight, N.left_weight, N.right_weight,
        N.wide_cross_output, N.wide_cross_key, N.wide_cross_value,
    ]
    saved = [
        N.slope_feed, N.z_norm_feed, N.r_norm_feed, N.q_c, N.k_c, N.v_c, N.p_c, N.z_norm_cross,
        N.r_norm_cross, N.q_s, N.k_s, N.v_s, N.p_s, N.z_norm_self, N.r_norm_self, N.z_middle,
        N.r_middle, N.slope_left, N.z_norm_conv, N.r_norm_conv, N.k_wc, N.v_wc, N.p_wc,
    ]

    def decode_forward():
        return fused(
            decoder_forward,
            DEC,
            dec[N.weights],
            later,
            dict(
                vectors=dec[N.vectors], memory=memory, q_wc=dec[N.q_wc], caps_cross=caps_cross,
                base=dec[N.base], mask=mask, caps=caps,
            ),
            strip_names(forward_out),
            {},
            dict(
                edged=edged, mixed=edged_two, y1=((size, D), F32), y2=((size, D), F32),
                y3=((size, D), F32), y4=((size, D), F32),
            ),
        )

    def decode_back():
        return fused(
            decoder_back,
            DEC,
            dec[N.weights],
            back_names,
            dict(vectors=dec[N.vectors], cotangent=given)
            | {n: forward[n] for n in saved}
            | dict(mask=mask, q_wc=dec[N.q_wc]),
            back_out,
            {},
            dict(
                dh=((size, D), F32), dmem=((size, D), F32), dheads=((size, D), BF), dspread=edged_two,
                dmiddle=((size, 2 * D), F32),
            ),
        )

    forward = lax.cond(~is_first, decode_forward, lambda: idle(strip_names(forward_out)))
    back = lax.cond(~is_first, decode_back, lambda: idle(back_out))
    returned = lax.ppermute(back[N.sent], "section", [(1, 0)])
    returned, back[N.d1] = lax.optimization_barrier((returned, back[N.d1]))

    enc_last = dict(
        dpre_feed=wide, d3=low, dq=low, dkey=low, dvalue=low, d2=low_like(size, 256), dleft=wide,
        dright=low_like(size, 256), dglu=low_like(size, 2 * D), token_grad=full, vector_sums=sums,
    )
    dec_last = dict(dq_ws=low, dk_ws=low, dv_ws=low, token_grad=full, vector_sums=sums)
    enc_names = [
        N.feed_out_weight, N.feed_in_weight, N.attn_output, N.attn_query, N.attn_key, N.attn_value,
        N.point_weight, N.right_weight, N.left_weight, N.glu_weight,
    ]
    enc_saved = [
        N.slope_feed, N.z_norm_feed, N.r_norm_feed, N.q, N.key, N.value, N.probs, N.z_norm_attn,
        N.r_norm_attn, N.z_middle, N.r_middle, N.slope_left, N.slope_right, N.z_norm_conv,
        N.r_norm_conv, N.glu_a, N.glu_s, N.z_norm_glu, N.r_norm_glu,
    ]
    enc_products = [
        (N.feed_out_weight, N.inner, N.returned), (N.feed_in_weight, N.h4, N.dpre_feed),
        (N.attn_output, N.heads, N.d3), (N.attn_query, N.h3, N.dq), (N.attn_key, N.h3, N.dkey),
        (N.attn_value, N.h3, N.dvalue), (N.point_weight, N.spread, N.d2),
        (N.right_weight, N.stacked, N.dright), (N.left_weight, N.h2, N.dleft), (N.glu_weight, N.h1, N.dglu),
    ]
    dec_products = [
        (N.feed_out_weight, N.inner, N.cotangent), (N.feed_in_weight, N.h_f, N.dpre_feed),
        (N.cross_output, N.o_c, N.d4), (N.cross_query, N.h_c, N.dq_c), (N.cross_key, N.memory, N.dk_c),
        (N.cross_value, N.memory, N.dv_c), (N.wide_cross_key, N.memory, N.dk_wc),
        (N.wide_cross_value, N.memory, N.dv_wc), (N.self_output, N.o_s, N.d3),
        (N.self_query, N.h_s, N.dq_s), (N.self_key, N.h_s, N.dk_s), (N.self_value, N.h_s, N.dv_s),
        (N.out_weight, N.out_in, N.d2), (N.left_weight, N.left_in, N.dleft),
        (N.right_weight, N.right_in, N.dright), (N.wide_cross_output, N.o_wc, N.d1),
        (N.wide_self_output, N.o_ws, N.d1), (N.wide_self_query, N.h, N.dq_ws), (N.wide_self_key, N.h, N.dk_ws),
        (N.wide_self_value, N.h, N.dv_ws), (N.wide_cross_query, N.h, N.dq_wc),
    ]

    def only(arrays, products):
        return {n: arrays[n] for p in products for n in p[1:]}

    if by_neighbours(count):
        main_shapes = [low_like(main_height, LANES)] * 16
        tail_shapes = [jax.ShapeDtypeStruct((8, tail_height, LANES), BF)] * 2
        main_targets = [(n, None) for n in range(16)]
        tail_targets = [(16 + o, n) for n in range(8) for o in range(2)]
    else:
        main_shapes = [jax.ShapeDtypeStruct((count, main_height, LANES), BF)]
        tail_shapes = [jax.ShapeDtypeStruct((count, tail_height, LANES), BF)]
        main_targets = [(0, j) for j in range(count)]
        tail_targets = [(1, j) for j in range(count)]

    def decoder_last():
        last = fused(
            branch_back,
            DEC,
            dec[N.weights],
            [
                N.wide_self_output, N.wide_self_query, N.wide_self_key, N.wide_self_value,
                N.wide_cross_query,
            ],
            dict(vectors=dec[N.vectors], d1=back[N.d1])
            | {n: dec[n] for n in (N.q_ws, N.k_ws, N.v_ws, N.p_ws)}
            | {n: dec[n] for n in (N.z_norm_branch, N.r_norm_branch)}
            | dict(dq_wc=back[N.dq_wc], dx=back[N.dx]),
            dec_last,
            {},
            dict(dheads=((size, D), BF), dh=((size, D), F32)),
        )
        arrays = dec | forward | back | last | dict(cotangent=given, memory=memory)
        grads = weight_gradients(
            DEC, dec_products, only(arrays, dec_products), [back[N.vector_sums], last[N.vector_sums]],
            main_shapes + tail_shapes, [main_targets, tail_targets], [0, own_rows], dec_rows, takers,
        )
        return last[N.token_grad], grads

    def encoder_last():
        last = fused(
            encoder_back,
            ENC,
            enc[N.weights],
            enc_names,
            dict(vectors=enc[N.vectors], returned=returned)
            | {n: enc[n] for n in enc_saved}
            | dict(mask=mask),
            enc_last,
            {},
            dict(
                dh=((size, D), F32), dx=((size, D), F32), dheads=((size, D), BF), dspread=edged_wide,
                dmiddle=((size, FF), F32),
            ),
        )
        return last

    def nothing(shapes):
        names = dict(enumerate(shapes))
        return tuple(idle(names).values())

    source_back = lax.cond(is_first, encoder_last, lambda: idle(enc_last))
    target_grad, dec_grads = lax.cond(
        ~is_first,
        decoder_last,
        lambda: (idle(dict(grad=full))[N.grad], nothing(main_shapes + tail_shapes)),
    )
    tails = hand_over_tails(dec_grads[len(main_shapes) :], count)
    enc_arrays = only(enc | source_back | dict(returned=returned), enc_products)
    grads = lax.cond(
        is_first,
        lambda: weight_gradients(
            ENC, enc_products, enc_arrays, [source_back[N.vector_sums]], main_shapes, [main_targets], [0],
            enc_rows, takers,
        ),
        lambda: dec_grads[: len(main_shapes)],
    )
    parts, tail = reduce_slots(grads, tails, enc_rows, count)
    param_out = add_up(parts, tail, enc_rows, own_rows).reshape(1, own_rows, LANES)
    token_grads = jnp.where(is_first, source_back[N.token_grad], target_grad)
    shape = (1, micro, pack_tokens, D)
    results = jnp.where(is_first, returned, forward[N.output])
    return (results.reshape(shape), token_grads.reshape(shape), param_out)


def strip_names(outs):
    return {n[:-2] if n.endswith(N._d) else n: v for n, v in outs.items()}


def idle(outs):
    names = list(outs)

    def kernel(*refs):
        return None

    any_spec = pl.BlockSpec(memory_space=pl.ANY)
    result = pl.pallas_call(
        kernel,
        out_shape=[outs[n] for n in names],
        out_specs=[any_spec] * len(names),
    )()
    return dict(zip(names, result))


def solution(mesh):
    return jax.shard_map(
        local,
        mesh=mesh,
        in_specs=(
            P("section", None, "dp", None),
            P(None, None, "dp", None),
            P("section", "dp", None),
            P(None, "dp", None),
        ),
        out_specs=(
            P("section", None, "dp", None),
            P("section", None, "dp", None),
            P("section", "dp", None),
        ),
        check_vma=False,
    )
```

```python
import math

import jax
import jax.numpy as jnp
from jax import lax
from jax.experimental import pallas as pl
from jax.experimental.pallas import tpu as pltpu
from jax.sharding import PartitionSpec as P


class Names:
    def __getattr__(self, name):
        return name


N = Names()
D = 512
FF = 2048
HEADS = 8
BRANCH_HEADS = 16
LANES = 128
PACK = 256
EDGE = 16

epsilon = 1e-06
blocked = -1000000000.0
BF = jnp.bfloat16
F32 = jnp.float32


def attention_entries(prefix):
    return [(prefix + part, (D, D)) for part in (N._query, N._key, N._value, N._output)]


def norm_entries(prefix, width_of):
    return [(prefix + N._gain, (width_of,)), (prefix + N._bias, (width_of,))]


def encoder_layout():
    half_width = D // 2
    return (
        norm_entries(N.norm_glu, D)
        + [(N.glu_weight, (D, 2 * D)), (N.glu_bias, (2 * D,))]
        + norm_entries(N.norm_conv, D)
        + [
            (N.left_weight, (D, FF)),
            (N.left_bias, (FF,)),
            (N.right_weight, (3 * D, half_width)),
            (N.right_bias, (half_width,)),
        ]
        + norm_entries(N.middle, FF)
        + [
            (N.depth_taps, (9, FF)),
            (N.point_weight, (FF, half_width)),
            (N.point_bias, (half_width,)),
        ]
        + norm_entries(N.norm_attn, D)
        + attention_entries(N.attn)
        + norm_entries(N.norm_feed, D)
        + [
            (N.feed_in_weight, (D, FF)),
            (N.feed_in_bias, (FF,)),
            (N.feed_out_weight, (FF, D)),
            (N.feed_out_bias, (D,)),
        ]
    )


def decoder_layout():
    half_width = D // 2
    return (
        norm_entries(N.norm_branch, D)
        + attention_entries(N.wide_self)
        + attention_entries(N.wide_cross)
        + norm_entries(N.norm_conv, D)
        + [
            (N.left_taps, (11, D)),
            (N.left_weight, (D, 2 * D)),
            (N.left_bias, (2 * D,)),
            (N.right_taps, (7, D)),
            (N.right_weight, (D, half_width)),
            (N.right_bias, (half_width,)),
        ]
        + norm_entries(N.middle, 2 * D)
        + [
            (N.out_taps, (7, 2 * D)),
            (N.out_weight, (2 * D, D)),
            (N.out_bias, (D,)),
        ]
        + norm_entries(N.norm_self, D)
        + attention_entries(N.self)
        + norm_entries(N.norm_cross, D)
        + attention_entries(N.cross)
        + norm_entries(N.norm_feed, D)
        + [
            (N.feed_in_weight, (D, FF)),
            (N.feed_in_bias, (FF,)),
            (N.feed_out_weight, (FF, D)),
            (N.feed_out_bias, (D,)),
        ]
    )


class Table:
    def __init__(self, entries):
        self.at, self.weights, self.vectors, self.heights = {}, {}, {}, {}
        offset = weight_rows = vector_rows = 0
        for name, shape in entries:
            rows = math.prod(shape) // LANES
            self.at[name] = offset
            self.heights[name] = rows
            if len(shape) == 2 and shape[0] >= D:
                self.weights[name] = (weight_rows, shape[0], shape[1] // LANES)
                weight_rows += rows
            else:
                self.vectors[name] = (vector_rows, rows)
                vector_rows += rows
            offset += rows
        self.rows, self.weight_rows, self.vector_rows = offset, weight_rows, vector_rows


ENC = Table(encoder_layout())
DEC = Table(decoder_layout())
WEIGHT_ROWS = max(ENC.weight_rows, DEC.weight_rows)
VECTOR_ROWS = -(-max(ENC.vector_rows, DEC.vector_rows) // 16) * 16


def up_to(value, step):
    return -(-value // step) * step


AXES = ("section", "dp")


def pairs(count, move, sections):
    return [
        (s * count + i, s * count + j)
        for s in sections
        for i in range(count)
        for j in [move(i)]
        if j is not None
    ]


def swap(value, bit, count, sections):
    return lax.ppermute(value, AXES, pairs(count, lambda i: i ^ bit, sections))


def shift(value, step, count, sections, senders):
    def move(i):
        return i + 4 * step if i // 4 in senders and 0 <= i + 4 * step < count else None

    return lax.ppermute(value, AXES, pairs(count, move, sections))


def pick(z, options):
    out = options[0]
    for k in range(1, len(options)):
        if options[k] is not options[k - 1]:
            out = jnp.where(z >= k, options[k], out)
    return out


def by_neighbours(count):
    return count == 16


REDUCE_ORDER = [[3, 2, 1, 0], [3, 2, 0, 1], [0, 1, 3, 2], [0, 1, 2, 3]]
GATHER_ORDER = [[0, 1, 2, 3], [1, 0, 2, 3], [2, 1, 3, 0], [3, 2, 1, 0]]


def slot_devices(order, count):
    if not by_neighbours(count):
        return jnp.arange(count, dtype=jnp.int32)
    me = lax.axis_index("dp")
    z, y, c = me // 4, (me // 2) % 2, me % 2
    return jnp.stack(
        [
            pick(z, [own[k] for own in order]) * 4 + yy * 2 + cc
            for k in range(4)
            for yy in (y, 1 - y)
            for cc in (c, 1 - c)
        ]
    ).astype(jnp.int32)


def gather_slots(own, start, count):
    if not by_neighbours(count):
        held = lax.all_gather(own, "dp", axis=0)
        tails = lax.ppermute(held[:, start:], "section", [(0, 1)])
        tails = jnp.pad(tails, ((0, 0), (0, -tails.shape[1] % 16), (0, 0)))
        return [(held, j) for j in range(count)], [tails]
    z = lax.axis_index("dp") // 4
    both = (0, 1)
    near, far, near_other, far_other = [own], [], [], []
    up = down = own
    held = []
    ends = []

    def cross(steps):
        tails = jnp.stack([slot[start:] for k in steps for slot in (near[k], far[k])])
        ends.append(lax.ppermute(tails, "section", [(0, 1)]))

    for step in range(4):
        swapped = swap(near[step], 2, count, both)
        ups, downs = up, down
        if step == 3:
            cross((0, 1, 2))
        if step < 3:
            up = shift(ups, 1, count, both, [(0, 1, 2), (1, 2), (2,)][step])
            down = shift(downs, -1, count, both, [(3, 2, 1), (1, 2), (1,)][step])
        near_other.append(swap(near[step], 1, count, both))
        if step:
            far_other.append(swap(far[step - 1], 1, count, both))
        swapped, up, down, near_other, far_other = lax.optimization_barrier(
            (swapped, up, down, near_other, far_other)
        )
        far.append(swapped)
        held.append((up, down))
        if step == 0:
            near.append(pick(z, [down, up, up, up]))
        if step == 1:
            first_down = held[0][1]
            near.append(pick(z, [down, first_down, first_down, up]))
        if step == 2:
            near.append(pick(z, [down, held[1][1], held[1][0], up]))
    far_other.append(swap(far[3], 1, count, both))
    cross((3,))
    whole = [
        (slot, None) for k in range(4) for slot in (near[k], near_other[k], far[k], far_other[k])
    ]
    return whole, ends


def share_tails(tails, count):
    if not by_neighbours(count):
        return [(tails[0], j) for j in range(count)]
    others = [swap(part, 1, count, (1,)) for part in tails]
    return [
        (held[part], n) for part in range(2) for n in range((6, 2)[part]) for held in (tails, others)
    ]


def hand_over_tails(tails, count):
    if not by_neighbours(count):
        tail = lax.psum_scatter(tails[0], "dp", scatter_dimension=0, tiled=False)
        return lax.ppermute(tail, "section", [(1, 0)])
    same, other = tails
    mine = same.astype(F32) + swap(other, 1, count, (1,)).astype(F32)
    return lax.ppermute(mine.astype(BF), "section", [(1, 0)])


def reduce_slots(slots, tails, start, count):
    if not by_neighbours(count):
        return [lax.psum_scatter(slots[0], "dp", scatter_dimension=0, tiled=False)], tails
    z = lax.axis_index("dp") // 4
    both = (0, 1)
    low = BF

    def add(*terms):
        return sum([term.astype(F32) for term in terms])

    def with_tail(total, n):
        return total + jnp.pad(tails[n].astype(F32), ((start, 0), (0, 0)))

    def crossed(k):
        return [swap(slots[4 * k + 2 * f + 1], 1, count, both) for f in (1, 0)]

    def leaving(k):
        return with_tail(add(slots[4 * k + 2], others[k][0]), 2 * k + 1).astype(low)

    def arrived(k):
        return with_tail(add(*joined[k]), 2 * k)

    others = [crossed(0), crossed(1)]
    out = leaving(0)
    joined = []
    up = down = None
    for k in range(4):
        got = swap(out, 2, count, both)
        sent_up = sent_down = None
        if k:
            sent_up = shift(up, 1, count, both, range(k))
            sent_down = shift(down, -1, count, both, range(4 - k, 4))
        if k < 3:
            out = leaving(k + 1)
        if k < 2:
            others.append(crossed(k + 2))
        got, sent_up, sent_down, out, others = lax.optimization_barrier(
            (got, sent_up, sent_down, out, others)
        )
        joined.append([slots[4 * k], others[k][1], got])
        if k == 0:
            up = down = arrived(0).astype(low)
        if k in (1, 2):
            up_from = [[k, k - 1, k - 1, k - 1], [2, 1, 2, 2]][k - 1]
            down_from = [[k - 1, k - 1, k - 1, k], [2, 2, 1, 2]][k - 1]
            totals = [arrived(n) for n in range(k + 1)]
            up = (pick(z, [totals[n] for n in up_from]) + sent_up.astype(F32)).astype(low)
            down = (pick(z, [totals[n] for n in down_from]) + sent_down.astype(F32)).astype(low)
    return joined[3] + [sent_up, sent_down], tails[6]


def loop(count, body, together=1):
    together = math.gcd(count, together)

    def step(i, carry):
        for part in range(together):
            body(i * together + part)
        return carry

    lax.fori_loop(0, count // together, step, 0)


def at(i, size):
    if isinstance(i, int):
        return pl.ds(i * size, size)
    return pl.ds(pl.multiple_of(i * size, size), size)


def block_at(start, size):
    if isinstance(start, int):
        return pl.ds(start, size)
    return pl.ds(pl.multiple_of(start, 256), size)


WINDOW = 12 * 2**20


class Queue:
    def __init__(self, copies, sizes, order):
        self.copies, self.sizes, self.waiting = dict(copies), sizes, list(order)
        self.running, self.asked = [], []
        self.fill()

    def fill(self):
        while self.waiting:
            ahead = sum([self.sizes[name] for name in self.running])
            if self.running and ahead + self.sizes[self.waiting[0]] > WINDOW:
                return
            name = self.waiting.pop(0)
            self.copies[name].start()
            self.running.append(name)

    def get(self, name):
        if name not in self.copies:
            return
        self.asked.append(name)
        if name in self.waiting:
            self.waiting.remove(name)
            self.copies[name].start()
        else:
            self.running.remove(name)
        self.copies.pop(name).wait()
        self.fill()


class Kernel:
    def __init__(self, table, weight_ref, queue, refs, outgoing):
        self.table, self.w, self.queue, self.refs = table, weight_ref, queue, refs
        self.outgoing, self.sent = outgoing, []

    def __getitem__(self, name):
        self.queue.get(name)
        return self.refs[name]

    def need(self, name):
        self.queue.get(name)

    def put(self, *names):
        for name in names:
            copy = self.outgoing.pop(name)
            copy.start()
            self.sent.append(copy)

    def columns(self, name, first, blocks):
        self.need(name)
        offset, height, unused = self.table.weights[name]
        parts = [
            self.w[block_at(offset + (first + i) * height, height), :]
            for i in range(blocks)
        ]
        return jnp.concatenate(parts, axis=1)

    def strip(self, name, first, rows, low=0):
        self.need(name)
        offset, height, blocks = self.table.weights[name]
        parts = [
            self.w[block_at(offset + j * height + low + first * rows, rows), :]
            for j in range(blocks)
        ]
        return jnp.concatenate(parts, axis=1)

    def row(self, name, j, blocks=1):
        offset, unused = self.table.vectors[name]
        parts = [self.refs[N.vectors][pl.ds(offset + j + i, 1), :] for i in range(blocks)]
        return parts[0] if blocks == 1 else jnp.concatenate(parts, axis=1)

    def add_rows(self, name, j, value):
        offset, unused = self.table.vectors[name]
        blocks = value.shape[1] // LANES
        for i in range(blocks):
            part = value[:, i * LANES : (i + 1) * LANES]
            part = part.reshape(part.shape[0] // 8, 8, LANES).sum(axis=0)
            place = at(offset + j + i, 8)
            self.refs[N.vector_sums][place, :] += part


def fused(body, table, weight_array, weight_names, ins, outs, blanks, temps):
    in_names, out_names, blank_names = list(ins), list(outs), list(blanks)
    temp_names = list(temps)
    copies_in = in_names + list(weight_names)
    total = len(copies_in) + len(out_names)
    sizes = {n: math.prod(ins[n].shape) * ins[n].dtype.itemsize for n in in_names}
    sizes |= {n: table.heights[n] * LANES * 2 for n in weight_names}

    def call(order, asked):
        def kernel(*refs):
            refs = list(refs)
            weight_hbm = refs.pop(0)
            in_hbm = {n: refs.pop(0) for n in in_names}
            out_hbm = {n: refs.pop(0) for n in out_names}
            for unused in blank_names:
                refs.pop(0)
            weight_vmem = refs.pop(0)
            vmem = {n: refs.pop(0) for n in in_names + out_names + temp_names}
            sems = refs.pop(0)
            copies = {}
            for at_sem, name in enumerate(copies_in):
                if name in table.weights:
                    offset, height, blocks = table.weights[name]
                    place = pl.ds(offset, height * blocks)
                    pair = (weight_hbm.at[place], weight_vmem.at[place])
                else:
                    pair = (in_hbm[name], vmem[name])
                copies[name] = pltpu.make_async_copy(pair[0], pair[1], sems.at[at_sem])
            outgoing = {
                name: pltpu.make_async_copy(vmem[name], out_hbm[name], sems.at[len(copies_in) + i])
                for i, name in enumerate(out_names)
            }
            queue = Queue(copies, sizes, order)
            k = Kernel(table, weight_vmem, queue, vmem, outgoing)
            body(k)
            for name in copies_in:
                queue.get(name)
            for name in list(outgoing):
                k.put(name)
            for copy in k.sent:
                copy.wait()
            asked[:] = queue.asked

        any_spec = pl.BlockSpec(memory_space=pl.ANY)
        return pl.pallas_call(
            kernel,
            out_shape=[outs[n] for n in out_names] + [blanks[n] for n in blank_names],
            in_specs=[any_spec] * (1 + len(in_names)),
            out_specs=[any_spec] * (len(out_names) + len(blank_names)),
            scratch_shapes=[pltpu.VMEM((weight_rows_used(table, weight_names), LANES), BF)]
            + [pltpu.VMEM(ins[n].shape, ins[n].dtype) for n in in_names]
            + [pltpu.VMEM(outs[n].shape, outs[n].dtype) for n in out_names]
            + [pltpu.VMEM(*temps[n]) for n in temp_names]
            + [pltpu.SemaphoreType.DMA((total,))],
            compiler_params=pltpu.CompilerParams(vmem_limit_bytes=62 * 2**20),
        )

    given = [weight_array] + [ins[n] for n in in_names]
    asked = []
    jax.eval_shape(call(copies_in, asked), *given)
    result = call(list(asked), [])(*given)
    return dict(zip(out_names + blank_names, result))


def weight_rows_used(table, names):
    return max(table.weights[n][0] + table.heights[n] for n in names)


def dot(left, right):
    return jnp.dot(left, right, preferred_element_type=F32)


def dot_t(left, right):
    return lax.dot_general(left, right, (((1,), (1,)), ((), ())), preferred_element_type=F32)


def blocks_of(width):
    return range(width // LANES)


def lanes(j):
    return slice(j * LANES, (j + 1) * LANES)


def normalize(k, read, norm, width, size, block, write):
    def body(i):
        rows = at(i, block)
        values = [read(rows, j) for j in blocks_of(width)]
        mean = jnp.sum(sum(values), axis=1, keepdims=True) * (1.0 / width)
        values = [v - mean for v in values]
        var = jnp.sum(sum([v * v for v in values]), axis=1, keepdims=True) * (1.0 / width)
        r = lax.rsqrt(var + epsilon)
        for j in blocks_of(width):
            z = values[j] * r
            write(rows, j, z, z * k.row(norm + N._gain, j) + k.row(norm + N._bias, j), r)

    loop(size // block, body, 4)


def norm_gradient(k, norm, width, zs, douts, r):
    dzs = []
    for j in blocks_of(width):
        k.add_rows(norm + N._gain, j, douts[j] * zs[j])
        k.add_rows(norm + N._bias, j, douts[j])
        dzs.append(douts[j] * k.row(norm + N._gain, j))
    first = jnp.sum(sum(dzs), axis=1, keepdims=True) * (1.0 / width)
    second = jnp.sum(sum([a * b for a, b in zip(dzs, zs)]), axis=1, keepdims=True) * (1.0 / width)
    return [(dz - first - z * second) * r for dz, z in zip(dzs, zs)]


GELU_A = math.sqrt(2.0 / math.pi)
GELU_B = GELU_A * 0.044715


def gelu_both(x):
    square = x * x
    half = 0.5 + 0.5 * jnp.tanh(x * (GELU_A + GELU_B * square))
    value = x * half
    slope = half + 2.0 * value * (1.0 - half) * (GELU_A + 3.0 * GELU_B * square)
    return value, slope


def sigmoid(x):
    return 0.5 + 0.5 * jnp.tanh(0.5 * x)


def silu_both(x):
    s = sigmoid(x)
    value = x * s
    return value, s + value * (1.0 - s)


def head_mask(h, size):
    lane = lax.broadcasted_iota(jnp.int32, (1, LANES), 1)
    return ((lane >= h * size) & (lane < (h + 1) * size)).astype(BF)


class Group:
    def __init__(self, index, **refs):
        groups = D // LANES
        pack, column = index // groups, lax.rem(index, groups)
        self.index, self.pack = index, pack
        self.rows, self.cols = at(pack, PACK), at(column, LANES)
        for name, ref in refs.items():
            setattr(self, name, ref[self.rows, self.cols])


def in_turn(count, stages):
    for k in range(count + max(delay for unused, delay in stages)):
        for stage, delay in stages:
            if 0 <= k - delay < count:
                stage(k - delay)


def attend(q, key, value, caps, probs, out, heads, tokens):
    size = D // heads
    per = LANES // size
    scale = size ** (-0.5) * math.log2(math.e)
    together = 4
    halves = [slice(0, LANES), slice(LANES, PACK)]

    def body(step):
        groups, scores, weights, parts = {}, {}, {}, {}

        def score(i):
            g, h = divmod(i, per)
            if h == 0:
                groups[g] = Group(step * together + g, q=q, key=key, value=value)
                groups[g].value = groups[g].value.T
                parts[g] = []
            masked = groups[g].key * head_mask(h, size)
            scores[i] = [dot_t(masked, groups[g].q[half]) for half in halves]

        def soften(i):
            g, h = divmod(i, per)
            done = []
            for half, s in zip(halves, scores.pop(i)):
                s = jnp.minimum(s * scale, caps[groups[g].pack, :, half])
                e = jnp.exp2(s - jnp.max(s, axis=0, keepdims=True))
                done.append((e * (1.0 / jnp.sum(e, axis=0, keepdims=True))).astype(BF))
            weights[i] = jnp.concatenate(done, axis=1)
            probs[at(groups[g].index * per + h, PACK), :] = weights[i]

        def collect(i):
            g, h = divmod(i, per)
            group = groups[g]
            parts[g].append(dot(group.value[h * size : (h + 1) * size], weights.pop(i)))
            if h == per - 1:
                out[group.rows, group.cols] = jnp.concatenate(parts[g], axis=0).T.astype(BF)

        in_turn(together * per, [(score, 0), (soften, 2), (collect, 3)])

    loop((tokens // PACK) * (D // LANES) // together, body)


def attend_back(q, key, value, probs, dout, dq, dkey, dvalue, heads, tokens, together=4):
    size = D // heads
    per = LANES // size
    scale = size ** (-0.5)
    masks = [head_mask(h, size) for h in range(per)]

    def body(step):
        groups, grads, weights, moved, parts = {}, {}, {}, {}, {}

        def first(i):
            g, h = divmod(i, per)
            if h == 0:
                groups[g] = Group(
                    step * together + g, q=q, key=key, value=value, dout=dout
                )
                groups[g].key = groups[g].key.T
                weights[g], moved[g], parts[g] = [], [], []
            grads[i] = dot_t(groups[g].value * masks[h], groups[g].dout)

        def soften(i):
            g, h = divmod(i, per)
            dp = grads.pop(i)
            low = probs[at(groups[g].index * per + h, PACK), :]
            wide = low.astype(F32)
            mean = jnp.sum(wide * dp, axis=0, keepdims=True)
            mean = mean / jnp.sum(wide, axis=0, keepdims=True)
            weights[g].append(low)
            moved[g].append((wide * (dp - mean)).astype(BF))

        def collect(i):
            g, h = divmod(i, per)
            group = groups[g]
            parts[g].append(dot(group.key[h * size : (h + 1) * size], moved[g][h]))
            if h == per - 1:
                douts = jnp.concatenate([group.dout * mask for mask in masks], axis=0)
                queries = jnp.concatenate([group.q * mask for mask in masks], axis=0)
                place = (group.rows, group.cols)
                dvalue[place] = dot(jnp.concatenate(weights[g], axis=1), douts).astype(BF)
                dkey[place] = (dot(jnp.concatenate(moved[g], axis=1), queries) * scale).astype(BF)
                dq[place] = (jnp.concatenate(parts[g], axis=0).T * scale).astype(BF)

        in_turn(together * per, [(first, 0), (soften, 2), (collect, 3)])

    loop((tokens // PACK) * (D // LANES) // together, body)


def chunks(count, product, finish):
    held = {}

    def ask(j):
        held[j] = product(j)

    in_turn(count, [(ask, 0), (lambda j: finish(j, held.pop(j)), 1)])


def project(k, name, x, out):
    def finish(j, total):
        out[:, at(j, 256)] = total.astype(BF)

    chunks(out.shape[1] // 256, lambda j: dot(x[...], k.columns(name, 2 * j, 2)), finish)


def project_back(k, terms, write, height, low=0):
    def product(j):
        return sum([dot_t(dout[...], k.strip(name, j, 256, low)) for name, dout in terms])

    chunks(height // 256, product, write)


def same_segment(segments, base, block, moves):
    here = segments[pl.ds(base + EDGE, block), :]
    return {
        move: jnp.where(segments[pl.ds(base + (EDGE + move), block), :] == here, 1.0, 0.0)
        for move in moves
        if move
    }


def masked(ref, base, block, j, move, held):
    value = ref.load(base + move, block, j)
    return value * held[move] if move else value


def taps_forward(k, name, moves, source, segments, out, width, size):
    block = 16

    def body(i):
        base = pl.multiple_of(i * block, block)
        held = same_segment(segments, base, block, moves)
        for j in blocks_of(width):
            total = jnp.zeros((block, LANES), F32)
            for tap, move in enumerate(moves):
                value = masked(source, base, block, j, move, held)
                total = total + value * k.row(name, tap * (width // LANES) + j)
            out[pl.ds(base, block), lanes(j)] = total.astype(out.dtype)

    loop(size // block, body, 2)


def taps_back(k, terms, center, segments, width, size, write):
    block = 32

    def body(i):
        base = pl.multiple_of(i * block, block)
        rows = pl.ds(base, block)
        held = same_segment(
            segments, base, block, sorted({-move for term in terms for move in term[1]})
        )
        for j in blocks_of(width):
            total = jnp.zeros((block, LANES), F32)
            here = center(rows, j)
            for name, moves, dout in terms:
                for tap, move in enumerate(moves):
                    entry = tap * (width // LANES) + j
                    value = masked(dout, base, block, j, -move, held)
                    total = total + value * k.row(name, entry)
                    k.add_rows(name, entry, value * here)
            write(rows, j, total)

    loop(size // block, body)


class Edged:
    def __init__(self, ref, size):
        self.ref, self.size, self.height = ref, size, size + 2 * EDGE
        for j in range(ref.shape[0] // self.height):
            for start in (0, size + EDGE):
                ref[pl.ds(j * self.height + start, EDGE), :] = jnp.zeros((EDGE, LANES), F32)

    def part(self, first, blocks):
        place = pl.ds(first * self.height, blocks * self.height)
        return Edged(self.ref.at[place], self.size)

    def place(self, start, rows, j):
        return pl.ds(start + (j * self.height + EDGE), rows)

    def load(self, start, rows, j):
        return self.ref[self.place(start, rows, j), :]

    def store(self, start, rows, j, value):
        self.ref[self.place(start, rows, j), :] = value

    def store_wide(self, j, value, add=False):
        for half in range(2):
            place = pl.ds((2 * j + half) * self.height + EDGE, self.size)
            if add:
                self.ref[place, :] += value[:, lanes(half)]
            else:
                self.ref[place, :] = value[:, lanes(half)]


def moves_of(count, first):
    return [first + i for i in range(count)]


def lay_out(table, sources, starts, piece_rows, devices):
    slots = 8
    count = devices.shape[0]
    heights = [end - start for start, end in zip(starts, starts[1:] + [piece_rows])]
    arrays = []
    for items in sources:
        for array, unused in items:
            if not any(array is other for other in arrays):
                arrays.append(array)

    def spot(array):
        return [array is other for other in arrays].index(True)

    pieces = [
        (a, j, spot(items[j][0]), items[j][1])
        for j in range(count)
        for a, items in enumerate(sources)
    ]

    def kernel(*refs):
        refs = list(refs)
        device = refs.pop(0)
        held = [refs.pop(0) for unused in arrays]
        weight_hbm, vector_hbm, ring, stream, stage, vector_stage, in_sems, out_sems = refs

        def fetch(step):
            a, unused, which, lead = pieces[step]
            rows = pl.ds(0, up_to(heights[a], 16))
            source = held[which] if lead is None else held[which].at[lead]
            place = ring.at[step % slots, rows]
            return pltpu.make_async_copy(source.at[rows], place, in_sems.at[step % slots])

        for step in range(min(slots, len(pieces))):
            fetch(step).start()
        for step, (a, j, unused, unused_too) in enumerate(pieces):
            fetch(step).wait()
            base = device[j] * piece_rows + starts[a]
            whole, rest = heights[a] // 256, heights[a] % 256

            def body(i, base=base, step=step):
                stream[pl.ds(base + i * 256, 256), :] = ring[step % slots, at(i, 256), :].astype(F32)

            if whole:
                loop(whole, body)
            if rest:
                padded = up_to(rest, 16)
                value = ring[step % slots, whole * 256 : whole * 256 + padded, :].astype(F32)
                stream[pl.ds(base + whole * 256, rest), :] = value[:rest]
            if step + slots < len(pieces):
                fetch(step + slots).start()
        copies = []
        for at_sem, (name, (offset, height, blocks)) in enumerate(table.weights.items()):
            start = table.at[name]
            per = height // 512

            def body(i, offset=offset, height=height, blocks=blocks, start=start, per=per):
                j, part = i // per, lax.rem(i, per)
                taken = stream[pl.ds(start + part * (512 * blocks) + j, 512, stride=blocks), :]
                stage[block_at(offset + j * height + part * 512, 512), :] = taken.astype(BF)

            loop(blocks * per, body, 4)
            place = pl.ds(offset, height * blocks)
            copies.append(
                pltpu.make_async_copy(stage.at[place], weight_hbm.at[place], out_sems.at[at_sem])
            )
            copies[-1].start()
        for name, (offset, rows) in table.vectors.items():
            vector_stage[offset : offset + rows, :] = stream[pl.ds(table.at[name], rows), :]
        copies.append(
            pltpu.make_async_copy(vector_stage, vector_hbm, out_sems.at[len(table.weights)])
        )
        copies[-1].start()
        for copy in copies:
            copy.wait()

    any_spec = pl.BlockSpec(memory_space=pl.ANY)
    return tuple(
        pl.pallas_call(
            kernel,
            out_shape=[
                jax.ShapeDtypeStruct((WEIGHT_ROWS, LANES), BF),
                jax.ShapeDtypeStruct((VECTOR_ROWS, LANES), F32),
            ],
            in_specs=[pl.BlockSpec(memory_space=pltpu.SMEM)] + [any_spec] * len(arrays),
            out_specs=[any_spec] * 2,
            scratch_shapes=[
                pltpu.VMEM((slots, up_to(max(heights), 16), LANES), BF),
                pltpu.VMEM((up_to(count * piece_rows, 8) + 64, LANES), F32),
                pltpu.VMEM((WEIGHT_ROWS, LANES), BF),
                pltpu.VMEM((VECTOR_ROWS, LANES), F32),
                pltpu.SemaphoreType.DMA((slots,)),
                pltpu.SemaphoreType.DMA((len(table.weights) + 1,)),
            ],
            compiler_params=pltpu.CompilerParams(vmem_limit_bytes=62 * 2**20),
        )(devices, *arrays)
    )


def weight_gradients(table, products, arrays, sums, shapes, targets, starts, piece_rows, devices, compact, into=(), active=None):
    count = devices.shape[0]
    heights = [end - start for start, end in zip(starts, starts[1:] + [piece_rows])]
    widths = [shapes[items[0][0]].shape[-2] for items in targets]
    names = list(arrays)
    slots = 4
    size = next(iter(arrays.values())).shape[0]
    widest = max(arrays[x].shape[1] for unused, x, unused_too in products)

    def kernel(*refs):
        if active is None:
            return inside(*refs)

        @pl.when(refs[1][0] == 1)
        def run():
            inside(refs[0], *refs[2:])

    def inside(*refs):
        refs = list(refs)
        device = refs.pop(0)
        hbm = [refs.pop(0) for unused in names + sums]
        for unused in into:
            refs.pop(0)
        out_hbm = [refs.pop(0) for unused in shapes]
        vmem = [refs.pop(0) for unused in names + sums]
        turned, stream, ring, in_sems, out_sems = refs
        wanted = []
        for unused, x, dout in products:
            wanted += [x, dout]
        wanted = list(dict.fromkeys(wanted)) + list(range(len(sums)))
        spot = {n: i for i, n in enumerate(names)} | {i: len(names) + i for i in range(len(sums))}
        copies = {
            n: pltpu.make_async_copy(hbm[spot[n]], vmem[spot[n]], in_sems.at[spot[n]]) for n in wanted
        }
        sizes = {n: math.prod(given[spot[n]].shape) * given[spot[n]].dtype.itemsize for n in wanted}
        queue = Queue(copies, sizes, wanted)

        def get(name):
            queue.get(name)
            return vmem[spot[name]]

        last = None
        for name, x_name, dout_name in products:
            unused, height, blocks = table.weights[name]
            start = table.at[name]
            x, dout = get(x_name), get(dout_name)
            if x_name != last:
                last = x_name

                def turn(j, x=x):
                    turned[at(j, 256), :] = x[:, at(j, 256)].T

                loop(height // 256, turn, 2)
            per = height // 512

            def product(i):
                j, part = i // per, i % per
                return dot(turned[at(part, 512), :], dout[:, at(j, 256)])

            def finish(i, total):
                j, part = i // per, i % per
                base = start + part * (512 * blocks) + 2 * j
                for half in range(2):
                    stream[pl.ds(base + half, 512, stride=blocks), :] = total[:, lanes(half)]

            steps = (blocks // 2) * per
            if compact and steps > 2 and steps % 2 == 0:
                pair = lambda i: chunks(2, lambda n: product(2 * i + n), lambda n, t: finish(2 * i + n, t))
                loop(steps // 2, pair)
            else:
                chunks(steps, product, finish)
        parts = [get(i) for i in range(len(sums))]
        for name, (offset, rows) in table.vectors.items():
            total = None
            for part in parts:
                for s in range(8):
                    value = part[pl.ds(offset * 8 + s, rows, stride=8), :]
                    total = value if total is None else total + value
            stream[pl.ds(table.at[name], rows), :] = total
        if table.rows < count * piece_rows:
            stream[pl.ds(table.rows, count * piece_rows - table.rows), :] = jnp.zeros(
                (count * piece_rows - table.rows, LANES), F32
            )
        sent = []
        if len(starts) == 1:
            gap = up_to(heights[0], 16)
            for slot in range(slots):
                ring[slot, gap : widths[0], :] = jnp.zeros((widths[0] - gap, LANES), BF)
        pieces = [(a, j) for j in range(count) for a in range(len(starts))]
        for step, (a, j) in enumerate(pieces):
            slot = step % slots
            base = device[j] * piece_rows + starts[a]
            if step >= slots:
                sent[step - slots].wait()
            height = up_to(heights[a], 16)
            whole, rest = height // 256, height % 256

            def body(i, base=base, slot=slot):
                ring[slot, at(i, 256), :] = stream[pl.ds(base + i * 256, 256), :].astype(BF)

            if whole:
                loop(whole, body)
            if rest:
                ring[slot, whole * 256 : whole * 256 + rest, :] = stream[
                    pl.ds(base + whole * 256, rest), :
                ].astype(BF)
            which, lead = targets[a][j]
            target = out_hbm[which] if lead is None else out_hbm[which].at[lead]
            sent.append(
                pltpu.make_async_copy(
                    ring.at[slot, pl.ds(0, widths[a])], target, out_sems.at[slot]
                )
            )
            sent[-1].start()
        for copy in sent[-slots:]:
            copy.wait()

    any_spec = pl.BlockSpec(memory_space=pl.ANY)
    given = [arrays[n] for n in names] + sums
    scalars = [devices]
    if active is not None:
        scalars.append(active.astype(jnp.int32).reshape(1))
    return tuple(
        pl.pallas_call(
            kernel,
            out_shape=list(shapes),
            in_specs=[pl.BlockSpec(memory_space=pltpu.SMEM)] * len(scalars)
            + [any_spec] * (len(given) + len(into)),
            input_output_aliases={len(scalars) + len(given) + n: n for n in range(len(into))},
            out_specs=[any_spec] * len(shapes),
            scratch_shapes=[pltpu.VMEM(a.shape, a.dtype) for a in given]
            + [
                pltpu.VMEM((widest, size), BF),
                pltpu.VMEM((up_to(count * piece_rows, 8) + 64, LANES), F32),
                pltpu.VMEM((slots, max(widths), LANES), BF),
                pltpu.SemaphoreType.DMA((len(given),)),
                pltpu.SemaphoreType.DMA((slots,)),
            ],
            compiler_params=pltpu.CompilerParams(vmem_limit_bytes=63 * 2**20),
        )(*scalars, *given, *into)
    )


def add_up(parts, tail, start, size):
    block = 512
    height = parts[0].shape[0]

    def kernel(*refs):
        refs = list(refs)
        held = [refs.pop(0) for unused in parts]
        tail_ref, out_hbm, stage, sem = refs
        for first in range(0, height, block):
            rows = slice(first, min(first + block, height))
            stage[rows, :] = sum([p[rows, :].astype(F32) for p in held])
        stage[start:size, :] += tail_ref[...].astype(F32)[: size - start]
        copy = pltpu.make_async_copy(stage.at[pl.ds(0, size)], out_hbm.at[:, 0, :], sem)
        copy.start()
        copy.wait()

    return pl.pallas_call(
        kernel,
        out_shape=jax.ShapeDtypeStruct((size, 1, LANES), F32),
        in_specs=[pl.BlockSpec(memory_space=pltpu.VMEM)] * (len(parts) + 1),
        out_specs=pl.BlockSpec(memory_space=pl.ANY),
        scratch_shapes=[pltpu.VMEM((height, LANES), F32), pltpu.SemaphoreType.DMA],
        compiler_params=pltpu.CompilerParams(vmem_limit_bytes=32 * 2**20),
    )(*parts, tail)


def keeping(k, norm, write_out):
    z_ref, r_ref = k[N.z_ + norm], k[N.r_ + norm]

    def write(rows, j, z, out, r):
        z_ref[rows, lanes(j)] = z.astype(BF)
        if j == 0:
            r_ref[rows, :] = jnp.broadcast_to(r, (rows.size, LANES))
        write_out(rows, j, out)

    return write


def to_low(ref):
    def write(rows, j, out):
        ref[rows, lanes(j)] = out.astype(BF)

    return write


def rows_of(ref):
    return lambda rows, j: ref[rows, lanes(j)].astype(F32)


def encoder_forward(k):
    vectors, x0 = k[N.vectors], k[N.tokens]
    size = x0.shape[0]
    h1, x1, glu_a, glu_s = k[N.h1], k[N.x1], k[N.glu_a], k[N.glu_s]
    normalize(k, rows_of(x0), N.norm_glu, D, size, 64, keeping(k, N.norm_glu, to_low(h1)))
    k.put(N.h1)
    def both(j):
        return [dot(h1[...], k.columns(N.glu_weight, c, 2)) for c in (2 * j, 4 + 2 * j)]

    def gate(j, totals):
        a = totals[0] + k.row(N.glu_bias, 2 * j, 2)
        s = sigmoid(totals[1] + k.row(N.glu_bias, 4 + 2 * j, 2))
        cols = at(j, 256)
        glu_a[:, cols] = a.astype(BF)
        glu_s[:, cols] = s.astype(BF)
        x1[:, cols] = x0[:, cols].astype(F32) + a * s

    chunks(2, both, gate)
    k.put(N.glu_a, N.glu_s)
    h2, stacked, mask = k[N.h2], k[N.stacked], k[N.mask]
    edged = Edged(k[N.edged], size)

    def keep_h2(rows, j, out):
        low = out.astype(BF)
        h2[rows, lanes(j)] = low
        stacked[rows, lanes(j + 4)] = low
        edged.store(rows.start, rows.size, j, low.astype(F32))

    normalize(k, rows_of(x1), N.norm_conv, D, size, 64, keeping(k, N.norm_conv, keep_h2))

    def stack(i):
        base = pl.multiple_of(i * 32, 32)
        held = same_segment(mask, base, 32, (-1, 1))
        for first, move in ((0, -1), (8, 1)):
            for j in blocks_of(D):
                value = masked(edged, base, 32, j, move, held)
                stacked[pl.ds(base, 32), lanes(first + j)] = value.astype(BF)

    loop(size // 32, stack, 4)
    k.put(N.h2, N.stacked)
    mixed = Edged(k[N.mixed], size)
    slope_left, slope_right = k[N.slope_left], k[N.slope_right]
    def left(j):
        if j == FF // 256:
            return dot(stacked[...], k.columns(N.right_weight, 0, 2))
        return dot(h2[...], k.columns(N.left_weight, 2 * j, 2))

    def keep_left(j, total):
        if j == FF // 256:
            value, slope = gelu_both(total + k.row(N.right_bias, 0, 2))
            mixed.store_wide(0, value, True)
            slope_right[...] = slope.astype(BF)
            return
        value, slope = gelu_both(total + k.row(N.left_bias, 2 * j, 2))
        mixed.store_wide(j, value)
        slope_left[:, at(j, 256)] = slope.astype(BF)

    chunks(FF // 256 + 1, left, keep_left)
    k.put(N.slope_left, N.slope_right)
    z_middle, r_middle, spread = k[N.z_middle], k[N.r_middle], k[N.spread]

    def keep_middle(rows, j, z, out, r):
        z_middle[rows, lanes(j)] = z.astype(BF)
        mixed.store(rows.start, rows.size, j, out)
        if j == 0:
            r_middle[rows, :] = jnp.broadcast_to(r, (rows.size, LANES))

    normalize(
        k, lambda rows, j: mixed.load(rows.start, rows.size, j), N.middle, FF, size, 16, keep_middle
    )
    k.put(N.z_middle, N.r_middle)
    taps_forward(k, N.depth_taps, moves_of(9, -4), mixed, mask, spread, FF, size)
    k.put(N.spread)
    x2 = k[N.x2]
    x2[:, 0:256] = (
        x1[:, 0:256]
        + dot(spread[...], k.columns(N.point_weight, 0, 2))
        + k.row(N.point_bias, 0, 2)
    )
    x2[:, 256:512] = x1[:, 256:512]
    h3, q, key, value = k[N.h3], k[N.q], k[N.key], k[N.value]
    normalize(k, rows_of(x2), N.norm_attn, D, size, 64, keeping(k, N.norm_attn, to_low(h3)))
    project(k, N.attn_query, h3, q)
    project(k, N.attn_key, h3, key)
    project(k, N.attn_value, h3, value)
    k.put(N.h3, N.q, N.key, N.value)
    attend(q, key, value, k[N.caps], k[N.probs], k[N.heads], HEADS, size)
    heads, x3, h4, inner, slope_feed = k[N.heads], k[N.x3], k[N.h4], k[N.inner], k[N.slope_feed]
    k.put(N.probs, N.heads)
    add_product(k, N.attn_output, heads, x2, x3)
    normalize(k, rows_of(x3), N.norm_feed, D, size, 64, keeping(k, N.norm_feed, to_low(h4)))
    feed_in(k, h4, inner, slope_feed, gelu_both)
    k.put(N.h4, N.inner, N.slope_feed)
    feed_out(k, inner, x3, k[N.memory])


def add_product(k, name, x, base, out):
    def finish(j, total):
        cols = at(j, 256)
        out[:, cols] = base[:, cols] + total

    chunks(D // 256, lambda j: dot(x[...], k.columns(name, 2 * j, 2)), finish)


def feed_in(k, h, inner, slopes, both):
    def finish(j, total):
        value, slope = both(total + k.row(N.feed_in_bias, 2 * j, 2))
        inner[:, at(j, 256)] = value.astype(BF)
        slopes[:, at(j, 256)] = slope.astype(BF)

    chunks(FF // 256, lambda j: dot(h[...], k.columns(N.feed_in_weight, 2 * j, 2)), finish)


def feed_out(k, inner, base, out):
    def finish(j, total):
        cols = at(j, 256)
        out[:, cols] = (base[:, cols] + total + k.row(N.feed_out_bias, 2 * j, 2)).astype(BF)

    chunks(D // 256, lambda j: dot(inner[...], k.columns(N.feed_out_weight, 2 * j, 2)), finish)


def add_all_rows(k, name, ref, width):
    def body(i):
        for j in blocks_of(width):
            k.add_rows(name, j, ref[at(i, 64), lanes(j)].astype(F32))

    loop(ref.shape[0] // 64, body, 4)


def feed_back(k, dout_low, slopes, dpre, dh):
    def finish(j, total):
        grad = total * slopes[:, at(j, 256)].astype(F32)
        k.add_rows(N.feed_in_bias, 2 * j, grad)
        dpre[:, at(j, 256)] = grad.astype(BF)

    chunks(FF // 256, lambda j: dot_t(dout_low[...], k.strip(N.feed_out_weight, j, 256)), finish)

    def write(j, total):
        dh[:, at(j, 256)] = total

    project_back(k, [(N.feed_in_weight, dpre)], write, D)


def add_norm_back(k, norm, size, dh, base, out, low=None):
    z, r = k[N.z_ + norm], k[N.r_ + norm]

    def body(i):
        rows = at(i, 32)
        zs = [z[rows, lanes(j)].astype(F32) for j in blocks_of(D)]
        douts = [dh[rows, lanes(j)] for j in blocks_of(D)]
        grads = norm_gradient(k, norm, D, zs, douts, r[rows, :])
        for j in blocks_of(D):
            total = base(rows, j) + grads[j]
            out[rows, lanes(j)] = total
            if low is not None:
                low[rows, lanes(j)] = total.astype(BF)

    loop(size // 32, body, 4)


def output_of(k, norm):
    z = k[N.z_ + norm]

    def read(rows, j):
        value = z[rows, lanes(j)].astype(F32) * k.row(norm + N._gain, j)
        return value + k.row(norm + N._bias, j)

    return read


def encoder_back(k):
    k[N.vectors]
    dmem = k[N.returned]
    size = dmem.shape[0]
    sums = k[N.vector_sums]
    sums[...] = jnp.zeros(sums.shape, F32)
    dpre, dh, dx = k[N.dpre_feed], k[N.dh], k[N.dx]
    add_all_rows(k, N.feed_out_bias, dmem, D)
    feed_back(k, dmem, k[N.slope_feed], dpre, dh)
    k.put(N.dpre_feed)
    d3 = k[N.d3]
    add_norm_back(k, N.norm_feed, size, dh, rows_of(dmem), dx, d3)
    k.put(N.d3)

    dheads = k[N.dheads]

    def write_heads(j, total):
        dheads[:, at(j, 256)] = total.astype(BF)

    project_back(k, [(N.attn_output, d3)], write_heads, D)
    dq, dkey, dvalue = k[N.dq], k[N.dkey], k[N.dvalue]
    attend_back(
        k[N.q], k[N.key], k[N.value], k[N.probs], dheads, dq, dkey, dvalue, HEADS, size
    )
    k.put(N.dq, N.dkey, N.dvalue)
    def write_dh(j, total):
        dh[:, at(j, 256)] = total

    project_back(
        k, [(N.attn_query, dq), (N.attn_key, dkey), (N.attn_value, dvalue)], write_dh, D
    )
    add_norm_back(k, N.norm_attn, size, dh, rows_of(dx), dx)
    d2, mask = k[N.d2], k[N.mask]
    dspread = Edged(k[N.dspread], size)
    d2[...] = dx[:, 0:256].astype(BF)
    k.put(N.d2)
    add_all_rows(k, N.point_bias, dx.at[:, 0:256], 256)

    def write_spread(j, total):
        dspread.store_wide(j, total)

    project_back(k, [(N.point_weight, d2)], write_spread, FF)
    z_middle, r_middle = k[N.z_middle], k[N.r_middle]

    dmiddle = k[N.dmiddle]

    def write_middle(rows, j, total):
        dmiddle[rows, lanes(j)] = total
    taps_back(
        k, [(N.depth_taps, moves_of(9, -4), dspread)], output_of(k, N.middle), mask, FF, size, write_middle
    )
    slope_left, slope_right = k[N.slope_left], k[N.slope_right]
    dleft, dright = k[N.dleft], k[N.dright]

    def middle(i):
        rows = at(i, 16)
        zs = [z_middle[rows, lanes(j)].astype(F32) for j in blocks_of(FF)]
        douts = [dmiddle[rows, lanes(j)] for j in blocks_of(FF)]
        grads = norm_gradient(k, N.middle, FF, zs, douts, r_middle[rows, :])
        for j in blocks_of(FF):
            grad = grads[j] * slope_left[rows, lanes(j)].astype(F32)
            k.add_rows(N.left_bias, j, grad)
            dleft[rows, lanes(j)] = grad.astype(BF)
        for j in range(2):
            grad = grads[j] * slope_right[rows, lanes(j)].astype(F32)
            k.add_rows(N.right_bias, j, grad)
            dright[rows, lanes(j)] = grad.astype(BF)

    loop(size // 16, middle, 4)
    k.put(N.dleft, N.dright)
    edged, edged_too = dspread.part(0, 4), dspread.part(4, 4)

    def write_before(j, total):
        edged.store_wide(j, total)

    def write_after(j, total):
        edged_too.store_wide(j, total)

    project_back(k, [(N.right_weight, dright)], write_before, D, 0)
    project_back(k, [(N.right_weight, dright)], write_after, D, 2 * D)
    def conv(j):
        total = dot_t(dleft[...], k.strip(N.left_weight, j, 256))
        return total + dot_t(dright[...], k.strip(N.right_weight, j, 256, D))

    chunks(D // 256, conv, write_dh)

    def untap(i):
        base = pl.multiple_of(i * 32, 32)
        held = same_segment(mask, base, 32, (-1, 1))
        for j in blocks_of(D):
            dh[pl.ds(base, 32), lanes(j)] += masked(edged, base, 32, j, 1, held) + masked(
                edged_too, base, 32, j, -1, held
            )

    loop(size // 32, untap, 4)
    add_norm_back(k, N.norm_conv, size, dh, rows_of(dx), dx)
    glu_a, glu_s, dglu = k[N.glu_a], k[N.glu_s], k[N.dglu]

    def gate(i):
        rows = at(i, 32)
        for j in blocks_of(D):
            a, s = glu_a[rows, lanes(j)].astype(F32), glu_s[rows, lanes(j)].astype(F32)
            d = dx[rows, lanes(j)]
            da = d * s
            dg = da * a * (1.0 - s)
            k.add_rows(N.glu_bias, j, da)
            k.add_rows(N.glu_bias, 4 + j, dg)
            dglu[rows, lanes(j)] = da.astype(BF)
            dglu[rows, lanes(4 + j)] = dg.astype(BF)

    loop(size // 32, gate, 4)
    k.put(N.dglu)
    project_back(k, [(N.glu_weight, dglu)], write_dh, D)
    add_norm_back(k, N.norm_glu, size, dh, rows_of(dx), k[N.token_grad])


def decoder_start(k):
    k[N.vectors]
    y0, h = k[N.tokens], k[N.h]
    size = y0.shape[0]
    normalize(k, rows_of(y0), N.norm_branch, D, size, 64, keeping(k, N.norm_branch, to_low(h)))
    k.put(N.h)
    q, key, value = k[N.q_ws], k[N.k_ws], k[N.v_ws]
    project(k, N.wide_self_query, h, q)
    project(k, N.wide_self_key, h, key)
    project(k, N.wide_self_value, h, value)
    k.put(N.q_ws, N.k_ws, N.v_ws)
    project(k, N.wide_cross_query, h, k[N.q_wc])
    k.put(N.q_wc)
    attend(q, key, value, k[N.caps], k[N.p_ws], k[N.o_ws], BRANCH_HEADS, size)
    k.put(N.p_ws, N.o_ws)
    o, base = k[N.o_ws], k[N.base]
    def finish(j, total):
        cols = at(j, 256)
        base[:, cols] = y0[:, cols].astype(F32) + total

    chunks(D // 256, lambda j: dot(o[...], k.columns(N.wide_self_output, 2 * j, 2)), finish)


def decoder_forward(k):
    k[N.vectors]
    memory = k[N.memory]
    size = memory.shape[0]
    project(k, N.wide_cross_key, memory, k[N.k_wc])
    project(k, N.wide_cross_value, memory, k[N.v_wc])
    k.put(N.k_wc, N.v_wc)
    attend(
        k[N.q_wc], k[N.k_wc], k[N.v_wc], k[N.caps_cross], k[N.p_wc], k[N.o_wc], BRANCH_HEADS, size
    )
    k.put(N.p_wc, N.o_wc)
    y1, edged = k[N.y1], Edged(k[N.edged], size)
    add_product(k, N.wide_cross_output, k[N.o_wc], k[N.base], y1)

    def keep_conv(rows, j, out):
        edged.store(rows.start, rows.size, j, out)

    normalize(k, rows_of(y1), N.norm_conv, D, size, 64, keeping(k, N.norm_conv, keep_conv))
    mask, left_in, right_in = k[N.mask], k[N.left_in], k[N.right_in]
    taps_forward(k, N.left_taps, moves_of(11, -10), edged, mask, left_in, D, size)
    taps_forward(k, N.right_taps, moves_of(7, -6), edged, mask, right_in, D, size)
    k.put(N.left_in, N.right_in)
    mixed, slope_left = Edged(k[N.mixed], size), k[N.slope_left]
    def left(j):
        if j == 2 * D // 256:
            return dot(right_in[...], k.columns(N.right_weight, 0, 2))
        return dot(left_in[...], k.columns(N.left_weight, 2 * j, 2))

    def keep_left(j, total):
        if j == 2 * D // 256:
            mixed.store_wide(0, total + k.row(N.right_bias, 0, 2), True)
            return
        value, slope = gelu_both(total + k.row(N.left_bias, 2 * j, 2))
        mixed.store_wide(j, value)
        slope_left[:, at(j, 256)] = slope.astype(BF)

    chunks(2 * D // 256 + 1, left, keep_left)
    k.put(N.slope_left)
    z_middle, r_middle = k[N.z_middle], k[N.r_middle]

    def keep_middle(rows, j, z, out, r):
        z_middle[rows, lanes(j)] = z.astype(BF)
        mixed.store(rows.start, rows.size, j, out)
        if j == 0:
            r_middle[rows, :] = jnp.broadcast_to(r, (rows.size, LANES))

    normalize(
        k, lambda rows, j: mixed.load(rows.start, rows.size, j), N.middle, 2 * D, size, 32, keep_middle
    )
    k.put(N.z_middle, N.r_middle)
    out_in, y2 = k[N.out_in], k[N.y2]
    taps_forward(k, N.out_taps, moves_of(7, -6), mixed, mask, out_in, 2 * D, size)
    k.put(N.out_in)
    def conv_out(j, total):
        cols = at(j, 256)
        y2[:, cols] = y1[:, cols] + total + k.row(N.out_bias, 2 * j, 2)

    chunks(D // 256, lambda j: dot(out_in[...], k.columns(N.out_weight, 2 * j, 2)), conv_out)
    h_s, y3 = k[N.h_s], k[N.y3]
    normalize(k, rows_of(y2), N.norm_self, D, size, 64, keeping(k, N.norm_self, to_low(h_s)))
    project(k, N.self_query, h_s, k[N.q_s])
    project(k, N.self_key, h_s, k[N.k_s])
    project(k, N.self_value, h_s, k[N.v_s])
    k.put(N.h_s, N.q_s, N.k_s, N.v_s)
    attend(k[N.q_s], k[N.k_s], k[N.v_s], k[N.caps], k[N.p_s], k[N.o_s], HEADS, size)
    k.put(N.p_s, N.o_s)
    add_product(k, N.self_output, k[N.o_s], y2, y3)
    h_c, y4 = k[N.h_c], k[N.y4]
    normalize(k, rows_of(y3), N.norm_cross, D, size, 64, keeping(k, N.norm_cross, to_low(h_c)))
    project(k, N.cross_query, h_c, k[N.q_c])
    project(k, N.cross_key, memory, k[N.k_c])
    project(k, N.cross_value, memory, k[N.v_c])
    k.put(N.h_c, N.q_c, N.k_c, N.v_c)
    attend(k[N.q_c], k[N.k_c], k[N.v_c], k[N.caps_cross], k[N.p_c], k[N.o_c], HEADS, size)
    k.put(N.p_c, N.o_c)
    add_product(k, N.cross_output, k[N.o_c], y3, y4)
    h_f, inner, slope_feed = k[N.h_f], k[N.inner], k[N.slope_feed]
    normalize(k, rows_of(y4), N.norm_feed, D, size, 64, keeping(k, N.norm_feed, to_low(h_f)))
    feed_in(k, h_f, inner, slope_feed, silu_both)
    k.put(N.h_f, N.inner, N.slope_feed)
    feed_out(k, inner, y4, k[N.output])


def decoder_back(k):
    k[N.vectors]
    dout = k[N.cotangent]
    size = dout.shape[0]
    sums = k[N.vector_sums]
    sums[...] = jnp.zeros(sums.shape, F32)
    dpre, dh, dx, dmem = k[N.dpre_feed], k[N.dh], k[N.dx], k[N.dmem]
    add_all_rows(k, N.feed_out_bias, dout, D)
    feed_back(k, dout, k[N.slope_feed], dpre, dh)
    k.put(N.dpre_feed)
    d4 = k[N.d4]
    add_norm_back(k, N.norm_feed, size, dh, rows_of(dout), dx, d4)
    k.put(N.d4)
    dheads = k[N.dheads]

    def write_heads(j, total):
        dheads[:, at(j, 256)] = total.astype(BF)

    def write_dh(j, total):
        dh[:, at(j, 256)] = total

    def write_dmem(j, total):
        dmem[:, at(j, 256)] = total

    project_back(k, [(N.cross_output, d4)], write_heads, D)
    dq, dkey, dvalue = k[N.dq_c], k[N.dk_c], k[N.dv_c]
    attend_back(k[N.q_c], k[N.k_c], k[N.v_c], k[N.p_c], dheads, dq, dkey, dvalue, HEADS, size)
    k.put(N.dq_c, N.dk_c, N.dv_c)
    project_back(k, [(N.cross_query, dq)], write_dh, D)
    project_back(k, [(N.cross_key, dkey), (N.cross_value, dvalue)], write_dmem, D)
    d3 = k[N.d3]
    add_norm_back(k, N.norm_cross, size, dh, rows_of(dx), dx, d3)
    k.put(N.d3)
    project_back(k, [(N.self_output, d3)], write_heads, D)
    dq, dkey, dvalue = k[N.dq_s], k[N.dk_s], k[N.dv_s]
    attend_back(k[N.q_s], k[N.k_s], k[N.v_s], k[N.p_s], dheads, dq, dkey, dvalue, HEADS, size)
    k.put(N.dq_s, N.dk_s, N.dv_s)
    project_back(
        k, [(N.self_query, dq), (N.self_key, dkey), (N.self_value, dvalue)], write_dh, D
    )
    d2 = k[N.d2]
    add_norm_back(k, N.norm_self, size, dh, rows_of(dx), dx, d2)
    k.put(N.d2)
    add_all_rows(k, N.out_bias, dx, D)
    dspread, mask = Edged(k[N.dspread], size), k[N.mask]

    def write_spread(j, total):
        dspread.store_wide(j, total)

    project_back(k, [(N.out_weight, d2)], write_spread, 2 * D)
    z_middle, r_middle = k[N.z_middle], k[N.r_middle]

    dmiddle = k[N.dmiddle]

    def write_middle(rows, j, total):
        dmiddle[rows, lanes(j)] = total
    taps_back(
        k, [(N.out_taps, moves_of(7, -6), dspread)], output_of(k, N.middle), mask, 2 * D, size, write_middle
    )
    slope_left, dleft, dright = k[N.slope_left], k[N.dleft], k[N.dright]

    def middle(i):
        rows = at(i, 16)
        zs = [z_middle[rows, lanes(j)].astype(F32) for j in blocks_of(2 * D)]
        douts = [dmiddle[rows, lanes(j)] for j in blocks_of(2 * D)]
        grads = norm_gradient(k, N.middle, 2 * D, zs, douts, r_middle[rows, :])
        for j in blocks_of(2 * D):
            grad = grads[j] * slope_left[rows, lanes(j)].astype(F32)
            k.add_rows(N.left_bias, j, grad)
            dleft[rows, lanes(j)] = grad.astype(BF)
        for j in range(2):
            k.add_rows(N.right_bias, j, grads[j])
            dright[rows, lanes(j)] = grads[j].astype(BF)

    loop(size // 16, middle, 4)
    k.put(N.dleft, N.dright)
    dleft_in, dright_in = dspread.part(0, 4), dspread.part(4, 4)

    def write_left(j, total):
        dleft_in.store_wide(j, total)

    def write_right(j, total):
        dright_in.store_wide(j, total)

    project_back(k, [(N.left_weight, dleft)], write_left, D)
    project_back(k, [(N.right_weight, dright)], write_right, D)
    def write_conv(rows, j, total):
        dh[rows, lanes(j)] = total

    taps_back(
        k,
        [(N.left_taps, moves_of(11, -10), dleft_in), (N.right_taps, moves_of(7, -6), dright_in)],
        output_of(k, N.norm_conv),
        mask,
        D,
        size,
        write_conv,
    )
    d1 = k[N.d1]
    add_norm_back(k, N.norm_conv, size, dh, rows_of(dx), dx, d1)
    k.put(N.d1, N.dx)
    project_back(k, [(N.wide_cross_output, d1)], write_heads, D)
    dq, dkey, dvalue = k[N.dq_wc], k[N.dk_wc], k[N.dv_wc]
    attend_back(
        k[N.q_wc], k[N.k_wc], k[N.v_wc], k[N.p_wc], dheads, dq, dkey, dvalue, BRANCH_HEADS, size
    )
    k.put(N.dq_wc, N.dk_wc, N.dv_wc)
    sent = k[N.sent]

    def write_sent(j, total):
        sent[:, at(j, 256)] = (dmem[:, at(j, 256)] + total).astype(BF)

    project_back(k, [(N.wide_cross_key, dkey), (N.wide_cross_value, dvalue)], write_sent, D)


def branch_back(k):
    k[N.vectors]
    d1 = k[N.d1]
    size = d1.shape[0]
    sums = k[N.vector_sums]
    sums[...] = jnp.zeros(sums.shape, F32)
    dheads, dh = k[N.dheads], k[N.dh]

    def write_heads(j, total):
        dheads[:, at(j, 256)] = total.astype(BF)

    project_back(k, [(N.wide_self_output, d1)], write_heads, D)
    dq, dkey, dvalue = k[N.dq_ws], k[N.dk_ws], k[N.dv_ws]
    attend_back(
        k[N.q_ws], k[N.k_ws], k[N.v_ws], k[N.p_ws], dheads, dq, dkey, dvalue, BRANCH_HEADS, size, 2
    )
    k.put(N.dq_ws, N.dk_ws, N.dv_ws)

    def write_dh(j, total):
        dh[:, at(j, 256)] = total

    project_back(
        k,
        [
            (N.wide_self_query, dq),
            (N.wide_self_key, dkey),
            (N.wide_self_value, dvalue),
            (N.wide_cross_query, k[N.dq_wc]),
        ],
        write_dh,
        D,
    )
    add_norm_back(k, N.norm_branch, size, dh, rows_of(k[N.dx]), k[N.token_grad])


def segment_ids(lengths_rows, token_count):
    ends_at = jnp.cumsum(lengths_rows, axis=-1)
    places = jnp.arange(token_count, dtype=jnp.int32)
    return jnp.sum((places[None, :, None] >= ends_at[:, None, :]).astype(jnp.int32), axis=2)


def spread_segments(segments):
    micro, tokens = segments.shape
    own = segments + tokens * jnp.arange(micro, dtype=jnp.int32)[:, None]
    own = jnp.pad(own.reshape(micro * tokens), (EDGE, EDGE), constant_values=-1)
    return jnp.broadcast_to(own.astype(F32)[:, None], (own.shape[0], LANES))


def caps_of(allowed):
    return jnp.where(allowed, jnp.float32(3e38), jnp.float32(-1e30))


def low_like(size, width, kind=BF):
    return jax.ShapeDtypeStruct((size, width), kind)


def tail_pad(value, rows):
    return jnp.pad(value, ((0, rows - value.shape[0]), (0, 0)))


def local(tokens, lengths, params, cotangent):
    count = lax.axis_size("dp")
    is_first = lax.axis_index("section") == 0
    enc_rows = 2 * -(-ENC.rows // (2 * count))
    dec_rows = 2 * -(-DEC.rows // (2 * count))
    own_rows = params.shape[1]
    own = params[0]
    micro, pack_tokens = tokens.shape[1], tokens.shape[2]
    size = micro * pack_tokens

    holders = slot_devices(GATHER_ORDER, count)
    takers = slot_devices(REDUCE_ORDER, count)
    main_height, tail_height = up_to(own_rows, 16), up_to(own_rows - enc_rows, 16)
    whole, tails = gather_slots(tail_pad(own.astype(BF), main_height), enc_rows, count)

    source_ids = segment_ids(lengths[0, :, 0], pack_tokens)
    target_ids = segment_ids(lengths[1, :, 0], pack_tokens)
    places = jnp.arange(pack_tokens, dtype=jnp.int32)
    early = places[:, None] <= places[None, :]
    mask = spread_segments(jnp.where(is_first, source_ids, target_ids))
    same_source = source_ids[:, :, None] == source_ids[:, None, :]
    same_target = (target_ids[:, :, None] == target_ids[:, None, :]) & early[None]
    caps = caps_of(jnp.where(is_first, same_source, same_target))
    caps_cross = caps_of(source_ids[:, :, None] == target_ids[:, None, :])
    mask, caps, caps_cross = lax.optimization_barrier((mask, caps, caps_cross))
    own_tokens = tokens[0].reshape(size, D)
    given = cotangent.reshape(size, D)

    low = low_like(size, D)
    full = low_like(size, D, F32)
    wide = low_like(size, FF)
    rows = low_like(size, LANES, F32)
    edged = ((4 * (size + 2 * EDGE), LANES), F32)
    edged_wide = ((16 * (size + 2 * EDGE), LANES), F32)
    edged_two = ((8 * (size + 2 * EDGE), LANES), F32)
    packs = size // PACK
    probs_16 = low_like(packs * BRANCH_HEADS * PACK, PACK)
    probs_8 = low_like(packs * HEADS * PACK, PACK)
    sums = low_like(VECTOR_ROWS * 8, LANES, F32)

    norm_out = lambda *names: {N.z_ + n: low for n in names} | {N.r_ + n: rows for n in names}
    enc_out = norm_out(N.norm_glu, N.norm_conv, N.norm_attn, N.norm_feed) | dict(
        h1=low, glu_a=low, glu_s=low, h2=low, stacked=low_like(size, 3 * D),
        slope_left=wide, slope_right=low_like(size, 256), z_middle=wide, r_middle=rows,
        spread=wide, h3=low, q=low, key=low, value=low, probs=probs_8, heads=low,
        h4=low, inner=wide, slope_feed=wide, memory=low,
    )
    start_out = norm_out(N.norm_branch) | dict(
        h=low, q_ws=low, k_ws=low, v_ws=low, q_wc=low, p_ws=probs_16, o_ws=low, base=full
    )
    made = dict(
        weights=low_like(WEIGHT_ROWS, LANES), vectors=low_like(VECTOR_ROWS, LANES, F32)
    )

    def encoder_start():
        weights, vectors = lay_out(ENC, [whole], [0], enc_rows, holders)
        result = fused(
            encoder_forward,
            ENC,
            weights,
            list(ENC.weights),
            dict(vectors=vectors, tokens=own_tokens, mask=mask, caps=caps),
            enc_out,
            {},
            dict(
                edged=edged, mixed=edged_wide, x1=((size, D), F32), x2=((size, D), F32),
                x3=((size, D), F32),
            ),
        )
        return result | dict(weights=weights, vectors=vectors)

    enc = lax.cond(is_first, encoder_start, lambda: idle(enc_out | made))
    tails[-1], enc[N.memory] = lax.optimization_barrier((tails[-1], enc[N.memory]))
    ends = share_tails(tails, count)

    def decoder_begin():
        weights, vectors = lay_out(DEC, [whole, ends], [0, own_rows], dec_rows, holders)
        result = fused(
            decoder_start,
            DEC,
            weights,
            [N.wide_self_query, N.wide_self_key, N.wide_self_value, N.wide_cross_query, N.wide_self_output],
            dict(vectors=vectors, tokens=own_tokens, caps=caps),
            start_out,
            {},
            {},
        )
        return result | dict(weights=weights, vectors=vectors)

    dec = lax.cond(~is_first, decoder_begin, lambda: idle(start_out | made))
    memory = lax.ppermute(enc[N.memory], "section", [(0, 1)])

    forward_out = norm_out(N.norm_conv, N.norm_self, N.norm_cross, N.norm_feed) | dict(
        k_wc=low, v_wc=low, p_wc=probs_16, o_wc=low, left_in=low, right_in=low,
        slope_left_d=low_like(size, 2 * D), z_middle_d=low_like(size, 2 * D), r_middle_d=rows,
        out_in=low_like(size, 2 * D), h_s=low, q_s=low, k_s=low, v_s=low, p_s=probs_8, o_s=low,
        h_c=low, q_c=low, k_c=low, v_c=low, p_c=probs_8, o_c=low, h_f=low,
        inner_d=wide, slope_feed_d=wide, output=low,
    )
    early_names = (N.wide_self, N.wide_cross_query)
    later = [n for n in DEC.weights if not n.startswith(early_names)]
    back_out = dict(
        dpre_feed=wide, d4=low, dq_c=low, dk_c=low, dv_c=low, d3=low, dq_s=low, dk_s=low, dv_s=low,
        d2=low, dleft=low_like(size, 2 * D), dright=low_like(size, 256), d1=low, dx=full,
        dq_wc=low, dk_wc=low, dv_wc=low, vector_sums=sums, sent=low,
    )
    back_names = [
        N.feed_out_weight, N.feed_in_weight, N.cross_output, N.cross_query, N.cross_key, N.cross_value,
        N.self_output, N.self_query, N.self_key, N.self_value, N.out_weight, N.left_weight, N.right_weight,
        N.wide_cross_output, N.wide_cross_key, N.wide_cross_value,
    ]
    saved = [
        N.slope_feed, N.z_norm_feed, N.r_norm_feed, N.q_c, N.k_c, N.v_c, N.p_c, N.z_norm_cross,
        N.r_norm_cross, N.q_s, N.k_s, N.v_s, N.p_s, N.z_norm_self, N.r_norm_self, N.z_middle,
        N.r_middle, N.slope_left, N.z_norm_conv, N.r_norm_conv, N.k_wc, N.v_wc, N.p_wc,
    ]

    def decode_forward():
        return fused(
            decoder_forward,
            DEC,
            dec[N.weights],
            later,
            dict(
                vectors=dec[N.vectors], memory=memory, q_wc=dec[N.q_wc], caps_cross=caps_cross,
                base=dec[N.base], mask=mask, caps=caps,
            ),
            strip_names(forward_out),
            {},
            dict(
                edged=edged, mixed=edged_two, y1=((size, D), F32), y2=((size, D), F32),
                y3=((size, D), F32), y4=((size, D), F32),
            ),
        )

    def decode_back():
        return fused(
            decoder_back,
            DEC,
            dec[N.weights],
            back_names,
            dict(vectors=dec[N.vectors], cotangent=given)
            | {n: forward[n] for n in saved}
            | dict(mask=mask, q_wc=dec[N.q_wc]),
            back_out,
            {},
            dict(
                dh=((size, D), F32), dmem=((size, D), F32), dheads=((size, D), BF), dspread=edged_two,
                dmiddle=((size, 2 * D), F32),
            ),
        )

    forward = lax.cond(~is_first, decode_forward, lambda: idle(strip_names(forward_out)))
    back = lax.cond(~is_first, decode_back, lambda: idle(back_out))
    returned = lax.ppermute(back[N.sent], "section", [(1, 0)])
    returned, back[N.d1] = lax.optimization_barrier((returned, back[N.d1]))

    enc_last = dict(
        dpre_feed=wide, d3=low, dq=low, dkey=low, dvalue=low, d2=low_like(size, 256), dleft=wide,
        dright=low_like(size, 256), dglu=low_like(size, 2 * D), token_grad=full, vector_sums=sums,
    )
    dec_last = dict(dq_ws=low, dk_ws=low, dv_ws=low, token_grad=full, vector_sums=sums)
    enc_names = [
        N.feed_out_weight, N.feed_in_weight, N.attn_output, N.attn_query, N.attn_key, N.attn_value,
        N.point_weight, N.right_weight, N.left_weight, N.glu_weight,
    ]
    enc_saved = [
        N.slope_feed, N.z_norm_feed, N.r_norm_feed, N.q, N.key, N.value, N.probs, N.z_norm_attn,
        N.r_norm_attn, N.z_middle, N.r_middle, N.slope_left, N.slope_right, N.z_norm_conv,
        N.r_norm_conv, N.glu_a, N.glu_s, N.z_norm_glu, N.r_norm_glu,
    ]
    enc_products = [
        (N.feed_out_weight, N.inner, N.returned), (N.feed_in_weight, N.h4, N.dpre_feed),
        (N.attn_output, N.heads, N.d3), (N.attn_query, N.h3, N.dq), (N.attn_key, N.h3, N.dkey),
        (N.attn_value, N.h3, N.dvalue), (N.point_weight, N.spread, N.d2),
        (N.right_weight, N.stacked, N.dright), (N.left_weight, N.h2, N.dleft), (N.glu_weight, N.h1, N.dglu),
    ]
    dec_products = [
        (N.feed_out_weight, N.inner, N.cotangent), (N.feed_in_weight, N.h_f, N.dpre_feed),
        (N.cross_output, N.o_c, N.d4), (N.cross_query, N.h_c, N.dq_c), (N.cross_key, N.memory, N.dk_c),
        (N.cross_value, N.memory, N.dv_c), (N.wide_cross_key, N.memory, N.dk_wc),
        (N.wide_cross_value, N.memory, N.dv_wc), (N.self_output, N.o_s, N.d3),
        (N.self_query, N.h_s, N.dq_s), (N.self_key, N.h_s, N.dk_s), (N.self_value, N.h_s, N.dv_s),
        (N.out_weight, N.out_in, N.d2), (N.left_weight, N.left_in, N.dleft),
        (N.right_weight, N.right_in, N.dright), (N.wide_cross_output, N.o_wc, N.d1),
        (N.wide_self_output, N.o_ws, N.d1), (N.wide_self_query, N.h, N.dq_ws), (N.wide_self_key, N.h, N.dk_ws),
        (N.wide_self_value, N.h, N.dv_ws), (N.wide_cross_query, N.h, N.dq_wc),
    ]

    def only(arrays, products):
        return {n: arrays[n] for p in products for n in p[1:]}

    if by_neighbours(count):
        main_shapes = [low_like(main_height, LANES)] * 16
        tail_shapes = [jax.ShapeDtypeStruct((8, tail_height, LANES), BF)] * 2
        main_targets = [(n, None) for n in range(16)]
        tail_targets = [(16 + o, n) for n in range(8) for o in range(2)]
    else:
        main_shapes = [jax.ShapeDtypeStruct((count, main_height, LANES), BF)]
        tail_shapes = [jax.ShapeDtypeStruct((count, tail_height, LANES), BF)]
        main_targets = [(0, j) for j in range(count)]
        tail_targets = [(1, j) for j in range(count)]

    def decoder_last():
        last = fused(
            branch_back,
            DEC,
            dec[N.weights],
            [
                N.wide_self_output, N.wide_self_query, N.wide_self_key, N.wide_self_value,
                N.wide_cross_query,
            ],
            dict(vectors=dec[N.vectors], d1=back[N.d1])
            | {n: dec[n] for n in (N.q_ws, N.k_ws, N.v_ws, N.p_ws)}
            | {n: dec[n] for n in (N.z_norm_branch, N.r_norm_branch)}
            | dict(dq_wc=back[N.dq_wc], dx=back[N.dx]),
            dec_last,
            {},
            dict(dheads=((size, D), BF), dh=((size, D), F32)),
        )
        arrays = dec | forward | back | last | dict(cotangent=given, memory=memory)
        grads = weight_gradients(
            DEC, dec_products, only(arrays, dec_products), [back[N.vector_sums], last[N.vector_sums]],
            main_shapes + tail_shapes, [main_targets, tail_targets], [0, own_rows], dec_rows, takers, False,
        )
        return last[N.token_grad], grads

    def encoder_last():
        last = fused(
            encoder_back,
            ENC,
            enc[N.weights],
            enc_names,
            dict(vectors=enc[N.vectors], returned=returned)
            | {n: enc[n] for n in enc_saved}
            | dict(mask=mask),
            enc_last,
            {},
            dict(
                dh=((size, D), F32), dx=((size, D), F32), dheads=((size, D), BF), dspread=edged_wide,
                dmiddle=((size, FF), F32),
            ),
        )
        return last

    def nothing(shapes):
        names = dict(enumerate(shapes))
        return tuple(idle(names).values())

    source_back = lax.cond(is_first, encoder_last, lambda: idle(enc_last))
    target_grad, dec_grads = lax.cond(
        ~is_first,
        decoder_last,
        lambda: (idle(dict(grad=full))[N.grad], nothing(main_shapes + tail_shapes)),
    )
    tails = hand_over_tails(dec_grads[len(main_shapes) :], count)
    enc_arrays = only(enc | source_back | dict(returned=returned), enc_products)
    grads = weight_gradients(
        ENC, enc_products, enc_arrays, [source_back[N.vector_sums]], main_shapes, [main_targets], [0],
        enc_rows, takers, False, dec_grads[: len(main_shapes)], is_first,
    )

    parts, tail = reduce_slots(grads, tails, enc_rows, count)
    param_out = add_up(parts, tail, enc_rows, own_rows).reshape(1, own_rows, LANES)
    token_grads = jnp.where(is_first, source_back[N.token_grad], target_grad)
    shape = (1, micro, pack_tokens, D)
    results = jnp.where(is_first, returned, forward[N.output])
    return (results.reshape(shape), token_grads.reshape(shape), param_out)


def strip_names(outs):
    return {n[:-2] if n.endswith(N._d) else n: v for n, v in outs.items()}


def idle(outs):
    names = list(outs)

    def kernel(*refs):
        return None

    any_spec = pl.BlockSpec(memory_space=pl.ANY)
    result = pl.pallas_call(
        kernel,
        out_shape=[outs[n] for n in names],
        out_specs=[any_spec] * len(names),
    )()
    return dict(zip(names, result))


def solution(mesh):
    return jax.shard_map(
        local,
        mesh=mesh,
        in_specs=(
            P("section", None, "dp", None),
            P(None, None, "dp", None),
            P("section", "dp", None),
            P(None, "dp", None),
        ),
        out_specs=(
            P("section", None, "dp", None),
            P("section", None, "dp", None),
            P("section", "dp", None),
        ),
        check_vma=False,
    )
```

```python
import math

import jax
import jax.numpy as jnp
from jax import lax
from jax.experimental import pallas as pl
from jax.experimental.pallas import tpu as pltpu
from jax.sharding import PartitionSpec as P


class Names:
    def __getattr__(self, name):
        return name


N = Names()
D = 512
FF = 2048
HEADS = 8
BRANCH_HEADS = 16
LANES = 128
PACK = 256
EDGE = 16

epsilon = 1e-06
blocked = -1000000000.0
BF = jnp.bfloat16
F32 = jnp.float32


def attention_entries(prefix):
    return [(prefix + part, (D, D)) for part in (N._query, N._key, N._value, N._output)]


def norm_entries(prefix, width_of):
    return [(prefix + N._gain, (width_of,)), (prefix + N._bias, (width_of,))]


def encoder_layout():
    half_width = D // 2
    return (
        norm_entries(N.norm_glu, D)
        + [(N.glu_weight, (D, 2 * D)), (N.glu_bias, (2 * D,))]
        + norm_entries(N.norm_conv, D)
        + [
            (N.left_weight, (D, FF)),
            (N.left_bias, (FF,)),
            (N.right_weight, (3 * D, half_width)),
            (N.right_bias, (half_width,)),
        ]
        + norm_entries(N.middle, FF)
        + [
            (N.depth_taps, (9, FF)),
            (N.point_weight, (FF, half_width)),
            (N.point_bias, (half_width,)),
        ]
        + norm_entries(N.norm_attn, D)
        + attention_entries(N.attn)
        + norm_entries(N.norm_feed, D)
        + [
            (N.feed_in_weight, (D, FF)),
            (N.feed_in_bias, (FF,)),
            (N.feed_out_weight, (FF, D)),
            (N.feed_out_bias, (D,)),
        ]
    )


def decoder_layout():
    half_width = D // 2
    return (
        norm_entries(N.norm_branch, D)
        + attention_entries(N.wide_self)
        + attention_entries(N.wide_cross)
        + norm_entries(N.norm_conv, D)
        + [
            (N.left_taps, (11, D)),
            (N.left_weight, (D, 2 * D)),
            (N.left_bias, (2 * D,)),
            (N.right_taps, (7, D)),
            (N.right_weight, (D, half_width)),
            (N.right_bias, (half_width,)),
        ]
        + norm_entries(N.middle, 2 * D)
        + [
            (N.out_taps, (7, 2 * D)),
            (N.out_weight, (2 * D, D)),
            (N.out_bias, (D,)),
        ]
        + norm_entries(N.norm_self, D)
        + attention_entries(N.self)
        + norm_entries(N.norm_cross, D)
        + attention_entries(N.cross)
        + norm_entries(N.norm_feed, D)
        + [
            (N.feed_in_weight, (D, FF)),
            (N.feed_in_bias, (FF,)),
            (N.feed_out_weight, (FF, D)),
            (N.feed_out_bias, (D,)),
        ]
    )


class Table:
    def __init__(self, entries):
        self.at, self.weights, self.vectors, self.heights = {}, {}, {}, {}
        offset = weight_rows = vector_rows = 0
        for name, shape in entries:
            rows = math.prod(shape) // LANES
            self.at[name] = offset
            self.heights[name] = rows
            if len(shape) == 2 and shape[0] >= D:
                self.weights[name] = (weight_rows, shape[0], shape[1] // LANES)
                weight_rows += rows
            else:
                self.vectors[name] = (vector_rows, rows)
                vector_rows += rows
            offset += rows
        self.rows, self.weight_rows, self.vector_rows = offset, weight_rows, vector_rows


ENC = Table(encoder_layout())
DEC = Table(decoder_layout())
WEIGHT_ROWS = max(ENC.weight_rows, DEC.weight_rows)
VECTOR_ROWS = -(-max(ENC.vector_rows, DEC.vector_rows) // 16) * 16


def up_to(value, step):
    return -(-value // step) * step


AXES = ("section", "dp")


def pairs(count, move, sections):
    return [
        (s * count + i, s * count + j)
        for s in sections
        for i in range(count)
        for j in [move(i)]
        if j is not None
    ]


def swap(value, bit, count, sections):
    return lax.ppermute(value, AXES, pairs(count, lambda i: i ^ bit, sections))


def shift(value, step, count, sections, senders):
    def move(i):
        return i + 4 * step if i // 4 in senders and 0 <= i + 4 * step < count else None

    return lax.ppermute(value, AXES, pairs(count, move, sections))


def pick(z, options):
    out = options[0]
    for k in range(1, len(options)):
        if options[k] is not options[k - 1]:
            out = jnp.where(z >= k, options[k], out)
    return out


def by_neighbours(count):
    return count == 16


REDUCE_ORDER = [[3, 2, 1, 0], [3, 2, 0, 1], [0, 1, 3, 2], [0, 1, 2, 3]]
GATHER_ORDER = [[0, 1, 2, 3], [1, 0, 2, 3], [2, 1, 3, 0], [3, 2, 1, 0]]


def slot_devices(order, count):
    if not by_neighbours(count):
        return jnp.arange(count, dtype=jnp.int32)
    me = lax.axis_index("dp")
    z, y, c = me // 4, (me // 2) % 2, me % 2
    return jnp.stack(
        [
            pick(z, [own[k] for own in order]) * 4 + yy * 2 + cc
            for k in range(4)
            for yy in (y, 1 - y)
            for cc in (c, 1 - c)
        ]
    ).astype(jnp.int32)


def gather_slots(own, start, count):
    if not by_neighbours(count):
        held = lax.all_gather(own, "dp", axis=0)
        tails = lax.ppermute(held[:, start:], "section", [(0, 1)])
        tails = jnp.pad(tails, ((0, 0), (0, -tails.shape[1] % 16), (0, 0)))
        return [(held, j) for j in range(count)], [tails]
    z = lax.axis_index("dp") // 4
    both = (0, 1)
    near, far, near_other, far_other = [own], [], [], []
    up = down = own
    held = []
    ends = []

    def cross(steps):
        tails = jnp.stack([slot[start:] for k in steps for slot in (near[k], far[k])])
        ends.append(lax.ppermute(tails, "section", [(0, 1)]))

    for step in range(4):
        swapped = swap(near[step], 2, count, both)
        ups, downs = up, down
        if step == 3:
            cross((0, 1, 2))
        if step < 3:
            up = shift(ups, 1, count, both, [(0, 1, 2), (1, 2), (2,)][step])
            down = shift(downs, -1, count, both, [(3, 2, 1), (1, 2), (1,)][step])
        near_other.append(swap(near[step], 1, count, both))
        if step:
            far_other.append(swap(far[step - 1], 1, count, both))
        swapped, up, down, near_other, far_other = lax.optimization_barrier(
            (swapped, up, down, near_other, far_other)
        )
        far.append(swapped)
        held.append((up, down))
        if step == 0:
            near.append(pick(z, [down, up, up, up]))
        if step == 1:
            first_down = held[0][1]
            near.append(pick(z, [down, first_down, first_down, up]))
        if step == 2:
            near.append(pick(z, [down, held[1][1], held[1][0], up]))
    far_other.append(swap(far[3], 1, count, both))
    cross((3,))
    whole = [
        (slot, None) for k in range(4) for slot in (near[k], near_other[k], far[k], far_other[k])
    ]
    return whole, ends


def share_tails(tails, count):
    if not by_neighbours(count):
        return [(tails[0], j) for j in range(count)]
    others = [swap(part, 1, count, (1,)) for part in tails]
    return [
        (held[part], n) for part in range(2) for n in range((6, 2)[part]) for held in (tails, others)
    ]


def hand_over_tails(tails, count):
    if not by_neighbours(count):
        tail = lax.psum_scatter(tails[0], "dp", scatter_dimension=0, tiled=False)
        return lax.ppermute(tail, "section", [(1, 0)])
    same, other = tails
    mine = same.astype(F32) + swap(other, 1, count, (1,)).astype(F32)
    mine = mine.reshape((4, 2) + mine.shape[1:])
    got = swap(mine[:, 1].astype(BF), 2, count, (1,))
    mine = (mine[:, 0] + got.astype(F32)).astype(BF)
    return lax.ppermute(mine, "section", [(1, 0)])


def reduce_slots(slots, tails, start, count):
    if not by_neighbours(count):
        return [lax.psum_scatter(slots[0], "dp", scatter_dimension=0, tiled=False)], tails
    z = lax.axis_index("dp") // 4
    both = (0, 1)
    low = BF

    def add(*terms):
        return sum([term.astype(F32) for term in terms])

    def with_tail(total, n):
        return total + jnp.pad(tails[n].astype(F32), ((start, 0), (0, 0)))

    def crossed(k):
        return [swap(slots[4 * k + 2 * f + 1], 1, count, both) for f in (1, 0)]

    def leaving(k):
        return add(slots[4 * k + 2], others[k][0]).astype(low)

    def arrived(k):
        return with_tail(add(*joined[k]), k)

    others = [crossed(0), crossed(1)]
    out = leaving(0)
    joined = []
    up = down = None
    for k in range(4):
        got = swap(out, 2, count, both)
        sent_up = sent_down = None
        if k:
            sent_up = shift(up, 1, count, both, range(k))
            sent_down = shift(down, -1, count, both, range(4 - k, 4))
        if k < 3:
            out = leaving(k + 1)
        if k < 2:
            others.append(crossed(k + 2))
        got, sent_up, sent_down, out, others = lax.optimization_barrier(
            (got, sent_up, sent_down, out, others)
        )
        joined.append([slots[4 * k], others[k][1], got])
        if k == 0:
            up = down = arrived(0).astype(low)
        if k in (1, 2):
            up_from = [[k, k - 1, k - 1, k - 1], [2, 1, 2, 2]][k - 1]
            down_from = [[k - 1, k - 1, k - 1, k], [2, 2, 1, 2]][k - 1]
            totals = [arrived(n) for n in range(k + 1)]
            up = (pick(z, [totals[n] for n in up_from]) + sent_up.astype(F32)).astype(low)
            down = (pick(z, [totals[n] for n in down_from]) + sent_down.astype(F32)).astype(low)
    return joined[3] + [sent_up, sent_down], tails[3]


def loop(count, body, together=1):
    together = math.gcd(count, together)

    def step(i, carry):
        for part in range(together):
            body(i * together + part)
        return carry

    lax.fori_loop(0, count // together, step, 0)


def at(i, size):
    if isinstance(i, int):
        return pl.ds(i * size, size)
    return pl.ds(pl.multiple_of(i * size, size), size)


def block_at(start, size):
    if isinstance(start, int):
        return pl.ds(start, size)
    return pl.ds(pl.multiple_of(start, 256), size)


WINDOW = 12 * 2**20


class Queue:
    def __init__(self, copies, sizes, order):
        self.copies, self.sizes, self.waiting = dict(copies), sizes, list(order)
        self.running, self.asked = [], []
        self.fill()

    def fill(self):
        while self.waiting:
            ahead = sum([self.sizes[name] for name in self.running])
            if self.running and ahead + self.sizes[self.waiting[0]] > WINDOW:
                return
            name = self.waiting.pop(0)
            self.copies[name].start()
            self.running.append(name)

    def get(self, name):
        if name not in self.copies:
            return
        self.asked.append(name)
        if name in self.waiting:
            self.waiting.remove(name)
            self.copies[name].start()
        else:
            self.running.remove(name)
        self.copies.pop(name).wait()
        self.fill()


class Kernel:
    def __init__(self, table, weight_ref, queue, refs, outgoing):
        self.table, self.w, self.queue, self.refs = table, weight_ref, queue, refs
        self.outgoing, self.sent = outgoing, []

    def __getitem__(self, name):
        self.queue.get(name)
        return self.refs[name]

    def need(self, name):
        self.queue.get(name)

    def put(self, *names):
        for name in names:
            copy = self.outgoing.pop(name)
            copy.start()
            self.sent.append(copy)

    def columns(self, name, first, blocks):
        self.need(name)
        offset, height, unused = self.table.weights[name]
        parts = [
            self.w[block_at(offset + (first + i) * height, height), :]
            for i in range(blocks)
        ]
        return jnp.concatenate(parts, axis=1)

    def strip(self, name, first, rows, low=0):
        self.need(name)
        offset, height, blocks = self.table.weights[name]
        parts = [
            self.w[block_at(offset + j * height + low + first * rows, rows), :]
            for j in range(blocks)
        ]
        return jnp.concatenate(parts, axis=1)

    def row(self, name, j, blocks=1):
        offset, unused = self.table.vectors[name]
        parts = [self.refs[N.vectors][pl.ds(offset + j + i, 1), :] for i in range(blocks)]
        return parts[0] if blocks == 1 else jnp.concatenate(parts, axis=1)

    def add_rows(self, name, j, value):
        offset, unused = self.table.vectors[name]
        blocks = value.shape[1] // LANES
        for i in range(blocks):
            part = value[:, i * LANES : (i + 1) * LANES]
            part = part.reshape(part.shape[0] // 8, 8, LANES).sum(axis=0)
            place = at(offset + j + i, 8)
            self.refs[N.vector_sums][place, :] += part


def fused(body, table, weight_array, weight_names, ins, outs, blanks, temps):
    in_names, out_names, blank_names = list(ins), list(outs), list(blanks)
    temp_names = list(temps)
    copies_in = in_names + list(weight_names)
    total = len(copies_in) + len(out_names)
    sizes = {n: math.prod(ins[n].shape) * ins[n].dtype.itemsize for n in in_names}
    sizes |= {n: table.heights[n] * LANES * 2 for n in weight_names}

    def call(order, asked):
        def kernel(*refs):
            refs = list(refs)
            weight_hbm = refs.pop(0)
            in_hbm = {n: refs.pop(0) for n in in_names}
            out_hbm = {n: refs.pop(0) for n in out_names}
            for unused in blank_names:
                refs.pop(0)
            weight_vmem = refs.pop(0)
            vmem = {n: refs.pop(0) for n in in_names + out_names + temp_names}
            sems = refs.pop(0)
            copies = {}
            for at_sem, name in enumerate(copies_in):
                if name in table.weights:
                    offset, height, blocks = table.weights[name]
                    place = pl.ds(offset, height * blocks)
                    pair = (weight_hbm.at[place], weight_vmem.at[place])
                else:
                    pair = (in_hbm[name], vmem[name])
                copies[name] = pltpu.make_async_copy(pair[0], pair[1], sems.at[at_sem])
            outgoing = {
                name: pltpu.make_async_copy(vmem[name], out_hbm[name], sems.at[len(copies_in) + i])
                for i, name in enumerate(out_names)
            }
            queue = Queue(copies, sizes, order)
            k = Kernel(table, weight_vmem, queue, vmem, outgoing)
            body(k)
            for name in copies_in:
                queue.get(name)
            for name in list(outgoing):
                k.put(name)
            for copy in k.sent:
                copy.wait()
            asked[:] = queue.asked

        any_spec = pl.BlockSpec(memory_space=pl.ANY)
        return pl.pallas_call(
            kernel,
            out_shape=[outs[n] for n in out_names] + [blanks[n] for n in blank_names],
            in_specs=[any_spec] * (1 + len(in_names)),
            out_specs=[any_spec] * (len(out_names) + len(blank_names)),
            scratch_shapes=[pltpu.VMEM((weight_rows_used(table, weight_names), LANES), BF)]
            + [pltpu.VMEM(ins[n].shape, ins[n].dtype) for n in in_names]
            + [pltpu.VMEM(outs[n].shape, outs[n].dtype) for n in out_names]
            + [pltpu.VMEM(*temps[n]) for n in temp_names]
            + [pltpu.SemaphoreType.DMA((total,))],
            compiler_params=pltpu.CompilerParams(vmem_limit_bytes=62 * 2**20),
        )

    given = [weight_array] + [ins[n] for n in in_names]
    asked = []
    jax.eval_shape(call(copies_in, asked), *given)
    result = call(list(asked), [])(*given)
    return dict(zip(out_names + blank_names, result))


def weight_rows_used(table, names):
    return max(table.weights[n][0] + table.heights[n] for n in names)


def dot(left, right):
    return jnp.dot(left, right, preferred_element_type=F32)


def dot_t(left, right):
    return lax.dot_general(left, right, (((1,), (1,)), ((), ())), preferred_element_type=F32)


def blocks_of(width):
    return range(width // LANES)


def lanes(j):
    return slice(j * LANES, (j + 1) * LANES)


def normalize(k, read, norm, width, size, block, write):
    def body(i):
        rows = at(i, block)
        values = [read(rows, j) for j in blocks_of(width)]
        mean = jnp.sum(sum(values), axis=1, keepdims=True) * (1.0 / width)
        values = [v - mean for v in values]
        var = jnp.sum(sum([v * v for v in values]), axis=1, keepdims=True) * (1.0 / width)
        r = lax.rsqrt(var + epsilon)
        for j in blocks_of(width):
            z = values[j] * r
            write(rows, j, z, z * k.row(norm + N._gain, j) + k.row(norm + N._bias, j), r)

    loop(size // block, body, 4)


def norm_gradient(k, norm, width, zs, douts, r):
    dzs = []
    for j in blocks_of(width):
        k.add_rows(norm + N._gain, j, douts[j] * zs[j])
        k.add_rows(norm + N._bias, j, douts[j])
        dzs.append(douts[j] * k.row(norm + N._gain, j))
    first = jnp.sum(sum(dzs), axis=1, keepdims=True) * (1.0 / width)
    second = jnp.sum(sum([a * b for a, b in zip(dzs, zs)]), axis=1, keepdims=True) * (1.0 / width)
    return [(dz - first - z * second) * r for dz, z in zip(dzs, zs)]


GELU_A = math.sqrt(2.0 / math.pi)
GELU_B = GELU_A * 0.044715


def gelu_both(x):
    square = x * x
    half = 0.5 + 0.5 * jnp.tanh(x * (GELU_A + GELU_B * square))
    value = x * half
    slope = half + 2.0 * value * (1.0 - half) * (GELU_A + 3.0 * GELU_B * square)
    return value, slope


def sigmoid(x):
    return 0.5 + 0.5 * jnp.tanh(0.5 * x)


def silu_both(x):
    s = sigmoid(x)
    value = x * s
    return value, s + value * (1.0 - s)


def head_mask(h, size):
    lane = lax.broadcasted_iota(jnp.int32, (1, LANES), 1)
    return ((lane >= h * size) & (lane < (h + 1) * size)).astype(BF)


class Group:
    def __init__(self, index, **refs):
        groups = D // LANES
        pack, column = index // groups, lax.rem(index, groups)
        self.index, self.pack = index, pack
        self.rows, self.cols = at(pack, PACK), at(column, LANES)
        for name, ref in refs.items():
            setattr(self, name, ref[self.rows, self.cols])


def in_turn(count, stages):
    for k in range(count + max(delay for unused, delay in stages)):
        for stage, delay in stages:
            if 0 <= k - delay < count:
                stage(k - delay)


def attend(q, key, value, caps, probs, out, heads, tokens):
    size = D // heads
    per = LANES // size
    scale = size ** (-0.5) * math.log2(math.e)
    together = 4
    halves = [slice(0, LANES), slice(LANES, PACK)]

    def body(step):
        groups, scores, weights, parts = {}, {}, {}, {}

        def score(i):
            g, h = divmod(i, per)
            if h == 0:
                groups[g] = Group(step * together + g, q=q, key=key, value=value)
                groups[g].value = groups[g].value.T
                parts[g] = []
            masked = groups[g].key * head_mask(h, size)
            scores[i] = [dot_t(masked, groups[g].q[half]) for half in halves]

        def soften(i):
            g, h = divmod(i, per)
            done = []
            for half, s in zip(halves, scores.pop(i)):
                s = jnp.minimum(s * scale, caps[groups[g].pack, :, half])
                e = jnp.exp2(s - jnp.max(s, axis=0, keepdims=True))
                done.append((e * (1.0 / jnp.sum(e, axis=0, keepdims=True))).astype(BF))
            weights[i] = jnp.concatenate(done, axis=1)
            probs[at(groups[g].index * per + h, PACK), :] = weights[i]

        def collect(i):
            g, h = divmod(i, per)
            group = groups[g]
            parts[g].append(dot(group.value[h * size : (h + 1) * size], weights.pop(i)))
            if h == per - 1:
                out[group.rows, group.cols] = jnp.concatenate(parts[g], axis=0).T.astype(BF)

        in_turn(together * per, [(score, 0), (soften, 2), (collect, 3)])

    loop((tokens // PACK) * (D // LANES) // together, body)


def attend_back(q, key, value, probs, dout, dq, dkey, dvalue, heads, tokens, together=4):
    size = D // heads
    per = LANES // size
    scale = size ** (-0.5)
    masks = [head_mask(h, size) for h in range(per)]

    def body(step):
        groups, grads, weights, moved, parts = {}, {}, {}, {}, {}

        def first(i):
            g, h = divmod(i, per)
            if h == 0:
                groups[g] = Group(
                    step * together + g, q=q, key=key, value=value, dout=dout
                )
                groups[g].key = groups[g].key.T
                weights[g], moved[g], parts[g] = [], [], []
            grads[i] = dot_t(groups[g].value * masks[h], groups[g].dout)

        def soften(i):
            g, h = divmod(i, per)
            dp = grads.pop(i)
            low = probs[at(groups[g].index * per + h, PACK), :]
            wide = low.astype(F32)
            mean = jnp.sum(wide * dp, axis=0, keepdims=True)
            mean = mean / jnp.sum(wide, axis=0, keepdims=True)
            weights[g].append(low)
            moved[g].append((wide * (dp - mean)).astype(BF))

        def collect(i):
            g, h = divmod(i, per)
            group = groups[g]
            parts[g].append(dot(group.key[h * size : (h + 1) * size], moved[g][h]))
            if h == per - 1:
                douts = jnp.concatenate([group.dout * mask for mask in masks], axis=0)
                queries = jnp.concatenate([group.q * mask for mask in masks], axis=0)
                place = (group.rows, group.cols)
                dvalue[place] = dot(jnp.concatenate(weights[g], axis=1), douts).astype(BF)
                dkey[place] = (dot(jnp.concatenate(moved[g], axis=1), queries) * scale).astype(BF)
                dq[place] = (jnp.concatenate(parts[g], axis=0).T * scale).astype(BF)

        in_turn(together * per, [(first, 0), (soften, 2), (collect, 3)])

    loop((tokens // PACK) * (D // LANES) // together, body)


def chunks(count, product, finish):
    held = {}

    def ask(j):
        held[j] = product(j)

    in_turn(count, [(ask, 0), (lambda j: finish(j, held.pop(j)), 1)])


def project(k, name, x, out):
    def finish(j, total):
        out[:, at(j, 256)] = total.astype(BF)

    chunks(out.shape[1] // 256, lambda j: dot(x[...], k.columns(name, 2 * j, 2)), finish)


def project_back(k, terms, write, height, low=0):
    def product(j):
        return sum([dot_t(dout[...], k.strip(name, j, 256, low)) for name, dout in terms])

    chunks(height // 256, product, write)


def same_segment(segments, base, block, moves):
    here = segments[pl.ds(base + EDGE, block), :]
    return {
        move: jnp.where(segments[pl.ds(base + (EDGE + move), block), :] == here, 1.0, 0.0)
        for move in moves
        if move
    }


def masked(ref, base, block, j, move, held):
    value = ref.load(base + move, block, j)
    return value * held[move] if move else value


def taps_forward(k, name, moves, source, segments, out, width, size):
    block = 16

    def body(i):
        base = pl.multiple_of(i * block, block)
        held = same_segment(segments, base, block, moves)
        for j in blocks_of(width):
            total = jnp.zeros((block, LANES), F32)
            for tap, move in enumerate(moves):
                value = masked(source, base, block, j, move, held)
                total = total + value * k.row(name, tap * (width // LANES) + j)
            out[pl.ds(base, block), lanes(j)] = total.astype(out.dtype)

    loop(size // block, body, 2)


def taps_back(k, terms, center, segments, width, size, write):
    block = 32

    def body(i):
        base = pl.multiple_of(i * block, block)
        rows = pl.ds(base, block)
        held = same_segment(
            segments, base, block, sorted({-move for term in terms for move in term[1]})
        )
        for j in blocks_of(width):
            total = jnp.zeros((block, LANES), F32)
            here = center(rows, j)
            for name, moves, dout in terms:
                for tap, move in enumerate(moves):
                    entry = tap * (width // LANES) + j
                    value = masked(dout, base, block, j, -move, held)
                    total = total + value * k.row(name, entry)
                    k.add_rows(name, entry, value * here)
            write(rows, j, total)

    loop(size // block, body)


class Edged:
    def __init__(self, ref, size):
        self.ref, self.size, self.height = ref, size, size + 2 * EDGE
        for j in range(ref.shape[0] // self.height):
            for start in (0, size + EDGE):
                ref[pl.ds(j * self.height + start, EDGE), :] = jnp.zeros((EDGE, LANES), F32)

    def part(self, first, blocks):
        place = pl.ds(first * self.height, blocks * self.height)
        return Edged(self.ref.at[place], self.size)

    def place(self, start, rows, j):
        return pl.ds(start + (j * self.height + EDGE), rows)

    def load(self, start, rows, j):
        return self.ref[self.place(start, rows, j), :]

    def store(self, start, rows, j, value):
        self.ref[self.place(start, rows, j), :] = value

    def store_wide(self, j, value, add=False):
        for half in range(2):
            place = pl.ds((2 * j + half) * self.height + EDGE, self.size)
            if add:
                self.ref[place, :] += value[:, lanes(half)]
            else:
                self.ref[place, :] = value[:, lanes(half)]


def moves_of(count, first):
    return [first + i for i in range(count)]


def lay_out(table, sources, starts, piece_rows, devices):
    slots = 8
    count = devices.shape[0]
    heights = [end - start for start, end in zip(starts, starts[1:] + [piece_rows])]
    arrays = []
    for items in sources:
        for array, unused in items:
            if not any(array is other for other in arrays):
                arrays.append(array)

    def spot(array):
        return [array is other for other in arrays].index(True)

    pieces = [
        (a, j, spot(items[j][0]), items[j][1])
        for j in range(count)
        for a, items in enumerate(sources)
    ]

    def kernel(*refs):
        refs = list(refs)
        device = refs.pop(0)
        held = [refs.pop(0) for unused in arrays]
        weight_hbm, vector_hbm, ring, stream, stage, vector_stage, in_sems, out_sems = refs

        def fetch(step):
            a, unused, which, lead = pieces[step]
            rows = pl.ds(0, up_to(heights[a], 16))
            source = held[which] if lead is None else held[which].at[lead]
            place = ring.at[step % slots, rows]
            return pltpu.make_async_copy(source.at[rows], place, in_sems.at[step % slots])

        for step in range(min(slots, len(pieces))):
            fetch(step).start()
        for step, (a, j, unused, unused_too) in enumerate(pieces):
            fetch(step).wait()
            base = device[j] * piece_rows + starts[a]
            whole, rest = heights[a] // 256, heights[a] % 256

            def body(i, base=base, step=step):
                stream[pl.ds(base + i * 256, 256), :] = ring[step % slots, at(i, 256), :].astype(F32)

            if whole:
                loop(whole, body)
            if rest:
                padded = up_to(rest, 16)
                value = ring[step % slots, whole * 256 : whole * 256 + padded, :].astype(F32)
                stream[pl.ds(base + whole * 256, rest), :] = value[:rest]
            if step + slots < len(pieces):
                fetch(step + slots).start()
        copies = []
        for at_sem, (name, (offset, height, blocks)) in enumerate(table.weights.items()):
            start = table.at[name]
            per = height // 512

            def body(i, offset=offset, height=height, blocks=blocks, start=start, per=per):
                j, part = i // per, lax.rem(i, per)
                taken = stream[pl.ds(start + part * (512 * blocks) + j, 512, stride=blocks), :]
                stage[block_at(offset + j * height + part * 512, 512), :] = taken.astype(BF)

            loop(blocks * per, body, 4)
            place = pl.ds(offset, height * blocks)
            copies.append(
                pltpu.make_async_copy(stage.at[place], weight_hbm.at[place], out_sems.at[at_sem])
            )
            copies[-1].start()
        for name, (offset, rows) in table.vectors.items():
            vector_stage[offset : offset + rows, :] = stream[pl.ds(table.at[name], rows), :]
        copies.append(
            pltpu.make_async_copy(vector_stage, vector_hbm, out_sems.at[len(table.weights)])
        )
        copies[-1].start()
        for copy in copies:
            copy.wait()

    any_spec = pl.BlockSpec(memory_space=pl.ANY)
    return tuple(
        pl.pallas_call(
            kernel,
            out_shape=[
                jax.ShapeDtypeStruct((WEIGHT_ROWS, LANES), BF),
                jax.ShapeDtypeStruct((VECTOR_ROWS, LANES), F32),
            ],
            in_specs=[pl.BlockSpec(memory_space=pltpu.SMEM)] + [any_spec] * len(arrays),
            out_specs=[any_spec] * 2,
            scratch_shapes=[
                pltpu.VMEM((slots, up_to(max(heights), 16), LANES), BF),
                pltpu.VMEM((up_to(count * piece_rows, 8) + 64, LANES), F32),
                pltpu.VMEM((WEIGHT_ROWS, LANES), BF),
                pltpu.VMEM((VECTOR_ROWS, LANES), F32),
                pltpu.SemaphoreType.DMA((slots,)),
                pltpu.SemaphoreType.DMA((len(table.weights) + 1,)),
            ],
            compiler_params=pltpu.CompilerParams(vmem_limit_bytes=62 * 2**20),
        )(devices, *arrays)
    )


def weight_gradients(table, products, arrays, sums, shapes, targets, starts, piece_rows, devices, compact, into=(), active=None):
    count = devices.shape[0]
    heights = [end - start for start, end in zip(starts, starts[1:] + [piece_rows])]
    widths = [shapes[items[0][0]].shape[-2] for items in targets]
    names = list(arrays)
    slots = 4
    size = next(iter(arrays.values())).shape[0]
    widest = max(arrays[x].shape[1] for unused, x, unused_too in products)

    def kernel(*refs):
        if active is None:
            return inside(*refs)

        @pl.when(refs[1][0] == 1)
        def run():
            inside(refs[0], *refs[2:])

    def inside(*refs):
        refs = list(refs)
        device = refs.pop(0)
        hbm = [refs.pop(0) for unused in names + sums]
        for unused in into:
            refs.pop(0)
        out_hbm = [refs.pop(0) for unused in shapes]
        vmem = [refs.pop(0) for unused in names + sums]
        turned, stream, ring, in_sems, out_sems = refs
        wanted = []
        for unused, x, dout in products:
            wanted += [x, dout]
        wanted = list(dict.fromkeys(wanted)) + list(range(len(sums)))
        spot = {n: i for i, n in enumerate(names)} | {i: len(names) + i for i in range(len(sums))}
        copies = {
            n: pltpu.make_async_copy(hbm[spot[n]], vmem[spot[n]], in_sems.at[spot[n]]) for n in wanted
        }
        sizes = {n: math.prod(given[spot[n]].shape) * given[spot[n]].dtype.itemsize for n in wanted}
        queue = Queue(copies, sizes, wanted)

        def get(name):
            queue.get(name)
            return vmem[spot[name]]

        last = None
        for name, x_name, dout_name in products:
            unused, height, blocks = table.weights[name]
            start = table.at[name]
            x, dout = get(x_name), get(dout_name)
            if x_name != last:
                last = x_name

                def turn(j, x=x):
                    turned[at(j, 256), :] = x[:, at(j, 256)].T

                loop(height // 256, turn, 2)
            per = height // 512

            def product(i):
                j, part = i // per, i % per
                return dot(turned[at(part, 512), :], dout[:, at(j, 256)])

            def finish(i, total):
                j, part = i // per, i % per
                base = start + part * (512 * blocks) + 2 * j
                for half in range(2):
                    stream[pl.ds(base + half, 512, stride=blocks), :] = total[:, lanes(half)]

            steps = (blocks // 2) * per
            if compact and steps > 2 and steps % 2 == 0:
                pair = lambda i: chunks(2, lambda n: product(2 * i + n), lambda n, t: finish(2 * i + n, t))
                loop(steps // 2, pair)
            else:
                chunks(steps, product, finish)
        parts = [get(i) for i in range(len(sums))]
        for name, (offset, rows) in table.vectors.items():
            total = None
            for part in parts:
                for s in range(8):
                    value = part[pl.ds(offset * 8 + s, rows, stride=8), :]
                    total = value if total is None else total + value
            stream[pl.ds(table.at[name], rows), :] = total
        if table.rows < count * piece_rows:
            stream[pl.ds(table.rows, count * piece_rows - table.rows), :] = jnp.zeros(
                (count * piece_rows - table.rows, LANES), F32
            )
        sent = []
        if len(starts) == 1:
            gap = up_to(heights[0], 16)
            for slot in range(slots):
                ring[slot, gap : widths[0], :] = jnp.zeros((widths[0] - gap, LANES), BF)
        pieces = [(a, j) for j in range(count) for a in range(len(starts))]
        for step, (a, j) in enumerate(pieces):
            slot = step % slots
            base = device[j] * piece_rows + starts[a]
            if step >= slots:
                sent[step - slots].wait()
            height = up_to(heights[a], 16)
            whole, rest = height // 256, height % 256

            def body(i, base=base, slot=slot):
                ring[slot, at(i, 256), :] = stream[pl.ds(base + i * 256, 256), :].astype(BF)

            if whole:
                loop(whole, body)
            if rest:
                ring[slot, whole * 256 : whole * 256 + rest, :] = stream[
                    pl.ds(base + whole * 256, rest), :
                ].astype(BF)
            which, lead = targets[a][j]
            target = out_hbm[which] if lead is None else out_hbm[which].at[lead]
            sent.append(
                pltpu.make_async_copy(
                    ring.at[slot, pl.ds(0, widths[a])], target, out_sems.at[slot]
                )
            )
            sent[-1].start()
        for copy in sent[-slots:]:
            copy.wait()

    any_spec = pl.BlockSpec(memory_space=pl.ANY)
    given = [arrays[n] for n in names] + sums
    scalars = [devices]
    if active is not None:
        scalars.append(active.astype(jnp.int32).reshape(1))
    return tuple(
        pl.pallas_call(
            kernel,
            out_shape=list(shapes),
            in_specs=[pl.BlockSpec(memory_space=pltpu.SMEM)] * len(scalars)
            + [any_spec] * (len(given) + len(into)),
            input_output_aliases={len(scalars) + len(given) + n: n for n in range(len(into))},
            out_specs=[any_spec] * len(shapes),
            scratch_shapes=[pltpu.VMEM(a.shape, a.dtype) for a in given]
            + [
                pltpu.VMEM((widest, size), BF),
                pltpu.VMEM((up_to(count * piece_rows, 8) + 64, LANES), F32),
                pltpu.VMEM((slots, max(widths), LANES), BF),
                pltpu.SemaphoreType.DMA((len(given),)),
                pltpu.SemaphoreType.DMA((slots,)),
            ],
            compiler_params=pltpu.CompilerParams(vmem_limit_bytes=63 * 2**20),
        )(*scalars, *given, *into)
    )


def add_up(parts, tail, start, size):
    block = 512
    height = parts[0].shape[0]

    def kernel(*refs):
        refs = list(refs)
        held = [refs.pop(0) for unused in parts]
        tail_ref, out_hbm, stage, sem = refs
        for first in range(0, height, block):
            rows = slice(first, min(first + block, height))
            stage[rows, :] = sum([p[rows, :].astype(F32) for p in held])
        stage[start:size, :] += tail_ref[...].astype(F32)[: size - start]
        copy = pltpu.make_async_copy(stage.at[pl.ds(0, size)], out_hbm.at[:, 0, :], sem)
        copy.start()
        copy.wait()

    return pl.pallas_call(
        kernel,
        out_shape=jax.ShapeDtypeStruct((size, 1, LANES), F32),
        in_specs=[pl.BlockSpec(memory_space=pltpu.VMEM)] * (len(parts) + 1),
        out_specs=pl.BlockSpec(memory_space=pl.ANY),
        scratch_shapes=[pltpu.VMEM((height, LANES), F32), pltpu.SemaphoreType.DMA],
        compiler_params=pltpu.CompilerParams(vmem_limit_bytes=32 * 2**20),
    )(*parts, tail)


def keeping(k, norm, write_out):
    z_ref, r_ref = k[N.z_ + norm], k[N.r_ + norm]

    def write(rows, j, z, out, r):
        z_ref[rows, lanes(j)] = z.astype(BF)
        if j == 0:
            r_ref[rows, :] = jnp.broadcast_to(r, (rows.size, LANES))
        write_out(rows, j, out)

    return write


def to_low(ref):
    def write(rows, j, out):
        ref[rows, lanes(j)] = out.astype(BF)

    return write


def rows_of(ref):
    return lambda rows, j: ref[rows, lanes(j)].astype(F32)


def encoder_forward(k):
    vectors, x0 = k[N.vectors], k[N.tokens]
    size = x0.shape[0]
    h1, x1, glu_a, glu_s = k[N.h1], k[N.x1], k[N.glu_a], k[N.glu_s]
    normalize(k, rows_of(x0), N.norm_glu, D, size, 64, keeping(k, N.norm_glu, to_low(h1)))
    k.put(N.h1)
    def both(j):
        return [dot(h1[...], k.columns(N.glu_weight, c, 2)) for c in (2 * j, 4 + 2 * j)]

    def gate(j, totals):
        a = totals[0] + k.row(N.glu_bias, 2 * j, 2)
        s = sigmoid(totals[1] + k.row(N.glu_bias, 4 + 2 * j, 2))
        cols = at(j, 256)
        glu_a[:, cols] = a.astype(BF)
        glu_s[:, cols] = s.astype(BF)
        x1[:, cols] = x0[:, cols].astype(F32) + a * s

    chunks(2, both, gate)
    k.put(N.glu_a, N.glu_s)
    h2, stacked, mask = k[N.h2], k[N.stacked], k[N.mask]
    edged = Edged(k[N.edged], size)

    def keep_h2(rows, j, out):
        low = out.astype(BF)
        h2[rows, lanes(j)] = low
        stacked[rows, lanes(j + 4)] = low
        edged.store(rows.start, rows.size, j, low.astype(F32))

    normalize(k, rows_of(x1), N.norm_conv, D, size, 64, keeping(k, N.norm_conv, keep_h2))

    def stack(i):
        base = pl.multiple_of(i * 32, 32)
        held = same_segment(mask, base, 32, (-1, 1))
        for first, move in ((0, -1), (8, 1)):
            for j in blocks_of(D):
                value = masked(edged, base, 32, j, move, held)
                stacked[pl.ds(base, 32), lanes(first + j)] = value.astype(BF)

    loop(size // 32, stack, 4)
    k.put(N.h2, N.stacked)
    mixed = Edged(k[N.mixed], size)
    slope_left, slope_right = k[N.slope_left], k[N.slope_right]
    def left(j):
        if j == FF // 256:
            return dot(stacked[...], k.columns(N.right_weight, 0, 2))
        return dot(h2[...], k.columns(N.left_weight, 2 * j, 2))

    def keep_left(j, total):
        if j == FF // 256:
            value, slope = gelu_both(total + k.row(N.right_bias, 0, 2))
            mixed.store_wide(0, value, True)
            slope_right[...] = slope.astype(BF)
            return
        value, slope = gelu_both(total + k.row(N.left_bias, 2 * j, 2))
        mixed.store_wide(j, value)
        slope_left[:, at(j, 256)] = slope.astype(BF)

    chunks(FF // 256 + 1, left, keep_left)
    k.put(N.slope_left, N.slope_right)
    z_middle, r_middle, spread = k[N.z_middle], k[N.r_middle], k[N.spread]

    def keep_middle(rows, j, z, out, r):
        z_middle[rows, lanes(j)] = z.astype(BF)
        mixed.store(rows.start, rows.size, j, out)
        if j == 0:
            r_middle[rows, :] = jnp.broadcast_to(r, (rows.size, LANES))

    normalize(
        k, lambda rows, j: mixed.load(rows.start, rows.size, j), N.middle, FF, size, 16, keep_middle
    )
    k.put(N.z_middle, N.r_middle)
    taps_forward(k, N.depth_taps, moves_of(9, -4), mixed, mask, spread, FF, size)
    k.put(N.spread)
    x2 = k[N.x2]
    x2[:, 0:256] = (
        x1[:, 0:256]
        + dot(spread[...], k.columns(N.point_weight, 0, 2))
        + k.row(N.point_bias, 0, 2)
    )
    x2[:, 256:512] = x1[:, 256:512]
    h3, q, key, value = k[N.h3], k[N.q], k[N.key], k[N.value]
    normalize(k, rows_of(x2), N.norm_attn, D, size, 64, keeping(k, N.norm_attn, to_low(h3)))
    project(k, N.attn_query, h3, q)
    project(k, N.attn_key, h3, key)
    project(k, N.attn_value, h3, value)
    k.put(N.h3, N.q, N.key, N.value)
    attend(q, key, value, k[N.caps], k[N.probs], k[N.heads], HEADS, size)
    heads, x3, h4, inner, slope_feed = k[N.heads], k[N.x3], k[N.h4], k[N.inner], k[N.slope_feed]
    k.put(N.probs, N.heads)
    add_product(k, N.attn_output, heads, x2, x3)
    normalize(k, rows_of(x3), N.norm_feed, D, size, 64, keeping(k, N.norm_feed, to_low(h4)))
    feed_in(k, h4, inner, slope_feed, gelu_both)
    k.put(N.h4, N.inner, N.slope_feed)
    feed_out(k, inner, x3, k[N.memory])


def add_product(k, name, x, base, out):
    def finish(j, total):
        cols = at(j, 256)
        out[:, cols] = base[:, cols] + total

    chunks(D // 256, lambda j: dot(x[...], k.columns(name, 2 * j, 2)), finish)


def feed_in(k, h, inner, slopes, both):
    def finish(j, total):
        value, slope = both(total + k.row(N.feed_in_bias, 2 * j, 2))
        inner[:, at(j, 256)] = value.astype(BF)
        slopes[:, at(j, 256)] = slope.astype(BF)

    chunks(FF // 256, lambda j: dot(h[...], k.columns(N.feed_in_weight, 2 * j, 2)), finish)


def feed_out(k, inner, base, out):
    def finish(j, total):
        cols = at(j, 256)
        out[:, cols] = (base[:, cols] + total + k.row(N.feed_out_bias, 2 * j, 2)).astype(BF)

    chunks(D // 256, lambda j: dot(inner[...], k.columns(N.feed_out_weight, 2 * j, 2)), finish)


def add_all_rows(k, name, ref, width):
    def body(i):
        for j in blocks_of(width):
            k.add_rows(name, j, ref[at(i, 64), lanes(j)].astype(F32))

    loop(ref.shape[0] // 64, body, 4)


def feed_back(k, dout_low, slopes, dpre, dh):
    def finish(j, total):
        grad = total * slopes[:, at(j, 256)].astype(F32)
        k.add_rows(N.feed_in_bias, 2 * j, grad)
        dpre[:, at(j, 256)] = grad.astype(BF)

    chunks(FF // 256, lambda j: dot_t(dout_low[...], k.strip(N.feed_out_weight, j, 256)), finish)

    def write(j, total):
        dh[:, at(j, 256)] = total

    project_back(k, [(N.feed_in_weight, dpre)], write, D)


def add_norm_back(k, norm, size, dh, base, out, low=None):
    z, r = k[N.z_ + norm], k[N.r_ + norm]

    def body(i):
        rows = at(i, 32)
        zs = [z[rows, lanes(j)].astype(F32) for j in blocks_of(D)]
        douts = [dh[rows, lanes(j)] for j in blocks_of(D)]
        grads = norm_gradient(k, norm, D, zs, douts, r[rows, :])
        for j in blocks_of(D):
            total = base(rows, j) + grads[j]
            out[rows, lanes(j)] = total
            if low is not None:
                low[rows, lanes(j)] = total.astype(BF)

    loop(size // 32, body, 4)


def output_of(k, norm):
    z = k[N.z_ + norm]

    def read(rows, j):
        value = z[rows, lanes(j)].astype(F32) * k.row(norm + N._gain, j)
        return value + k.row(norm + N._bias, j)

    return read


def encoder_back(k):
    k[N.vectors]
    dmem = k[N.returned]
    size = dmem.shape[0]
    sums = k[N.vector_sums]
    sums[...] = jnp.zeros(sums.shape, F32)
    dpre, dh, dx = k[N.dpre_feed], k[N.dh], k[N.dx]
    add_all_rows(k, N.feed_out_bias, dmem, D)
    feed_back(k, dmem, k[N.slope_feed], dpre, dh)
    k.put(N.dpre_feed)
    d3 = k[N.d3]
    add_norm_back(k, N.norm_feed, size, dh, rows_of(dmem), dx, d3)
    k.put(N.d3)

    dheads = k[N.dheads]

    def write_heads(j, total):
        dheads[:, at(j, 256)] = total.astype(BF)

    project_back(k, [(N.attn_output, d3)], write_heads, D)
    dq, dkey, dvalue = k[N.dq], k[N.dkey], k[N.dvalue]
    attend_back(
        k[N.q], k[N.key], k[N.value], k[N.probs], dheads, dq, dkey, dvalue, HEADS, size
    )
    k.put(N.dq, N.dkey, N.dvalue)
    def write_dh(j, total):
        dh[:, at(j, 256)] = total

    project_back(
        k, [(N.attn_query, dq), (N.attn_key, dkey), (N.attn_value, dvalue)], write_dh, D
    )
    add_norm_back(k, N.norm_attn, size, dh, rows_of(dx), dx)
    d2, mask = k[N.d2], k[N.mask]
    dspread = Edged(k[N.dspread], size)
    d2[...] = dx[:, 0:256].astype(BF)
    k.put(N.d2)
    add_all_rows(k, N.point_bias, dx.at[:, 0:256], 256)

    def write_spread(j, total):
        dspread.store_wide(j, total)

    project_back(k, [(N.point_weight, d2)], write_spread, FF)
    z_middle, r_middle = k[N.z_middle], k[N.r_middle]

    dmiddle = k[N.dmiddle]

    def write_middle(rows, j, total):
        dmiddle[rows, lanes(j)] = total
    taps_back(
        k, [(N.depth_taps, moves_of(9, -4), dspread)], output_of(k, N.middle), mask, FF, size, write_middle
    )
    slope_left, slope_right = k[N.slope_left], k[N.slope_right]
    dleft, dright = k[N.dleft], k[N.dright]

    def middle(i):
        rows = at(i, 16)
        zs = [z_middle[rows, lanes(j)].astype(F32) for j in blocks_of(FF)]
        douts = [dmiddle[rows, lanes(j)] for j in blocks_of(FF)]
        grads = norm_gradient(k, N.middle, FF, zs, douts, r_middle[rows, :])
        for j in blocks_of(FF):
            grad = grads[j] * slope_left[rows, lanes(j)].astype(F32)
            k.add_rows(N.left_bias, j, grad)
            dleft[rows, lanes(j)] = grad.astype(BF)
        for j in range(2):
            grad = grads[j] * slope_right[rows, lanes(j)].astype(F32)
            k.add_rows(N.right_bias, j, grad)
            dright[rows, lanes(j)] = grad.astype(BF)

    loop(size // 16, middle, 4)
    k.put(N.dleft, N.dright)
    edged, edged_too = dspread.part(0, 4), dspread.part(4, 4)

    def write_before(j, total):
        edged.store_wide(j, total)

    def write_after(j, total):
        edged_too.store_wide(j, total)

    project_back(k, [(N.right_weight, dright)], write_before, D, 0)
    project_back(k, [(N.right_weight, dright)], write_after, D, 2 * D)
    def conv(j):
        total = dot_t(dleft[...], k.strip(N.left_weight, j, 256))
        return total + dot_t(dright[...], k.strip(N.right_weight, j, 256, D))

    chunks(D // 256, conv, write_dh)

    def untap(i):
        base = pl.multiple_of(i * 32, 32)
        held = same_segment(mask, base, 32, (-1, 1))
        for j in blocks_of(D):
            dh[pl.ds(base, 32), lanes(j)] += masked(edged, base, 32, j, 1, held) + masked(
                edged_too, base, 32, j, -1, held
            )

    loop(size // 32, untap, 4)
    add_norm_back(k, N.norm_conv, size, dh, rows_of(dx), dx)
    glu_a, glu_s, dglu = k[N.glu_a], k[N.glu_s], k[N.dglu]

    def gate(i):
        rows = at(i, 32)
        for j in blocks_of(D):
            a, s = glu_a[rows, lanes(j)].astype(F32), glu_s[rows, lanes(j)].astype(F32)
            d = dx[rows, lanes(j)]
            da = d * s
            dg = da * a * (1.0 - s)
            k.add_rows(N.glu_bias, j, da)
            k.add_rows(N.glu_bias, 4 + j, dg)
            dglu[rows, lanes(j)] = da.astype(BF)
            dglu[rows, lanes(4 + j)] = dg.astype(BF)

    loop(size // 32, gate, 4)
    k.put(N.dglu)
    project_back(k, [(N.glu_weight, dglu)], write_dh, D)
    add_norm_back(k, N.norm_glu, size, dh, rows_of(dx), k[N.token_grad])


def decoder_start(k):
    k[N.vectors]
    y0, h = k[N.tokens], k[N.h]
    size = y0.shape[0]
    normalize(k, rows_of(y0), N.norm_branch, D, size, 64, keeping(k, N.norm_branch, to_low(h)))
    k.put(N.h)
    q, key, value = k[N.q_ws], k[N.k_ws], k[N.v_ws]
    project(k, N.wide_self_query, h, q)
    project(k, N.wide_self_key, h, key)
    project(k, N.wide_self_value, h, value)
    k.put(N.q_ws, N.k_ws, N.v_ws)
    project(k, N.wide_cross_query, h, k[N.q_wc])
    k.put(N.q_wc)
    attend(q, key, value, k[N.caps], k[N.p_ws], k[N.o_ws], BRANCH_HEADS, size)
    k.put(N.p_ws, N.o_ws)
    o, base = k[N.o_ws], k[N.base]
    def finish(j, total):
        cols = at(j, 256)
        base[:, cols] = y0[:, cols].astype(F32) + total

    chunks(D // 256, lambda j: dot(o[...], k.columns(N.wide_self_output, 2 * j, 2)), finish)


def decoder_forward(k):
    k[N.vectors]
    memory = k[N.memory]
    size = memory.shape[0]
    project(k, N.wide_cross_key, memory, k[N.k_wc])
    project(k, N.wide_cross_value, memory, k[N.v_wc])
    k.put(N.k_wc, N.v_wc)
    attend(
        k[N.q_wc], k[N.k_wc], k[N.v_wc], k[N.caps_cross], k[N.p_wc], k[N.o_wc], BRANCH_HEADS, size
    )
    k.put(N.p_wc, N.o_wc)
    y1, edged = k[N.y1], Edged(k[N.edged], size)
    add_product(k, N.wide_cross_output, k[N.o_wc], k[N.base], y1)

    def keep_conv(rows, j, out):
        edged.store(rows.start, rows.size, j, out)

    normalize(k, rows_of(y1), N.norm_conv, D, size, 64, keeping(k, N.norm_conv, keep_conv))
    mask, left_in, right_in = k[N.mask], k[N.left_in], k[N.right_in]
    taps_forward(k, N.left_taps, moves_of(11, -10), edged, mask, left_in, D, size)
    taps_forward(k, N.right_taps, moves_of(7, -6), edged, mask, right_in, D, size)
    k.put(N.left_in, N.right_in)
    mixed, slope_left = Edged(k[N.mixed], size), k[N.slope_left]
    def left(j):
        if j == 2 * D // 256:
            return dot(right_in[...], k.columns(N.right_weight, 0, 2))
        return dot(left_in[...], k.columns(N.left_weight, 2 * j, 2))

    def keep_left(j, total):
        if j == 2 * D // 256:
            mixed.store_wide(0, total + k.row(N.right_bias, 0, 2), True)
            return
        value, slope = gelu_both(total + k.row(N.left_bias, 2 * j, 2))
        mixed.store_wide(j, value)
        slope_left[:, at(j, 256)] = slope.astype(BF)

    chunks(2 * D // 256 + 1, left, keep_left)
    k.put(N.slope_left)
    z_middle, r_middle = k[N.z_middle], k[N.r_middle]

    def keep_middle(rows, j, z, out, r):
        z_middle[rows, lanes(j)] = z.astype(BF)
        mixed.store(rows.start, rows.size, j, out)
        if j == 0:
            r_middle[rows, :] = jnp.broadcast_to(r, (rows.size, LANES))

    normalize(
        k, lambda rows, j: mixed.load(rows.start, rows.size, j), N.middle, 2 * D, size, 32, keep_middle
    )
    k.put(N.z_middle, N.r_middle)
    out_in, y2 = k[N.out_in], k[N.y2]
    taps_forward(k, N.out_taps, moves_of(7, -6), mixed, mask, out_in, 2 * D, size)
    k.put(N.out_in)
    def conv_out(j, total):
        cols = at(j, 256)
        y2[:, cols] = y1[:, cols] + total + k.row(N.out_bias, 2 * j, 2)

    chunks(D // 256, lambda j: dot(out_in[...], k.columns(N.out_weight, 2 * j, 2)), conv_out)
    h_s, y3 = k[N.h_s], k[N.y3]
    normalize(k, rows_of(y2), N.norm_self, D, size, 64, keeping(k, N.norm_self, to_low(h_s)))
    project(k, N.self_query, h_s, k[N.q_s])
    project(k, N.self_key, h_s, k[N.k_s])
    project(k, N.self_value, h_s, k[N.v_s])
    k.put(N.h_s, N.q_s, N.k_s, N.v_s)
    attend(k[N.q_s], k[N.k_s], k[N.v_s], k[N.caps], k[N.p_s], k[N.o_s], HEADS, size)
    k.put(N.p_s, N.o_s)
    add_product(k, N.self_output, k[N.o_s], y2, y3)
    h_c, y4 = k[N.h_c], k[N.y4]
    normalize(k, rows_of(y3), N.norm_cross, D, size, 64, keeping(k, N.norm_cross, to_low(h_c)))
    project(k, N.cross_query, h_c, k[N.q_c])
    project(k, N.cross_key, memory, k[N.k_c])
    project(k, N.cross_value, memory, k[N.v_c])
    k.put(N.h_c, N.q_c, N.k_c, N.v_c)
    attend(k[N.q_c], k[N.k_c], k[N.v_c], k[N.caps_cross], k[N.p_c], k[N.o_c], HEADS, size)
    k.put(N.p_c, N.o_c)
    add_product(k, N.cross_output, k[N.o_c], y3, y4)
    h_f, inner, slope_feed = k[N.h_f], k[N.inner], k[N.slope_feed]
    normalize(k, rows_of(y4), N.norm_feed, D, size, 64, keeping(k, N.norm_feed, to_low(h_f)))
    feed_in(k, h_f, inner, slope_feed, silu_both)
    k.put(N.h_f, N.inner, N.slope_feed)
    feed_out(k, inner, y4, k[N.output])


def decoder_back(k):
    k[N.vectors]
    dout = k[N.cotangent]
    size = dout.shape[0]
    sums = k[N.vector_sums]
    sums[...] = jnp.zeros(sums.shape, F32)
    dpre, dh, dx, dmem = k[N.dpre_feed], k[N.dh], k[N.dx], k[N.dmem]
    add_all_rows(k, N.feed_out_bias, dout, D)
    feed_back(k, dout, k[N.slope_feed], dpre, dh)
    k.put(N.dpre_feed)
    d4 = k[N.d4]
    add_norm_back(k, N.norm_feed, size, dh, rows_of(dout), dx, d4)
    k.put(N.d4)
    dheads = k[N.dheads]

    def write_heads(j, total):
        dheads[:, at(j, 256)] = total.astype(BF)

    def write_dh(j, total):
        dh[:, at(j, 256)] = total

    def write_dmem(j, total):
        dmem[:, at(j, 256)] = total

    project_back(k, [(N.cross_output, d4)], write_heads, D)
    dq, dkey, dvalue = k[N.dq_c], k[N.dk_c], k[N.dv_c]
    attend_back(k[N.q_c], k[N.k_c], k[N.v_c], k[N.p_c], dheads, dq, dkey, dvalue, HEADS, size)
    k.put(N.dq_c, N.dk_c, N.dv_c)
    project_back(k, [(N.cross_query, dq)], write_dh, D)
    project_back(k, [(N.cross_key, dkey), (N.cross_value, dvalue)], write_dmem, D)
    d3 = k[N.d3]
    add_norm_back(k, N.norm_cross, size, dh, rows_of(dx), dx, d3)
    k.put(N.d3)
    project_back(k, [(N.self_output, d3)], write_heads, D)
    dq, dkey, dvalue = k[N.dq_s], k[N.dk_s], k[N.dv_s]
    attend_back(k[N.q_s], k[N.k_s], k[N.v_s], k[N.p_s], dheads, dq, dkey, dvalue, HEADS, size)
    k.put(N.dq_s, N.dk_s, N.dv_s)
    project_back(
        k, [(N.self_query, dq), (N.self_key, dkey), (N.self_value, dvalue)], write_dh, D
    )
    d2 = k[N.d2]
    add_norm_back(k, N.norm_self, size, dh, rows_of(dx), dx, d2)
    k.put(N.d2)
    add_all_rows(k, N.out_bias, dx, D)
    dspread, mask = Edged(k[N.dspread], size), k[N.mask]

    def write_spread(j, total):
        dspread.store_wide(j, total)

    project_back(k, [(N.out_weight, d2)], write_spread, 2 * D)
    z_middle, r_middle = k[N.z_middle], k[N.r_middle]

    dmiddle = k[N.dmiddle]

    def write_middle(rows, j, total):
        dmiddle[rows, lanes(j)] = total
    taps_back(
        k, [(N.out_taps, moves_of(7, -6), dspread)], output_of(k, N.middle), mask, 2 * D, size, write_middle
    )
    slope_left, dleft, dright = k[N.slope_left], k[N.dleft], k[N.dright]

    def middle(i):
        rows = at(i, 16)
        zs = [z_middle[rows, lanes(j)].astype(F32) for j in blocks_of(2 * D)]
        douts = [dmiddle[rows, lanes(j)] for j in blocks_of(2 * D)]
        grads = norm_gradient(k, N.middle, 2 * D, zs, douts, r_middle[rows, :])
        for j in blocks_of(2 * D):
            grad = grads[j] * slope_left[rows, lanes(j)].astype(F32)
            k.add_rows(N.left_bias, j, grad)
            dleft[rows, lanes(j)] = grad.astype(BF)
        for j in range(2):
            k.add_rows(N.right_bias, j, grads[j])
            dright[rows, lanes(j)] = grads[j].astype(BF)

    loop(size // 16, middle, 4)
    k.put(N.dleft, N.dright)
    dleft_in, dright_in = dspread.part(0, 4), dspread.part(4, 4)

    def write_left(j, total):
        dleft_in.store_wide(j, total)

    def write_right(j, total):
        dright_in.store_wide(j, total)

    project_back(k, [(N.left_weight, dleft)], write_left, D)
    project_back(k, [(N.right_weight, dright)], write_right, D)
    def write_conv(rows, j, total):
        dh[rows, lanes(j)] = total

    taps_back(
        k,
        [(N.left_taps, moves_of(11, -10), dleft_in), (N.right_taps, moves_of(7, -6), dright_in)],
        output_of(k, N.norm_conv),
        mask,
        D,
        size,
        write_conv,
    )
    d1 = k[N.d1]
    add_norm_back(k, N.norm_conv, size, dh, rows_of(dx), dx, d1)
    k.put(N.d1, N.dx)
    project_back(k, [(N.wide_cross_output, d1)], write_heads, D)
    dq, dkey, dvalue = k[N.dq_wc], k[N.dk_wc], k[N.dv_wc]
    attend_back(
        k[N.q_wc], k[N.k_wc], k[N.v_wc], k[N.p_wc], dheads, dq, dkey, dvalue, BRANCH_HEADS, size
    )
    k.put(N.dq_wc, N.dk_wc, N.dv_wc)
    sent = k[N.sent]

    def write_sent(j, total):
        sent[:, at(j, 256)] = (dmem[:, at(j, 256)] + total).astype(BF)

    project_back(k, [(N.wide_cross_key, dkey), (N.wide_cross_value, dvalue)], write_sent, D)


def branch_back(k):
    k[N.vectors]
    d1 = k[N.d1]
    size = d1.shape[0]
    sums = k[N.vector_sums]
    sums[...] = jnp.zeros(sums.shape, F32)
    dheads, dh = k[N.dheads], k[N.dh]

    def write_heads(j, total):
        dheads[:, at(j, 256)] = total.astype(BF)

    project_back(k, [(N.wide_self_output, d1)], write_heads, D)
    dq, dkey, dvalue = k[N.dq_ws], k[N.dk_ws], k[N.dv_ws]
    attend_back(
        k[N.q_ws], k[N.k_ws], k[N.v_ws], k[N.p_ws], dheads, dq, dkey, dvalue, BRANCH_HEADS, size, 2
    )
    k.put(N.dq_ws, N.dk_ws, N.dv_ws)

    def write_dh(j, total):
        dh[:, at(j, 256)] = total

    project_back(
        k,
        [
            (N.wide_self_query, dq),
            (N.wide_self_key, dkey),
            (N.wide_self_value, dvalue),
            (N.wide_cross_query, k[N.dq_wc]),
        ],
        write_dh,
        D,
    )
    add_norm_back(k, N.norm_branch, size, dh, rows_of(k[N.dx]), k[N.token_grad])


def segment_ids(lengths_rows, token_count):
    ends_at = jnp.cumsum(lengths_rows, axis=-1)
    places = jnp.arange(token_count, dtype=jnp.int32)
    return jnp.sum((places[None, :, None] >= ends_at[:, None, :]).astype(jnp.int32), axis=2)


def spread_segments(segments):
    micro, tokens = segments.shape
    own = segments + tokens * jnp.arange(micro, dtype=jnp.int32)[:, None]
    own = jnp.pad(own.reshape(micro * tokens), (EDGE, EDGE), constant_values=-1)
    return jnp.broadcast_to(own.astype(F32)[:, None], (own.shape[0], LANES))


def caps_of(allowed):
    return jnp.where(allowed, jnp.float32(3e38), jnp.float32(-1e30))


def low_like(size, width, kind=BF):
    return jax.ShapeDtypeStruct((size, width), kind)


def tail_pad(value, rows):
    return jnp.pad(value, ((0, rows - value.shape[0]), (0, 0)))


def local(tokens, lengths, params, cotangent):
    count = lax.axis_size("dp")
    is_first = lax.axis_index("section") == 0
    enc_rows = 2 * -(-ENC.rows // (2 * count))
    dec_rows = 2 * -(-DEC.rows // (2 * count))
    own_rows = params.shape[1]
    own = params[0]
    micro, pack_tokens = tokens.shape[1], tokens.shape[2]
    size = micro * pack_tokens

    holders = slot_devices(GATHER_ORDER, count)
    takers = slot_devices(REDUCE_ORDER, count)
    main_height, tail_height = up_to(own_rows, 16), up_to(own_rows - enc_rows, 16)
    whole, tails = gather_slots(tail_pad(own.astype(BF), main_height), enc_rows, count)

    source_ids = segment_ids(lengths[0, :, 0], pack_tokens)
    target_ids = segment_ids(lengths[1, :, 0], pack_tokens)
    places = jnp.arange(pack_tokens, dtype=jnp.int32)
    early = places[:, None] <= places[None, :]
    mask = spread_segments(jnp.where(is_first, source_ids, target_ids))
    same_source = source_ids[:, :, None] == source_ids[:, None, :]
    same_target = (target_ids[:, :, None] == target_ids[:, None, :]) & early[None]
    caps = caps_of(jnp.where(is_first, same_source, same_target))
    caps_cross = caps_of(source_ids[:, :, None] == target_ids[:, None, :])
    mask, caps, caps_cross = lax.optimization_barrier((mask, caps, caps_cross))
    own_tokens = tokens[0].reshape(size, D)
    given = cotangent.reshape(size, D)

    low = low_like(size, D)
    full = low_like(size, D, F32)
    wide = low_like(size, FF)
    rows = low_like(size, LANES, F32)
    edged = ((4 * (size + 2 * EDGE), LANES), F32)
    edged_wide = ((16 * (size + 2 * EDGE), LANES), F32)
    edged_two = ((8 * (size + 2 * EDGE), LANES), F32)
    packs = size // PACK
    probs_16 = low_like(packs * BRANCH_HEADS * PACK, PACK)
    probs_8 = low_like(packs * HEADS * PACK, PACK)
    sums = low_like(VECTOR_ROWS * 8, LANES, F32)

    norm_out = lambda *names: {N.z_ + n: low for n in names} | {N.r_ + n: rows for n in names}
    enc_out = norm_out(N.norm_glu, N.norm_conv, N.norm_attn, N.norm_feed) | dict(
        h1=low, glu_a=low, glu_s=low, h2=low, stacked=low_like(size, 3 * D),
        slope_left=wide, slope_right=low_like(size, 256), z_middle=wide, r_middle=rows,
        spread=wide, h3=low, q=low, key=low, value=low, probs=probs_8, heads=low,
        h4=low, inner=wide, slope_feed=wide, memory=low,
    )
    start_out = norm_out(N.norm_branch) | dict(
        h=low, q_ws=low, k_ws=low, v_ws=low, q_wc=low, p_ws=probs_16, o_ws=low, base=full
    )
    made = dict(
        weights=low_like(WEIGHT_ROWS, LANES), vectors=low_like(VECTOR_ROWS, LANES, F32)
    )

    def encoder_start():
        weights, vectors = lay_out(ENC, [whole], [0], enc_rows, holders)
        result = fused(
            encoder_forward,
            ENC,
            weights,
            list(ENC.weights),
            dict(vectors=vectors, tokens=own_tokens, mask=mask, caps=caps),
            enc_out,
            {},
            dict(
                edged=edged, mixed=edged_wide, x1=((size, D), F32), x2=((size, D), F32),
                x3=((size, D), F32),
            ),
        )
        return result | dict(weights=weights, vectors=vectors)

    enc = lax.cond(is_first, encoder_start, lambda: idle(enc_out | made))
    tails[-1], enc[N.memory] = lax.optimization_barrier((tails[-1], enc[N.memory]))
    ends = share_tails(tails, count)

    def decoder_begin():
        weights, vectors = lay_out(DEC, [whole, ends], [0, own_rows], dec_rows, holders)
        result = fused(
            decoder_start,
            DEC,
            weights,
            [N.wide_self_query, N.wide_self_key, N.wide_self_value, N.wide_cross_query, N.wide_self_output],
            dict(vectors=vectors, tokens=own_tokens, caps=caps),
            start_out,
            {},
            {},
        )
        return result | dict(weights=weights, vectors=vectors)

    dec = lax.cond(~is_first, decoder_begin, lambda: idle(start_out | made))
    memory = lax.ppermute(enc[N.memory], "section", [(0, 1)])

    forward_out = norm_out(N.norm_conv, N.norm_self, N.norm_cross, N.norm_feed) | dict(
        k_wc=low, v_wc=low, p_wc=probs_16, o_wc=low, left_in=low, right_in=low,
        slope_left_d=low_like(size, 2 * D), z_middle_d=low_like(size, 2 * D), r_middle_d=rows,
        out_in=low_like(size, 2 * D), h_s=low, q_s=low, k_s=low, v_s=low, p_s=probs_8, o_s=low,
        h_c=low, q_c=low, k_c=low, v_c=low, p_c=probs_8, o_c=low, h_f=low,
        inner_d=wide, slope_feed_d=wide, output=low,
    )
    early_names = (N.wide_self, N.wide_cross_query)
    later = [n for n in DEC.weights if not n.startswith(early_names)]
    back_out = dict(
        dpre_feed=wide, d4=low, dq_c=low, dk_c=low, dv_c=low, d3=low, dq_s=low, dk_s=low, dv_s=low,
        d2=low, dleft=low_like(size, 2 * D), dright=low_like(size, 256), d1=low, dx=full,
        dq_wc=low, dk_wc=low, dv_wc=low, vector_sums=sums, sent=low,
    )
    back_names = [
        N.feed_out_weight, N.feed_in_weight, N.cross_output, N.cross_query, N.cross_key, N.cross_value,
        N.self_output, N.self_query, N.self_key, N.self_value, N.out_weight, N.left_weight, N.right_weight,
        N.wide_cross_output, N.wide_cross_key, N.wide_cross_value,
    ]
    saved = [
        N.slope_feed, N.z_norm_feed, N.r_norm_feed, N.q_c, N.k_c, N.v_c, N.p_c, N.z_norm_cross,
        N.r_norm_cross, N.q_s, N.k_s, N.v_s, N.p_s, N.z_norm_self, N.r_norm_self, N.z_middle,
        N.r_middle, N.slope_left, N.z_norm_conv, N.r_norm_conv, N.k_wc, N.v_wc, N.p_wc,
    ]

    def decode_forward():
        return fused(
            decoder_forward,
            DEC,
            dec[N.weights],
            later,
            dict(
                vectors=dec[N.vectors], memory=memory, q_wc=dec[N.q_wc], caps_cross=caps_cross,
                base=dec[N.base], mask=mask, caps=caps,
            ),
            strip_names(forward_out),
            {},
            dict(
                edged=edged, mixed=edged_two, y1=((size, D), F32), y2=((size, D), F32),
                y3=((size, D), F32), y4=((size, D), F32),
            ),
        )

    def decode_back():
        return fused(
            decoder_back,
            DEC,
            dec[N.weights],
            back_names,
            dict(vectors=dec[N.vectors], cotangent=given)
            | {n: forward[n] for n in saved}
            | dict(mask=mask, q_wc=dec[N.q_wc]),
            back_out,
            {},
            dict(
                dh=((size, D), F32), dmem=((size, D), F32), dheads=((size, D), BF), dspread=edged_two,
                dmiddle=((size, 2 * D), F32),
            ),
        )

    forward = lax.cond(~is_first, decode_forward, lambda: idle(strip_names(forward_out)))
    back = lax.cond(~is_first, decode_back, lambda: idle(back_out))
    returned = lax.ppermute(back[N.sent], "section", [(1, 0)])
    returned, back[N.d1] = lax.optimization_barrier((returned, back[N.d1]))

    enc_last = dict(
        dpre_feed=wide, d3=low, dq=low, dkey=low, dvalue=low, d2=low_like(size, 256), dleft=wide,
        dright=low_like(size, 256), dglu=low_like(size, 2 * D), token_grad=full, vector_sums=sums,
    )
    dec_last = dict(dq_ws=low, dk_ws=low, dv_ws=low, token_grad=full, vector_sums=sums)
    enc_names = [
        N.feed_out_weight, N.feed_in_weight, N.attn_output, N.attn_query, N.attn_key, N.attn_value,
        N.point_weight, N.right_weight, N.left_weight, N.glu_weight,
    ]
    enc_saved = [
        N.slope_feed, N.z_norm_feed, N.r_norm_feed, N.q, N.key, N.value, N.probs, N.z_norm_attn,
        N.r_norm_attn, N.z_middle, N.r_middle, N.slope_left, N.slope_right, N.z_norm_conv,
        N.r_norm_conv, N.glu_a, N.glu_s, N.z_norm_glu, N.r_norm_glu,
    ]
    enc_products = [
        (N.feed_out_weight, N.inner, N.returned), (N.feed_in_weight, N.h4, N.dpre_feed),
        (N.attn_output, N.heads, N.d3), (N.attn_query, N.h3, N.dq), (N.attn_key, N.h3, N.dkey),
        (N.attn_value, N.h3, N.dvalue), (N.point_weight, N.spread, N.d2),
        (N.right_weight, N.stacked, N.dright), (N.left_weight, N.h2, N.dleft), (N.glu_weight, N.h1, N.dglu),
    ]
    dec_products = [
        (N.feed_out_weight, N.inner, N.cotangent), (N.feed_in_weight, N.h_f, N.dpre_feed),
        (N.cross_output, N.o_c, N.d4), (N.cross_query, N.h_c, N.dq_c), (N.cross_key, N.memory, N.dk_c),
        (N.cross_value, N.memory, N.dv_c), (N.wide_cross_key, N.memory, N.dk_wc),
        (N.wide_cross_value, N.memory, N.dv_wc), (N.self_output, N.o_s, N.d3),
        (N.self_query, N.h_s, N.dq_s), (N.self_key, N.h_s, N.dk_s), (N.self_value, N.h_s, N.dv_s),
        (N.out_weight, N.out_in, N.d2), (N.left_weight, N.left_in, N.dleft),
        (N.right_weight, N.right_in, N.dright), (N.wide_cross_output, N.o_wc, N.d1),
        (N.wide_self_output, N.o_ws, N.d1), (N.wide_self_query, N.h, N.dq_ws), (N.wide_self_key, N.h, N.dk_ws),
        (N.wide_self_value, N.h, N.dv_ws), (N.wide_cross_query, N.h, N.dq_wc),
    ]

    def only(arrays, products):
        return {n: arrays[n] for p in products for n in p[1:]}

    if by_neighbours(count):
        main_shapes = [low_like(main_height, LANES)] * 16
        tail_shapes = [jax.ShapeDtypeStruct((8, tail_height, LANES), BF)] * 2
        main_targets = [(n, None) for n in range(16)]
        tail_targets = [(16 + o, n) for n in range(8) for o in range(2)]
    else:
        main_shapes = [jax.ShapeDtypeStruct((count, main_height, LANES), BF)]
        tail_shapes = [jax.ShapeDtypeStruct((count, tail_height, LANES), BF)]
        main_targets = [(0, j) for j in range(count)]
        tail_targets = [(1, j) for j in range(count)]

    def decoder_last():
        last = fused(
            branch_back,
            DEC,
            dec[N.weights],
            [
                N.wide_self_output, N.wide_self_query, N.wide_self_key, N.wide_self_value,
                N.wide_cross_query,
            ],
            dict(vectors=dec[N.vectors], d1=back[N.d1])
            | {n: dec[n] for n in (N.q_ws, N.k_ws, N.v_ws, N.p_ws)}
            | {n: dec[n] for n in (N.z_norm_branch, N.r_norm_branch)}
            | dict(dq_wc=back[N.dq_wc], dx=back[N.dx]),
            dec_last,
            {},
            dict(dheads=((size, D), BF), dh=((size, D), F32)),
        )
        arrays = dec | forward | back | last | dict(cotangent=given, memory=memory)
        grads = weight_gradients(
            DEC, dec_products, only(arrays, dec_products), [back[N.vector_sums], last[N.vector_sums]],
            main_shapes + tail_shapes, [main_targets, tail_targets], [0, own_rows], dec_rows, takers, False,
        )
        return last[N.token_grad], grads

    def encoder_last():
        last = fused(
            encoder_back,
            ENC,
            enc[N.weights],
            enc_names,
            dict(vectors=enc[N.vectors], returned=returned)
            | {n: enc[n] for n in enc_saved}
            | dict(mask=mask),
            enc_last,
            {},
            dict(
                dh=((size, D), F32), dx=((size, D), F32), dheads=((size, D), BF), dspread=edged_wide,
                dmiddle=((size, FF), F32),
            ),
        )
        return last

    def nothing(shapes):
        names = dict(enumerate(shapes))
        return tuple(idle(names).values())

    source_back = lax.cond(is_first, encoder_last, lambda: idle(enc_last))
    target_grad, dec_grads = lax.cond(
        ~is_first,
        decoder_last,
        lambda: (idle(dict(grad=full))[N.grad], nothing(main_shapes + tail_shapes)),
    )
    tails = hand_over_tails(dec_grads[len(main_shapes) :], count)
    enc_arrays = only(enc | source_back | dict(returned=returned), enc_products)
    grads = weight_gradients(
        ENC, enc_products, enc_arrays, [source_back[N.vector_sums]], main_shapes, [main_targets], [0],
        enc_rows, takers, False, dec_grads[: len(main_shapes)], is_first,
    )

    parts, tail = reduce_slots(grads, tails, enc_rows, count)
    param_out = add_up(parts, tail, enc_rows, own_rows).reshape(1, own_rows, LANES)
    token_grads = jnp.where(is_first, source_back[N.token_grad], target_grad)
    shape = (1, micro, pack_tokens, D)
    results = jnp.where(is_first, returned, forward[N.output])
    return (results.reshape(shape), token_grads.reshape(shape), param_out)


def strip_names(outs):
    return {n[:-2] if n.endswith(N._d) else n: v for n, v in outs.items()}


def idle(outs):
    names = list(outs)

    def kernel(*refs):
        return None

    any_spec = pl.BlockSpec(memory_space=pl.ANY)
    result = pl.pallas_call(
        kernel,
        out_shape=[outs[n] for n in names],
        out_specs=[any_spec] * len(names),
    )()
    return dict(zip(names, result))


def solution(mesh):
    return jax.shard_map(
        local,
        mesh=mesh,
        in_specs=(
            P("section", None, "dp", None),
            P(None, None, "dp", None),
            P("section", "dp", None),
            P(None, "dp", None),
        ),
        out_specs=(
            P("section", None, "dp", None),
            P("section", None, "dp", None),
            P("section", "dp", None),
        ),
        check_vma=False,
    )
```
